256 devices in a mesh: docs: 32 (over z, y), cent: 8 (over x, core).
Axes of the slice: x: 4, y: 4, z: 8, core: 2. Of those that a mesh axis runs over, the one named last changes fastest.
Arguments:
- embeddings: bfloat16 [32768, 768], P('docs'), may hold values from -16 to 16
- centroids: bfloat16 [32768, 768], P('cent')
Outputs:
- new_centroids: bfloat16 [8, 4096, 768], P('cent', 'docs')
The draws below stay inside these ranges and needn't reach their ends.
All inputs are finite; a program needn't handle non-finite values.
Results may differ from the reference program's by a relative error of at most 0.0049.
Values may be sent and summed in bfloat16 or wider, within the bound.
A program may use at most 128 MiB of HBM per device.

```python
import jax
import jax.numpy as jnp
from jax import lax

D = 768
K_DEV = 4096
PASSES = 3
ROWS = 32768
K = 32768
N_CENT = 8


def shared_centroids(key):
    inner = jax.random.fold_in(key, 11)
    values = jax.random.truncated_normal(inner, -6.0, 6.0, (K, D), jnp.float32)
    return values * D ** (-0.5)


def draw_centroids(key, part):
    shared = shared_centroids(key)
    return shared.astype(jnp.bfloat16)


def draw_embeddings(key, part):
    key = jax.random.fold_in(key, 2)
    keys = jax.random.split(key, 1)
    values = jax.random.truncated_normal(keys[0], -6.0, 6.0, (ROWS, D), jnp.float32)
    return jnp.clip(values, -16.0, 16.0).astype(jnp.bfloat16)


def setup_inputs(seed: int = 0) -> dict:
    key_of = jax.random.split(jax.random.key(seed), 3)
    embeddings = draw_embeddings(jax.random.fold_in(key_of[2], 71), 0)
    centroids = draw_centroids(jax.random.fold_in(key_of[2], 71), 0)
    return dict(embeddings=embeddings, centroids=centroids)


inv_eps = 10.0
highest = lax.Precision.HIGHEST


def block_logits(embeddings, block):
    return lax.dot_general(embeddings, block, (((1,), (1,)), ((), ())), preferred_element_type=jnp.float32) * inv_eps


def reference(embeddings, centroids):
    blocks = centroids.reshape(N_CENT, K_DEV, D)

    def first_sweep(carry, block):
        running_top, running_sum = carry
        scores = block_logits(embeddings, block)
        fresh = jnp.maximum(running_top, jnp.max(scores, axis=1))
        total = running_sum * jnp.exp(running_top - fresh) + jnp.sum(jnp.exp(scores - fresh[:, None]), axis=1)
        return (fresh, total), None

    start = (jnp.full((ROWS,), -jnp.inf, jnp.float32), jnp.zeros((ROWS,), jnp.float32))
    (top, row), _ = lax.scan(first_sweep, start, blocks)
    for step in range(PASSES):
        row_weight = 1.0 / (ROWS * row)
        last = step + 1 == PASSES

        def sweep(carry, block):
            scores = block_logits(embeddings, block)
            kernel = jnp.exp(scores - top[:, None])
            mass = jnp.dot(row_weight, kernel, precision=highest)
            scale = 1.0 / (K * mass)
            carry = carry + jnp.dot(kernel, scale, precision=highest)
            if last:
                weights = (kernel * row_weight[:, None]).astype(jnp.bfloat16)
                numerator = lax.dot_general(weights, embeddings, (((0,), (0,)), ((), ())), preferred_element_type=jnp.float32)
                return carry, (numerator / mass[:, None]).astype(jnp.bfloat16)
            return carry, None

        row, outputs = lax.scan(sweep, jnp.zeros((ROWS,), jnp.float32), blocks)
    return outputs
```

```python
import jax
import jax.numpy as jnp
import numpy as np
from jax import lax
from jax.experimental import pallas as pl
from jax.experimental.pallas import tpu as pltpu
from jax.sharding import PartitionSpec as P

MESH = pl.DeviceIdType.MESH
F32 = jnp.float32
BF16 = jnp.bfloat16

NX, NY, NZ = 4, 4, 8
D = 768
PIECE = 64
NB, BW = 8, 512
CH = 128
C = NZ * CH
TOTAL = 32768.0
EXP2_SCALE = 10.0 * float(np.log2(np.e))

ORDER = (4, 3, -3, 2, -2, 1, -1, 0)
POS = {q: i for i, q in enumerate(ORDER)}


def body(
    emb_hbm, cen_hbm, out_ref,
    emb, cen, kern, buf0, buf1,
    st, st2, r0a, r0b, rl, rl2, ra, rb, fac, rw, part, scol, ml, mr, w0, w1, num, snd, rcv,
    ld_sem, ag_s, ag_r, r1_s, r1_r, r2_s, r2_r, m_s, m_r, rs_s, rs_r,
):
    docs = lax.axis_index("docs")
    cent = lax.axis_index("cent")
    z, y = docs // NY, docs % NY
    x, c = cent // 2, cent % 2

    def at(dz=0, dy=0, dx=0, flip=False):
        zz = (z + dz + NZ) % NZ
        yy = (y + dy + NY) % NY
        xx = (x + dx + NX) % NX
        return (zz * NY + yy, xx * 2 + ((1 - c) if flip else c))

    load_e = pltpu.make_async_copy(emb_hbm, emb.at[pl.ds(y * 16, 16)], ld_sem.at[0])
    load_c = pltpu.make_async_copy(cen_hbm.at[:, y], cen, ld_sem.at[1])
    load_e.start()
    load_c.start()

    cent_peers = [(docs, (cent + k) % 8) for k in range(1, 8)]
    y_peers = [at(dy=k) for k in range(1, NY)]
    z_peers = [at(dz=k) for k in range(1, NZ)]
    barrier = pltpu.get_barrier_semaphore()
    for peer in cent_peers + y_peers + z_peers:
        pl.semaphore_signal(barrier, inc=1, device_id=peer, device_id_type=MESH)
    pl.semaphore_wait(barrier, len(cent_peers) + len(y_peers) + len(z_peers))

    def piece(dy, h, dx):
        return ((y + dy + NY) % NY) * 16 + h * 8 + ((x + dx + NX) % NX) * 2 + c

    ag = {}

    def send(name, where, target):
        i = len(ag)
        copy = pltpu.make_async_remote_copy(
            src_ref=emb.at[where], dst_ref=emb.at[where], send_sem=ag_s.at[i], recv_sem=ag_r.at[i],
            device_id=target, device_id_type=MESH,
        )
        copy.start()
        ag[name] = copy

    def got(*names):
        for name in names:
            ag[name].wait_recv()

    def to_sibling(*pieces):
        for dy, h, dx in pieces:
            send(("s", dy, h, dx), piece(dy, h, dx), at(flip=True))

    def to_x(*pieces):
        for dy, h, dx in pieces:
            for s in (1, -1):
                send(("x1", s, dy, h), piece(dy, h, dx), at(dx=s))

    def block_ready(dy, h):
        for dx in range(NX):
            got(("s", dy, h, dx if dx < 3 else -1))

    load_e.wait()
    for s in (1, -1):
        send(("u", s), piece(0, 1, 0), at(dy=s))
    for s in (1, -1):
        send(("l", s), piece(0, 0, 0), at(dy=s))
    for s in (1, -1):
        send(("k", s, 1), piece(0, 0, 1), at(dy=s))
    load_c.wait()

    def phase_1():
        for s in (1, -1):
            got(("u", s))
            to_x((-s, 1, 0))
        for s in (1, -1):
            got(("l", s))
        send(("y3", 1), piece(-1, 0, 0), at(dy=1))
        send(("y3", -1), piece(1, 1, 0), at(dy=-1))
        for k in (2, -1):
            for s in (1, -1):
                send(("k", s, k), piece(0, 0, k), at(dy=s))
        to_sibling((1, 1, 0), (-1, 1, 0), (1, 0, 0), (-1, 0, 0))

    def phase_2():
        got(("y3", 1), ("y3", -1))
        to_x((2, 0, 0), (2, 1, 0))
        to_sibling((2, 0, 0), (2, 1, 0))
        got(("x1", 1, 1, 1), ("x1", -1, -1, 1))
        send(("x2", 1, 1, 1), piece(1, 1, -1), at(dx=1))
        send(("x2", -1, -1, 1), piece(-1, 1, 1), at(dx=-1))
        to_sibling((1, 1, -1), (-1, 1, 1))
        got(("x1", 1, -1, 1), ("x1", -1, 1, 1))
        to_sibling((-1, 1, -1), (1, 1, 1))
        for s in (1, -1):
            got(("k", s, 1))
            to_sibling((-s, 0, 1))

    def phase_3():
        for k in (2, -1):
            for s in (1, -1):
                got(("k", s, k))
                to_sibling((-s, 0, k))

    def phase_4():
        got(("x1", 1, 2, 0), ("x1", -1, 2, 1))
        send(("x2", 1, 2, 0), piece(2, 0, -1), at(dx=1))
        send(("x2", -1, 2, 1), piece(2, 1, 1), at(dx=-1))
        to_sibling((2, 0, -1), (2, 1, 1))
        got(("x1", 1, 2, 1), ("x1", -1, 2, 0))
        to_sibling((2, 1, -1), (2, 0, 1))
        got(("x2", 1, 1, 1), ("x2", -1, -1, 1))
        to_sibling((1, 1, 2), (-1, 1, 2))

    def phase_5():
        got(("x2", 1, 2, 0), ("x2", -1, 2, 1))
        to_sibling((2, 0, 2), (2, 1, 2))

    def block_at(dy, h):
        return ((y + dy + NY) % NY) * 2 + h

    def step(new, new_buf, old, old_buf, old_max):
        if old is not None:
            top = jnp.max(old_max, axis=0, keepdims=True)
            total = jnp.zeros((8, BW), F32)
        new_max = None
        if new is not None:
            e = emb[pl.ds(new * 8, 8)].reshape(BW, D)
        for i in range(4):
            rows = slice(256 * i, 256 * i + 256)
            if new is not None:
                raw = lax.dot_general(
                    cen[2 * i:2 * i + 2].reshape(256, D), e, (((1,), (1,)), ((), ())),
                    preferred_element_type=F32,
                )
                new_buf[rows, :] = raw
                high = jnp.max(raw.reshape(32, 8, BW), axis=0)
                new_max = high if new_max is None else jnp.maximum(new_max, high)
            if old is not None:
                value = jnp.exp2((old_buf[rows, :] - top) * EXP2_SCALE)
                kern[old, rows, :] = value
                total = total + jnp.sum(value.reshape(32, 8, BW), axis=0)
        if old is not None:
            st[0, pl.ds(old, 1), :] = top
            st[1, pl.ds(old, 1), :] = jnp.sum(total, axis=0, keepdims=True)
        return new_max

    blocks = ((0, 0), (0, 1), (1, 0), (-1, 0), (1, 1), (-1, 1), (2, 0), (2, 1))
    before = {1: phase_1, 2: lambda: (phase_2(), phase_3()), 4: phase_4, 6: phase_5}
    bufs = (buf0, buf1)
    high = None
    for i in range(NB + 1):
        if i in before:
            before[i]()
        if 2 <= i < NB:
            block_ready(*blocks[i])
        new = block_at(*blocks[i]) if i < NB else None
        old = block_at(*blocks[i - 1]) if i > 0 else None
        high = step(new, bufs[i % 2], old, bufs[(i + 1) % 2], high)

    def push(src, dst, peers, ssem, rsem):
        copies = []
        for k, peer in enumerate(peers):
            copy = pltpu.make_async_remote_copy(
                src_ref=src, dst_ref=dst.at[k], send_sem=ssem.at[k], recv_sem=rsem.at[k],
                device_id=peer, device_id_type=MESH,
            )
            copy.start()
            copies.append(copy)
        return copies

    sent = []

    def exchange(src, dst, peers, ssem, rsem):
        copies = push(src, dst, peers, ssem, rsem)
        for copy in copies:
            copy.wait_recv()
        sent.extend(copies)

    def merge(own, others, n):
        top = own[0]
        for k in range(n):
            top = jnp.maximum(top, others[k, 0])
        total = own[1] * jnp.exp2((own[0] - top) * EXP2_SCALE)
        for k in range(n):
            total = total + others[k, 1] * jnp.exp2((others[k, 0] - top) * EXP2_SCALE)
        return top, total

    exchange(st, r0a, cent_peers, r1_s.at[0], r1_r.at[0])
    top, total = merge(st, r0a, 7)
    st2[0] = top
    st2[1] = total
    exchange(st2, r0b, y_peers, r2_s.at[0], r2_r.at[0])
    top, total = merge(st2, r0b, 3)
    factor = jnp.exp2((st[0] - top) * EXP2_SCALE)
    fac[...] = factor
    rw[...] = factor / (TOTAL * total)

    def mass_of(n):
        def chunk(g, _):
            rows = pl.ds(pl.multiple_of(g * 64, 64), 64)
            acc = jnp.zeros((64, 128), F32)
            for b in range(NB):
                for l in range(BW // 128):
                    lanes = slice(l * 128, l * 128 + 128)
                    acc = acc + kern[b, rows, lanes] * rw[b:b + 1, lanes]
            part[rows, :] = acc
            return 0

        lax.fori_loop(0, C // 64, chunk, 0)
        for t in range(NZ):
            ml[n, t:t + 1, :] = jnp.sum(part[t * CH:(t + 1) * CH, :].T, axis=0, keepdims=True)

    def summed(own, others, n):
        total = own
        for k in range(n):
            total = total + others[k]
        return total

    for n in range(2):
        mass_of(n)
        exchange(ml.at[n], mr.at[n], z_peers, m_s.at[n], m_r.at[n])
        scale = 1.0 / (TOTAL * summed(ml[n], mr.at[n], 7))
        for t in range(NZ):
            scol[t * CH:(t + 1) * CH, :] = jnp.broadcast_to(scale[t:t + 1, :], (CH, CH)).T

        def row_block(b, _):
            def chunk(g, acc):
                rows = pl.ds(pl.multiple_of(g * 128, 128), 128)
                s = scol[rows, :]
                value = kern[b, rows, :] * jnp.concatenate([s] * (BW // 128), axis=1)
                return acc + jnp.sum(value.reshape(16, 8, BW), axis=0)

            acc = lax.fori_loop(0, C // 128, chunk, jnp.zeros((8, BW), F32))
            rl[n, pl.ds(b, 1), :] = jnp.sum(acc, axis=0, keepdims=True) * fac[pl.ds(b, 1), :]
            return 0

        lax.fori_loop(0, NB, row_block, 0)
        exchange(rl.at[n], ra.at[n], cent_peers, r1_s.at[n + 1], r1_r.at[n + 1])
        rl2[n] = summed(rl[n], ra.at[n], 7)
        exchange(rl2.at[n], rb.at[n], y_peers, r2_s.at[n + 1], r2_r.at[n + 1])
        rw[...] = fac[...] / (TOTAL * summed(rl2[n], rb.at[n], 3))

    ws = (w0, w1)

    def weigh(pair, j):
        q = ORDER[2 * pair + j]
        t = (z + q + NZ) % NZ
        rows = pl.ds(pl.multiple_of(t * CH, CH), CH)
        acc = jnp.zeros((CH, 128), F32)
        for b in range(NB):
            for l in range(BW // 128):
                lanes = slice(l * 128, l * 128 + 128)
                value = kern[b, rows, lanes] * rw[b:b + 1, lanes]
                acc = acc + value
                ws[pair % 2][j * CH:(j + 1) * CH, b * BW + l * 128:b * BW + (l + 1) * 128] = value.astype(BF16)
        ml[2, pl.ds(t, 1), :] = jnp.sum(acc.T, axis=0, keepdims=True)

    def multiply(pair):
        e = emb[...].reshape(NB * BW, D)
        num[2 * pair:2 * pair + 2] = jnp.dot(
            ws[pair % 2][...], e, preferred_element_type=F32
        ).reshape(2, CH, D)

    rs = {}

    def hop(name, q, rows, before=None):
        chain, sign = name[0], (1 if name[0] in ("RA", "RB") else -1)
        i = len(rs)
        value = num[POS[q], rows, :]
        if before is not None:
            rs[before].wait_recv()
            value = value + rcv[slot[before]].astype(F32)
        snd[i] = value.astype(BF16)
        slot[name] = i
        copy = pltpu.make_async_remote_copy(
            src_ref=snd.at[i], dst_ref=rcv.at[i], send_sem=rs_s.at[i], recv_sem=rs_r.at[i],
            device_id=at(dz=sign), device_id_type=MESH,
        )
        copy.start()
        rs[name] = copy

    slot = {}
    lo, hi = slice(0, 64), slice(64, 128)
    weigh(0, 0)
    weigh(0, 1)
    for pair in range(4):
        multiply(pair)
        if pair < 3:
            weigh(pair + 1, 0)
            weigh(pair + 1, 1)
        if pair == 0:
            hop(("RB", 0), 4, lo)
            hop(("LB", 0), 4, hi)
            hop(("RA", 1), 3, hi)
        elif pair == 1:
            hop(("LA", 1), -3, lo)
        elif pair == 2:
            last = push(ml.at[2], mr.at[2], z_peers, m_s.at[2], m_r.at[2])
            sent.extend(last)
            hop(("RB", 1), 3, lo, ("RB", 0))
            hop(("LB", 1), -3, hi, ("LB", 0))
    hop(("RA", 2), 2, hi, ("RA", 1))
    hop(("LA", 2), -2, lo, ("LA", 1))
    hop(("RB", 2), 2, lo, ("RB", 1))
    hop(("LB", 2), -2, hi, ("LB", 1))
    hop(("RA", 3), 1, hi, ("RA", 2))
    hop(("LA", 3), -1, lo, ("LA", 2))
    hop(("RB", 3), 1, lo, ("RB", 2))
    hop(("LB", 3), -1, hi, ("LB", 2))

    for copy in last:
        copy.wait_recv()
    mass = ml[2, pl.ds(z, 1), :]
    for k in range(7):
        mass = mass + mr[2, k, pl.ds(z, 1), :]
    column = jnp.broadcast_to(mass, (CH, CH)).T
    column = jnp.concatenate([column] * (D // CH), axis=1)
    for rows, one, two in ((hi, ("RA", 3), ("LB", 3)), (lo, ("LA", 3), ("RB", 3))):
        rs[one].wait_recv()
        rs[two].wait_recv()
        total = num[POS[0], rows, :] + rcv[slot[one]].astype(F32) + rcv[slot[two]].astype(F32)
        out_ref[rows, :] = (total / column[rows, :]).astype(BF16)

    for copy in list(ag.values()) + sent + list(rs.values()):
        copy.wait_send()


def local(embeddings, centroids):
    e = embeddings.reshape(16, PIECE, D)
    k = centroids.reshape(NZ, NY, CH, D)
    dma = pltpu.SemaphoreType.DMA
    v = pltpu.VMEM
    out = pl.pallas_call(
        body,
        out_shape=jax.ShapeDtypeStruct((CH, D), BF16),
        in_specs=[pl.BlockSpec(memory_space=pl.ANY)] * 2,
        out_specs=pl.BlockSpec(memory_space=pltpu.VMEM),
        scratch_shapes=[
            v((64, PIECE, D), BF16), v((NZ, CH, D), BF16), v((NB, C, BW), F32), v((C, BW), F32), v((C, BW), F32),
            v((2, NB, BW), F32), v((2, NB, BW), F32), v((7, 2, NB, BW), F32), v((3, 2, NB, BW), F32),
            v((2, NB, BW), F32), v((2, NB, BW), F32), v((2, 7, NB, BW), F32), v((2, 3, NB, BW), F32),
            v((NB, BW), F32), v((NB, BW), F32), v((C, 128), F32), v((C, 128), F32),
            v((3, NZ, CH), F32), v((3, 7, NZ, CH), F32),
            v((2 * CH, NB * BW), BF16), v((2 * CH, NB * BW), BF16), v((NZ, CH, D), F32),
            v((14, 64, D), BF16), v((14, 64, D), BF16),
            dma((2,)), dma((48,)), dma((48,)), dma((3, 7)), dma((3, 7)), dma((3, 3)), dma((3, 3)),
            dma((3, 7)), dma((3, 7)), dma((14,)), dma((14,)),
        ],
        compiler_params=pltpu.CompilerParams(
            collective_id=0, has_side_effects=True, vmem_limit_bytes=60 * 1024 * 1024
        ),
        cost_estimate=pl.CostEstimate(
            flops=4 * C * NB * BW * D, bytes_accessed=8 * 1024 * 1024, transcendentals=C * NB * BW
        ),
    )(e, k)
    return out[None]


def solution(mesh):
    return jax.shard_map(
        local,
        mesh=mesh,
        in_specs=(P("docs", None), P("cent", None)),
        out_specs=P("cent", "docs", None),
        check_vma=False,
    )
```

```python
import jax
import jax.numpy as jnp
import numpy as np
from jax import lax
from jax.experimental import pallas as pl
from jax.experimental.pallas import tpu as pltpu
from jax.sharding import PartitionSpec as P

MESH = pl.DeviceIdType.MESH
F32 = jnp.float32
BF16 = jnp.bfloat16

NX, NY, NZ = 4, 4, 8
D = 768
PIECE = 64
NB, BW = 8, 512
CH = 128
C = NZ * CH
TOTAL = 32768.0
EXP2_SCALE = 10.0 * float(np.log2(np.e))

GROUPS = ((4,), (3, -3), (2, -2), (1, -1), (0,))
POS = {q: i for i, q in enumerate(q for group in GROUPS for q in group)}
LN2 = float(np.log(2.0))


def body(
    emb_hbm, cen_hbm, out_ref,
    emb, cen, kern, buf0, buf1,
    top_of, rl, rl2, ra, rb, fac, rw, part, scol, ml, mr, w0, w1, num, snd, rcv,
    ld_sem, ag_s, ag_r, r1_s, r1_r, r2_s, r2_r, m_s, m_r, rs_s, rs_r,
):
    docs = lax.axis_index("docs")
    cent = lax.axis_index("cent")
    z, y = docs // NY, docs % NY
    x, c = cent // 2, cent % 2

    def at(dz=0, dy=0, dx=0, flip=False):
        zz = (z + dz + NZ) % NZ
        yy = (y + dy + NY) % NY
        xx = (x + dx + NX) % NX
        return (zz * NY + yy, xx * 2 + ((1 - c) if flip else c))

    load_e = pltpu.make_async_copy(emb_hbm, emb.at[pl.ds(y * 16, 16)], ld_sem.at[0])
    load_c = pltpu.make_async_copy(cen_hbm.at[:, y], cen, ld_sem.at[1])
    load_e.start()
    load_c.start()

    cent_peers = [(docs, (cent + k) % 8) for k in range(1, 8)]
    y_peers = [at(dy=k) for k in range(1, NY)]
    z_peers = [at(dz=k) for k in range(1, NZ)]
    barrier = pltpu.get_barrier_semaphore()
    for peer in cent_peers + y_peers + z_peers:
        pl.semaphore_signal(barrier, inc=1, device_id=peer, device_id_type=MESH)
    pl.semaphore_wait(barrier, len(cent_peers) + len(y_peers) + len(z_peers))

    def piece(dy, h, dx):
        return ((y + dy + NY) % NY) * 16 + h * 8 + ((x + dx + NX) % NX) * 2 + c

    ag = {}

    def send(name, where, target, src=None):
        i = len(ag)
        copy = pltpu.make_async_remote_copy(
            src_ref=emb.at[where] if src is None else src, dst_ref=emb.at[where],
            send_sem=ag_s.at[i], recv_sem=ag_r.at[i], device_id=target, device_id_type=MESH,
        )
        copy.start()
        ag[name] = copy

    def send_own(name, h, dx, s):
        send(name, piece(0, h, dx), at(dy=s), emb_hbm.at[h * 8 + ((x + dx + NX) % NX) * 2 + c])

    def got(*names):
        for name in names:
            ag[name].wait_recv()

    def to_sibling(*pieces):
        for dy, h, dx in pieces:
            send(("s", dy, h, dx), piece(dy, h, dx), at(flip=True))

    def to_x(*pieces):
        for s, dy, h in pieces:
            send(("x1", s, dy, h), piece(dy, h, 0), at(dx=s))

    def block_ready(dy, h):
        for dx in (0, 1, 2, -1):
            got(("s", dy, h, dx))

    send_own(("f", 1), 1, 0, 1)
    send_own(("f", -1), 0, 0, -1)
    send_own(("g", 1), 0, 0, 1)
    send_own(("g", -1), 1, 0, -1)
    load_e.wait()
    load_c.wait()

    def phase_a():
        got(("f", 1), ("f", -1))
        to_x((1, -1, 1), (-1, -1, 1))
        send(("y3", 1), piece(-1, 1, 0), at(dy=1))
        send(("y3", -1), piece(1, 0, 0), at(dy=-1))
        for k in (1, 2, -1):
            for s in (1, -1):
                send_own(("k", s, k), 0, k, s)
        to_sibling((-1, 1, 0), (1, 0, 0))

    def phase_b():
        got(("g", 1), ("g", -1))
        to_x((1, 1, 1), (-1, 1, 1))
        to_sibling((-1, 0, 0), (1, 1, 0))

    def phase_c():
        got(("x1", -1, -1, 1), ("x1", 1, -1, 1))
        send(("x2", -1, -1, 1), piece(-1, 1, 1), at(dx=-1))
        to_sibling((-1, 1, 1), (-1, 1, -1))
        got(("x1", 1, 1, 1), ("x1", -1, 1, 1))
        send(("x2", 1, 1, 1), piece(1, 1, -1), at(dx=1))
        to_sibling((1, 1, -1), (1, 1, 1))
        got(("y3", 1), ("y3", -1))
        to_x((1, 2, 0), (-1, 2, 1), (1, 2, 1), (-1, 2, 0))
        to_sibling((2, 1, 0), (2, 0, 0))
        got(("x2", 1, 1, 1), ("x2", -1, -1, 1))
        to_sibling((1, 1, 2), (-1, 1, 2))

    def phase_f():
        for k in (1, 2):
            got(("k", 1, k), ("k", -1, k))
            to_sibling((1, 0, k), (-1, 0, k))

    def phase_g():
        got(("x1", 1, 2, 0), ("x1", -1, 2, 1))
        send(("x2", 1, 2, 0), piece(2, 0, -1), at(dx=1))
        send(("x2", -1, 2, 1), piece(2, 1, 1), at(dx=-1))
        to_sibling((2, 0, -1), (2, 1, 1))
        got(("k", 1, -1), ("k", -1, -1))
        to_sibling((1, 0, -1), (-1, 0, -1))

    def phase_h():
        got(("x1", 1, 2, 1), ("x1", -1, 2, 0))
        to_sibling((2, 1, -1), (2, 0, 1))

    def phase_i():
        got(("x2", 1, 2, 0), ("x2", -1, 2, 1))
        to_sibling((2, 0, 2), (2, 1, 2))

    sent = []

    def push(src, dst, peers, ssem, rsem):
        copies = []
        for k, peer in enumerate(peers):
            copy = pltpu.make_async_remote_copy(
                src_ref=src, dst_ref=dst.at[k], send_sem=ssem.at[k], recv_sem=rsem.at[k],
                device_id=peer, device_id_type=MESH,
            )
            copy.start()
            copies.append(copy)
        sent.extend(copies)
        return copies

    def landed(copies):
        for copy in copies:
            copy.wait_recv()

    def push_1(n, half):
        return push(rl.at[n, half], ra.at[n, half], cent_peers, r1_s.at[n, half], r1_r.at[n, half])

    def push_2(n, half):
        return push(rl2.at[n, half], rb.at[n, half], y_peers, r2_s.at[n, half], r2_r.at[n, half])

    def summed(own, others, n):
        total = own
        for k in range(n):
            total = total + others[k]
        return total

    def log_summed(own, others, n):
        top = own
        for k in range(n):
            top = jnp.maximum(top, others[k])
        total = jnp.exp2(own - top)
        for k in range(n):
            total = total + jnp.exp2(others[k] - top)
        return top + jnp.log(total) * (1.0 / LN2)

    def block_at(dy, h):
        return ((y + dy + NY) % NY) * 2 + h

    blocks = ((0, 0), (0, 1), (1, 1), (-1, 1), (1, 0), (-1, 0), (2, 0), (2, 1))
    bufs = (buf0, buf1)
    highs = {}

    def step(new, old):
        if old is not None:
            top = jnp.max(highs[old], axis=0, keepdims=True)
            total = jnp.zeros((8, BW), F32)
            old_buf, place = bufs[old % 2], block_at(*blocks[old])
        if new is not None:
            e = emb[pl.ds(block_at(*blocks[new]) * 8, 8)].reshape(BW, D)
            new_buf, new_max = bufs[new % 2], None
        for i in range(4):
            rows = slice(256 * i, 256 * i + 256)
            if new is not None:
                raw = lax.dot_general(
                    cen[2 * i:2 * i + 2].reshape(256, D), e, (((1,), (1,)), ((), ())),
                    preferred_element_type=F32,
                )
                new_buf[rows, :] = raw
                high = jnp.max(raw.reshape(32, 8, BW), axis=0)
                new_max = high if new_max is None else jnp.maximum(new_max, high)
            if old is not None:
                value = jnp.exp2((old_buf[rows, :] - top) * EXP2_SCALE)
                kern[place, rows, :] = value
                total = total + jnp.sum(value.reshape(32, 8, BW), axis=0)
        if new is not None:
            highs[new] = new_max
        if old is not None:
            scaled = top * EXP2_SCALE
            whole = scaled + jnp.log(jnp.sum(total, axis=0, keepdims=True)) * (1.0 / LN2)
            for j in range(2):
                lanes = slice(256 * j, 256 * j + 256)
                r = (old % 4) * 2 + j
                rl[0, old // 4, r:r + 1, :] = whole[:, lanes]
                top_of[place // 4, pl.ds((place % 4) * 2 + j, 1), :] = scaled[:, lanes]

    step(0, None)
    phase_a()
    step(1, 0)
    phase_b()
    step(None, 1)
    phase_c()
    block_ready(*blocks[2])
    step(2, None)
    phase_f()
    block_ready(*blocks[3])
    step(3, 2)
    phase_g()
    block_ready(*blocks[4])
    step(4, 3)
    first = push_1(0, 0)
    phase_h()
    block_ready(*blocks[5])
    step(5, 4)
    phase_i()
    block_ready(*blocks[6])
    step(6, 5)
    block_ready(*blocks[7])
    step(7, 6)
    step(None, 7)
    second = push_1(0, 1)
    for half, copies in ((0, first), (1, second)):
        landed(copies)
        merged = log_summed(rl[0, half], ra.at[0, half], 7)
        for j in range(8):
            place = block_at(*blocks[4 * half + j // 2])
            rl2[0, place // 4, pl.ds((place % 4) * 2 + j % 2, 1), :] = merged[j:j + 1, :]
    first, second = push_2(0, 0), push_2(0, 1)

    def start_weights(half):
        whole = log_summed(rl2[0, half], rb.at[0, half], 3)
        factor = jnp.exp2(top_of[half] - whole)
        fac[half] = factor
        rw[half] = factor * (1.0 / TOTAL)

    landed(first)
    start_weights(0)

    def weighted(b, rows, l):
        r = (b % 4) * 2 + l // 2
        w = rw[b // 4, r:r + 1, (l % 2) * 128:(l % 2) * 128 + 128]
        return kern[b, rows, l * 128:l * 128 + 128] * w

    def mass_half(half):
        def chunk(g, _):
            rows = pl.ds(pl.multiple_of(g * 64, 64), 64)
            acc = jnp.zeros((64, 128), F32) if half == 0 else part[rows, :]
            for b in range(4 * half, 4 * half + 4):
                for l in range(BW // 128):
                    acc = acc + weighted(b, rows, l)
            part[rows, :] = acc
            return 0

        lax.fori_loop(0, C // 64, chunk, 0)

    def row_half(n, half):
        def row_block(b, _):
            def chunk(g, acc):
                rows = pl.ds(pl.multiple_of(g * 128, 128), 128)
                s = scol[rows, :]
                value = kern[4 * half + b, rows, :] * jnp.concatenate([s] * (BW // 128), axis=1)
                return acc + jnp.sum(value.reshape(16, 8, BW), axis=0)

            acc = lax.fori_loop(0, C // 128, chunk, jnp.zeros((8, BW), F32))
            acc = jnp.sum(acc, axis=0, keepdims=True)
            for j in range(2):
                r = pl.ds(b * 2 + j, 1)
                rl[n, half, r, :] = acc[:, 256 * j:256 * j + 256] * fac[half, r, :]
            return 0

        lax.fori_loop(0, 4, row_block, 0)

    for n in range(2):
        mass_half(0)
        landed(second)
        if n == 0:
            start_weights(1)
        else:
            rw[1] = fac[1] / (TOTAL * summed(rl2[n, 1], rb.at[n, 1], 3))
        mass_half(1)
        for t in range(NZ):
            ml[n, t:t + 1, :] = jnp.sum(part[t * CH:(t + 1) * CH, :].T, axis=0, keepdims=True)
        landed(push(ml.at[n], mr.at[n], z_peers, m_s.at[n], m_r.at[n]))
        scale = 1.0 / (TOTAL * summed(ml[n], mr.at[n], 7))
        for t in range(NZ):
            scol[t * CH:(t + 1) * CH, :] = jnp.broadcast_to(scale[t:t + 1, :], (CH, CH)).T
        row_half(n + 1, 0)
        first = push_1(n + 1, 0)
        row_half(n + 1, 1)
        second = push_1(n + 1, 1)
        landed(first)
        rl2[n + 1, 0] = summed(rl[n + 1, 0], ra.at[n + 1, 0], 7)
        first = push_2(n + 1, 0)
        landed(second)
        rl2[n + 1, 1] = summed(rl[n + 1, 1], ra.at[n + 1, 1], 7)
        second = push_2(n + 1, 1)
        landed(first)
        rw[0] = fac[0] / (TOTAL * summed(rl2[n + 1, 0], rb.at[n + 1, 0], 3))

    ws = (w0, w1)

    def weigh(i, halfway=None):
        for j, q in enumerate(GROUPS[i]):
            t = (z + q + NZ) % NZ
            rows = pl.ds(pl.multiple_of(t * CH, CH), CH)
            acc = jnp.zeros((CH, 128), F32)
            for b in range(NB):
                if b == 4 and halfway is not None:
                    halfway()
                for l in range(BW // 128):
                    value = weighted(b, rows, l)
                    acc = acc + value
                    ws[i % 2][j * CH:(j + 1) * CH, b * BW + l * 128:b * BW + (l + 1) * 128] = value.astype(BF16)
            ml[2, pl.ds(t, 1), :] = jnp.sum(acc.T, axis=0, keepdims=True)

    def multiply(i):
        n = len(GROUPS[i])
        first = POS[GROUPS[i][0]]
        e = emb[...].reshape(NB * BW, D)
        num[first:first + n] = jnp.dot(
            ws[i % 2][0:n * CH, :], e, preferred_element_type=F32
        ).reshape(n, CH, D)

    rs = {}

    def hop(name, q, rows, before=None):
        sign = (1 if name[0] in ("RA", "RB") else -1)
        i = len(rs)
        value = num[POS[q], rows, :]
        if before is not None:
            rs[before].wait_recv()
            value = value + rcv[slot[before]].astype(F32)
        snd[i] = value.astype(BF16)
        slot[name] = i
        copy = pltpu.make_async_remote_copy(
            src_ref=snd.at[i], dst_ref=rcv.at[i], send_sem=rs_s.at[i], recv_sem=rs_r.at[i],
            device_id=at(dz=sign), device_id_type=MESH,
        )
        copy.start()
        rs[name] = copy

    slot = {}
    lo, hi = slice(0, 64), slice(64, 128)

    def last_weights():
        landed(second)
        rw[1] = fac[1] / (TOTAL * summed(rl2[2, 1], rb.at[2, 1], 3))

    weigh(0, last_weights)
    for i in range(5):
        multiply(i)
        if i < 4:
            weigh(i + 1)
        if i == 0:
            hop(("RB", 0), 4, lo)
            hop(("LB", 0), 4, hi)
        elif i == 1:
            hop(("RA", 1), 3, hi)
            hop(("LA", 1), -3, lo)
        elif i == 2:
            hop(("RB", 1), 3, lo, ("RB", 0))
            hop(("LB", 1), -3, hi, ("LB", 0))
        elif i == 3:
            hop(("RA", 2), 2, hi, ("RA", 1))
            hop(("LA", 2), -2, lo, ("LA", 1))
            last = push(ml.at[2], mr.at[2], z_peers, m_s.at[2], m_r.at[2])
    hop(("RB", 2), 2, lo, ("RB", 1))
    hop(("LB", 2), -2, hi, ("LB", 1))
    hop(("RA", 3), 1, hi, ("RA", 2))
    hop(("LA", 3), -1, lo, ("LA", 2))
    hop(("RB", 3), 1, lo, ("RB", 2))
    hop(("LB", 3), -1, hi, ("LB", 2))

    for copy in last:
        copy.wait_recv()
    mass = ml[2, pl.ds(z, 1), :]
    for k in range(7):
        mass = mass + mr[2, k, pl.ds(z, 1), :]
    column = jnp.broadcast_to(mass, (CH, CH)).T
    column = jnp.concatenate([column] * (D // CH), axis=1)
    for rows, one, two in ((hi, ("RA", 3), ("LB", 3)), (lo, ("LA", 3), ("RB", 3))):
        rs[one].wait_recv()
        rs[two].wait_recv()
        total = num[POS[0], rows, :] + rcv[slot[one]].astype(F32) + rcv[slot[two]].astype(F32)
        out_ref[rows, :] = (total / column[rows, :]).astype(BF16)

    for copy in list(ag.values()) + sent + list(rs.values()):
        copy.wait_send()


def local(embeddings, centroids):
    e = embeddings.reshape(16, PIECE, D)
    k = centroids.reshape(NZ, NY, CH, D)
    dma = pltpu.SemaphoreType.DMA
    v = pltpu.VMEM
    out = pl.pallas_call(
        body,
        out_shape=jax.ShapeDtypeStruct((CH, D), BF16),
        in_specs=[pl.BlockSpec(memory_space=pl.ANY)] * 2,
        out_specs=pl.BlockSpec(memory_space=pltpu.VMEM),
        scratch_shapes=[
            v((64, PIECE, D), BF16), v((NZ, CH, D), BF16), v((NB, C, BW), F32), v((C, BW), F32), v((C, BW), F32),
            v((2, 8, 256), F32), v((3, 2, 8, 256), F32), v((3, 2, 8, 256), F32),
            v((3, 2, 7, 8, 256), F32), v((3, 2, 3, 8, 256), F32),
            v((2, 8, 256), F32), v((2, 8, 256), F32), v((C, 128), F32), v((C, 128), F32),
            v((3, NZ, CH), F32), v((3, 7, NZ, CH), F32),
            v((2 * CH, NB * BW), BF16), v((2 * CH, NB * BW), BF16), v((NZ, CH, D), F32),
            v((14, 64, D), BF16), v((14, 64, D), BF16),
            dma((2,)), dma((48,)), dma((48,)), dma((3, 2, 7)), dma((3, 2, 7)), dma((3, 2, 3)), dma((3, 2, 3)),
            dma((3, 7)), dma((3, 7)), dma((14,)), dma((14,)),
        ],
        compiler_params=pltpu.CompilerParams(
            collective_id=0, has_side_effects=True, vmem_limit_bytes=60 * 1024 * 1024
        ),
        cost_estimate=pl.CostEstimate(
            flops=4 * C * NB * BW * D, bytes_accessed=8 * 1024 * 1024, transcendentals=C * NB * BW
        ),
    )(e, k)
    return out[None]


def solution(mesh):
    return jax.shard_map(
        local,
        mesh=mesh,
        in_specs=(P("docs", None), P("cent", None)),
        out_specs=P("cent", "docs", None),
        check_vma=False,
    )
```

```python
import jax
import jax.numpy as jnp
import numpy as np
from jax import lax
from jax.experimental import pallas as pl
from jax.experimental.pallas import tpu as pltpu
from jax.sharding import PartitionSpec as P

MESH = pl.DeviceIdType.MESH
F32 = jnp.float32
BF16 = jnp.bfloat16

NX, NY, NZ = 4, 4, 8
D = 768
PIECE = 64
NB, BW = 8, 512
CH = 128
C = NZ * CH
TOTAL = 32768.0
EXP2_SCALE = 10.0 * float(np.log2(np.e))

GROUPS = ((4, 3), (-3, 2), (-2, 1), (-1, 0))
POS = {q: i for i, q in enumerate(q for group in GROUPS for q in group)}
LN2 = float(np.log(2.0))


def body(
    emb_hbm, cen_hbm, out_ref,
    emb, cen, kern, buf0, buf1,
    top_of, rl, rl2, ra, rb, fac, rw, part, scol, ml, mr, w0, w1, num, snd, rcv,
    ld_sem, ag_s, ag_r, r1_s, r1_r, r2_s, r2_r, m_s, m_r, rs_s, rs_r,
):
    docs = lax.axis_index("docs")
    cent = lax.axis_index("cent")
    z, y = docs // NY, docs % NY
    x, c = cent // 2, cent % 2

    def at(dz=0, dy=0, dx=0, flip=False):
        zz = (z + dz + NZ) % NZ
        yy = (y + dy + NY) % NY
        xx = (x + dx + NX) % NX
        return (zz * NY + yy, xx * 2 + ((1 - c) if flip else c))

    load_e = pltpu.make_async_copy(emb_hbm, emb.at[pl.ds(y * 16, 16)], ld_sem.at[0])
    load_c = pltpu.make_async_copy(cen_hbm.at[:, y], cen, ld_sem.at[1])
    load_e.start()
    load_c.start()

    cent_peers = [(docs, (cent + k) % 8) for k in range(1, 8)]
    y_peers = [at(dy=k) for k in range(1, NY)]
    z_peers = [at(dz=k) for k in range(1, NZ)]
    barrier = pltpu.get_barrier_semaphore()
    for peer in cent_peers + y_peers + z_peers:
        pl.semaphore_signal(barrier, inc=1, device_id=peer, device_id_type=MESH)
    pl.semaphore_wait(barrier, len(cent_peers) + len(y_peers) + len(z_peers))

    def piece(dy, h, dx):
        return ((y + dy + NY) % NY) * 16 + h * 8 + ((x + dx + NX) % NX) * 2 + c

    ag = {}

    def plan(name, where, target, src=None):
        i = len(ag)
        ag[name] = pltpu.make_async_remote_copy(
            src_ref=emb.at[where] if src is None else src, dst_ref=emb.at[where],
            send_sem=ag_s.at[i], recv_sem=ag_r.at[i], device_id=target, device_id_type=MESH,
        )

    def plan_own(name, h, dx, s):
        plan(name, piece(0, h, dx), at(dy=s), emb_hbm.at[h * 8 + ((x + dx + NX) % NX) * 2 + c])

    plan_own(("f", 1), 1, 0, 1)
    plan_own(("f", -1), 0, 0, -1)
    plan_own(("g", 1), 0, 0, 1)
    plan_own(("g", -1), 1, 0, -1)
    plan(("y3", 1), piece(-1, 1, 0), at(dy=1))
    plan(("y3", -1), piece(1, 0, 0), at(dy=-1))
    for k in (1, 2, -1):
        for s in (1, -1):
            plan_own(("k", s, k), 0, k, s)
    for dy, h in ((-1, 1), (1, 1), (2, 0), (2, 1)):
        for s in (1, -1):
            plan(("x1", s, dy, h), piece(dy, h, 0), at(dx=s))
    for s, dy, h in ((-1, -1, 1), (1, 1, 1), (1, 2, 0), (-1, 2, 1)):
        plan(("x2", s, dy, h), piece(dy, h, -s), at(dx=s))
    for dy in (-1, 1, 2):
        for h in (0, 1):
            for dx in (0, 1, 2, -1):
                plan(("s", dy, h, dx), piece(dy, h, dx), at(flip=True))

    def send(*names):
        for name in names:
            ag[name].start()

    def got(*names):
        for name in names:
            ag[name].wait_recv()

    def to_sibling(*pieces):
        send(*[("s", *p) for p in pieces])

    def block_ready(dy, h):
        got(*[("s", dy, h, dx) for dx in (0, 1, 2, -1)])

    send(("f", 1), ("f", -1), ("g", 1), ("g", -1))
    load_e.wait()
    load_c.wait()

    def phase_a():
        got(("f", 1), ("f", -1))
        send(("x1", 1, -1, 1), ("x1", -1, -1, 1), ("y3", 1), ("y3", -1))
        send(*[("k", s, k) for k in (1, 2, -1) for s in (1, -1)])
        to_sibling((-1, 1, 0), (1, 0, 0))

    def phase_c():
        got(("g", 1), ("g", -1))
        send(("x1", 1, 1, 1), ("x1", -1, 1, 1))
        to_sibling((-1, 0, 0), (1, 1, 0))
        got(("x1", -1, -1, 1), ("x1", 1, -1, 1))
        send(("x2", -1, -1, 1))
        to_sibling((-1, 1, 1), (-1, 1, -1))
        got(("x1", 1, 1, 1), ("x1", -1, 1, 1))
        send(("x2", 1, 1, 1))
        to_sibling((1, 1, -1), (1, 1, 1))
        got(("y3", 1), ("y3", -1))
        send(("x1", 1, 2, 0), ("x1", -1, 2, 1), ("x1", 1, 2, 1), ("x1", -1, 2, 0))
        to_sibling((2, 1, 0), (2, 0, 0))
        got(("x2", 1, 1, 1), ("x2", -1, -1, 1))
        to_sibling((1, 1, 2), (-1, 1, 2))
        block_ready(1, 1)

    def phase_f():
        for k in (1, 2):
            got(("k", 1, k), ("k", -1, k))
            to_sibling((1, 0, k), (-1, 0, k))
        block_ready(-1, 1)

    def phase_g():
        got(("x1", 1, 2, 0), ("x1", -1, 2, 1))
        send(("x2", 1, 2, 0), ("x2", -1, 2, 1))
        to_sibling((2, 0, -1), (2, 1, 1))
        got(("k", 1, -1), ("k", -1, -1))
        to_sibling((1, 0, -1), (-1, 0, -1))
        block_ready(1, 0)

    def phase_h():
        got(("x1", 1, 2, 1), ("x1", -1, 2, 0))
        to_sibling((2, 1, -1), (2, 0, 1))
        block_ready(-1, 0)

    def phase_i():
        got(("x2", 1, 2, 0), ("x2", -1, 2, 1))
        to_sibling((2, 0, 2), (2, 1, 2))
        block_ready(2, 0)

    def phase_j():
        block_ready(2, 1)

    sent = []

    def push(src, dst, peers, ssem, rsem, start=True):
        copies = []
        for k, peer in enumerate(peers):
            copy = pltpu.make_async_remote_copy(
                src_ref=src, dst_ref=dst.at[k], send_sem=ssem.at[k], recv_sem=rsem.at[k],
                device_id=peer, device_id_type=MESH,
            )
            copies.append(copy)
        sent.extend(copies)
        if start:
            begin(copies)
        return copies

    def begin(copies):
        for copy in copies:
            copy.start()

    def landed(copies):
        for copy in copies:
            copy.wait_recv()

    def push_1(n, half, start=True):
        return push(rl.at[n, half], ra.at[n, half], cent_peers, r1_s.at[n, half], r1_r.at[n, half], start)

    def push_2(n, half):
        return push(rl2.at[n, half], rb.at[n, half], y_peers, r2_s.at[n, half], r2_r.at[n, half])

    def summed(own, others, n):
        total = own
        for k in range(n):
            total = total + others[k]
        return total

    def log_summed(own, others, n):
        top = own
        for k in range(n):
            top = jnp.maximum(top, others[k])
        total = jnp.exp2(own - top)
        for k in range(n):
            total = total + jnp.exp2(others[k] - top)
        return top + jnp.log(total) * (1.0 / LN2)

    def place_of(p, odd):
        d = (p + 1) // 2
        if odd:
            return ((y - d + NY) % NY) * 2 + 1 - (1 - p % 2) * (p // 2)
        return ((y + d) % NY) * 2 + (p % 2) * (1 - p // 2)

    def step(new_buf, new, old_buf, old, old_max, half, row):
        top = jnp.max(old_max, axis=0, keepdims=True)
        total = jnp.zeros((8, BW), F32)
        new_max = None
        if new is not None:
            e = emb[pl.ds(new * 8, 8)].reshape(BW, D)
        for i in range(4):
            rows = slice(256 * i, 256 * i + 256)
            if new is not None:
                raw = lax.dot_general(
                    cen[2 * i:2 * i + 2].reshape(256, D), e, (((1,), (1,)), ((), ())),
                    preferred_element_type=F32,
                )
                new_buf[rows, :] = raw
                high = jnp.max(raw.reshape(32, 8, BW), axis=0)
                new_max = high if new_max is None else jnp.maximum(new_max, high)
            value = jnp.exp2((old_buf[rows, :] - top) * EXP2_SCALE)
            kern[old, rows, :] = value
            total = total + jnp.sum(value.reshape(32, 8, BW), axis=0)
        scaled = top * EXP2_SCALE
        whole = scaled + jnp.log(jnp.sum(total, axis=0, keepdims=True)) * (1.0 / LN2)
        for j in range(2):
            lanes = slice(256 * j, 256 * j + 256)
            rl[0, half, pl.ds(row + j, 1), :] = whole[:, lanes]
            top_of[old // 4, pl.ds((old % 4) * 2 + j, 1), :] = scaled[:, lanes]
        return new_max

    first = push_1(0, 0, start=False)

    def two_steps(p, high):
        pl.when(p == 1)(phase_c)
        pl.when(p == 2)(phase_g)
        pl.when(p == 3)(phase_i)
        q = (p + 3) % 4
        high = step(buf0, place_of(p, False), buf1, place_of(q, True), high, q // 2, (q % 2) * 4 + 2)
        pl.when(p == 0)(phase_a)
        pl.when(p == 1)(phase_f)

        @pl.when(p == 2)
        def _():
            begin(first)
            phase_h()

        pl.when(p == 3)(phase_j)
        return step(buf1, place_of(p, True), buf0, place_of(p, False), high, p // 2, (p % 2) * 4)

    buf1[...] = jnp.zeros((C, BW), F32)
    high = lax.fori_loop(0, 4, two_steps, jnp.zeros((8, BW), F32))
    step(None, None, buf1, place_of(3, True), high, 1, 6)
    second = push_1(0, 1)
    for half, copies in ((0, first), (1, second)):
        landed(copies)
        merged = log_summed(rl[0, half], ra.at[0, half], 7)
        for j in range(8):
            place = place_of(2 * half + j // 4, j // 2 % 2 == 1)
            rl2[0, place // 4, pl.ds((place % 4) * 2 + j % 2, 1), :] = merged[j:j + 1, :]
    first, second = push_2(0, 0), push_2(0, 1)

    def start_weights(half):
        whole = log_summed(rl2[0, half], rb.at[0, half], 3)
        factor = jnp.exp2(top_of[half] - whole)
        fac[half] = factor
        rw[half] = factor * (1.0 / TOTAL)

    landed(first)
    start_weights(0)

    def weighted(b, rows, l):
        r = (b % 4) * 2 + l // 2
        w = rw[b // 4, r:r + 1, (l % 2) * 128:(l % 2) * 128 + 128]
        return kern[b, rows, l * 128:l * 128 + 128] * w

    def mass_half(half):
        def chunk(g, _):
            rows = pl.ds(pl.multiple_of(g * 64, 64), 64)
            acc = jnp.zeros((64, 128), F32) if half == 0 else part[rows, :]
            for b in range(4 * half, 4 * half + 4):
                for l in range(BW // 128):
                    acc = acc + weighted(b, rows, l)
            part[rows, :] = acc
            return 0

        lax.fori_loop(0, C // 64, chunk, 0)

    def row_half(n, half):
        def row_block(b, _):
            def chunk(g, acc):
                rows = pl.ds(pl.multiple_of(g * 128, 128), 128)
                s = scol[rows, :]
                value = kern[4 * half + b, rows, :] * jnp.concatenate([s] * (BW // 128), axis=1)
                return acc + jnp.sum(value.reshape(16, 8, BW), axis=0)

            acc = lax.fori_loop(0, C // 128, chunk, jnp.zeros((8, BW), F32))
            acc = jnp.sum(acc, axis=0, keepdims=True)
            for j in range(2):
                r = pl.ds(b * 2 + j, 1)
                rl[n, half, r, :] = acc[:, 256 * j:256 * j + 256] * fac[half, r, :]
            return 0

        lax.fori_loop(0, 4, row_block, 0)

    for n in range(2):
        mass_half(0)
        landed(second)
        if n == 0:
            start_weights(1)
        else:
            rw[1] = fac[1] / (TOTAL * summed(rl2[n, 1], rb.at[n, 1], 3))
        mass_half(1)
        for t in range(NZ):
            ml[n, t:t + 1, :] = jnp.sum(part[t * CH:(t + 1) * CH, :].T, axis=0, keepdims=True)
        landed(push(ml.at[n], mr.at[n], z_peers, m_s.at[n], m_r.at[n]))
        scale = 1.0 / (TOTAL * summed(ml[n], mr.at[n], 7))
        for t in range(NZ):
            scol[t * CH:(t + 1) * CH, :] = jnp.broadcast_to(scale[t:t + 1, :], (CH, CH)).T
        row_half(n + 1, 0)
        first = push_1(n + 1, 0)
        row_half(n + 1, 1)
        second = push_1(n + 1, 1)
        landed(first)
        rl2[n + 1, 0] = summed(rl[n + 1, 0], ra.at[n + 1, 0], 7)
        first = push_2(n + 1, 0)
        landed(second)
        rl2[n + 1, 1] = summed(rl[n + 1, 1], ra.at[n + 1, 1], 7)
        second = push_2(n + 1, 1)
        landed(first)
        rw[0] = fac[0] / (TOTAL * summed(rl2[n + 1, 0], rb.at[n + 1, 0], 3))

    def chunk_at(q):
        return (z + q + NZ) % NZ

    def weigh(w, i, b):
        ws = [rw[b // 4, pl.ds((b % 4) * 2 + j, 1), :] for j in range(2)]
        for j, q in enumerate(GROUPS[i]):
            rows = pl.ds(pl.multiple_of(chunk_at(q) * CH, CH), CH)
            place = slice((2 * i + j) * CH, (2 * i + j + 1) * CH)
            acc = part[place, :]
            for l in range(BW // 128):
                value = kern[b, rows, l * 128:l * 128 + 128] * ws[l // 2][:, (l % 2) * 128:(l % 2) * 128 + 128]
                acc = acc + value
                w[j * CH:(j + 1) * CH, l * 128:(l + 1) * 128] = value.astype(BF16)
            part[place, :] = acc

    def multiply(w, i, b):
        e = emb[pl.ds(b * 8, 8)].reshape(BW, D)
        num[2 * i:2 * i + 2] += jnp.dot(w[...], e, preferred_element_type=F32).reshape(2, CH, D)

    def group(i):
        num[2 * i:2 * i + 2] = jnp.zeros((2, CH, D), F32)

        def two(k, _):
            weigh(w1, i, 2 * k + 1)
            multiply(w0, i, 2 * k)
            weigh(w0, i, 2 * k + 2)
            multiply(w1, i, 2 * k + 1)
            return 0

        lax.fori_loop(0, 3, two, 0)
        weigh(w1, i, 7)
        multiply(w0, i, 6)
        if i < 3:
            weigh(w0, i + 1, 0)
        multiply(w1, i, 7)

    rs = {}

    def hop(name, q, rows, before=None):
        sign = (1 if name[0] in ("RA", "RB") else -1)
        i = len(rs)
        value = num[POS[q], rows, :]
        if before is not None:
            rs[before].wait_recv()
            value = value + rcv[slot[before]].astype(F32)
        snd[i] = value.astype(BF16)
        slot[name] = i
        copy = pltpu.make_async_remote_copy(
            src_ref=snd.at[i], dst_ref=rcv.at[i], send_sem=rs_s.at[i], recv_sem=rs_r.at[i],
            device_id=at(dz=sign), device_id_type=MESH,
        )
        copy.start()
        rs[name] = copy

    slot = {}
    lo, hi = slice(0, 64), slice(64, 128)

    part[...] = jnp.zeros((C, 128), F32)
    weigh(w0, 0, 0)
    landed(second)
    rw[1] = fac[1] / (TOTAL * summed(rl2[2, 1], rb.at[2, 1], 3))
    for i in range(4):
        group(i)
        if i == 0:
            hop(("RB", 0), 4, lo)
            hop(("LB", 0), 4, hi)
            hop(("RA", 1), 3, hi)
        elif i == 1:
            hop(("LA", 1), -3, lo)
        elif i == 2:
            hop(("RB", 1), 3, lo, ("RB", 0))
            hop(("LB", 1), -3, hi, ("LB", 0))
    for j, q in enumerate(q for g in GROUPS for q in g):
        ml[2, pl.ds(chunk_at(q), 1), :] = jnp.sum(part[j * CH:(j + 1) * CH, :].T, axis=0, keepdims=True)
    last = push(ml.at[2], mr.at[2], z_peers, m_s.at[2], m_r.at[2])
    hop(("RA", 2), 2, hi, ("RA", 1))
    hop(("LA", 2), -2, lo, ("LA", 1))
    hop(("RB", 2), 2, lo, ("RB", 1))
    hop(("LB", 2), -2, hi, ("LB", 1))
    hop(("RA", 3), 1, hi, ("RA", 2))
    hop(("LA", 3), -1, lo, ("LA", 2))
    hop(("RB", 3), 1, lo, ("RB", 2))
    hop(("LB", 3), -1, hi, ("LB", 2))

    for copy in last:
        copy.wait_recv()
    mass = ml[2, pl.ds(z, 1), :]
    for k in range(7):
        mass = mass + mr[2, k, pl.ds(z, 1), :]
    column = jnp.broadcast_to(mass, (CH, CH)).T
    column = jnp.concatenate([column] * (D // CH), axis=1)
    for rows, one, two in ((hi, ("RA", 3), ("LB", 3)), (lo, ("LA", 3), ("RB", 3))):
        rs[one].wait_recv()
        rs[two].wait_recv()
        total = num[POS[0], rows, :] + rcv[slot[one]].astype(F32) + rcv[slot[two]].astype(F32)
        out_ref[rows, :] = (total / column[rows, :]).astype(BF16)

    for copy in list(ag.values()) + sent + list(rs.values()):
        copy.wait_send()


def local(embeddings, centroids):
    e = embeddings.reshape(16, PIECE, D)
    k = centroids.reshape(NZ, NY, CH, D)
    dma = pltpu.SemaphoreType.DMA
    v = pltpu.VMEM
    out = pl.pallas_call(
        body,
        out_shape=jax.ShapeDtypeStruct((CH, D), BF16),
        in_specs=[pl.BlockSpec(memory_space=pl.ANY)] * 2,
        out_specs=pl.BlockSpec(memory_space=pltpu.VMEM),
        scratch_shapes=[
            v((64, PIECE, D), BF16), v((NZ, CH, D), BF16), v((NB, C, BW), F32), v((C, BW), F32), v((C, BW), F32),
            v((2, 8, 256), F32), v((3, 2, 8, 256), F32), v((3, 2, 8, 256), F32),
            v((3, 2, 7, 8, 256), F32), v((3, 2, 3, 8, 256), F32),
            v((2, 8, 256), F32), v((2, 8, 256), F32), v((C, 128), F32), v((C, 128), F32),
            v((3, NZ, CH), F32), v((3, 7, NZ, CH), F32),
            v((2 * CH, BW), BF16), v((2 * CH, BW), BF16), v((NZ, CH, D), F32),
            v((14, 64, D), BF16), v((14, 64, D), BF16),
            dma((2,)), dma((48,)), dma((48,)), dma((3, 2, 7)), dma((3, 2, 7)), dma((3, 2, 3)), dma((3, 2, 3)),
            dma((3, 7)), dma((3, 7)), dma((14,)), dma((14,)),
        ],
        compiler_params=pltpu.CompilerParams(
            collective_id=0, has_side_effects=True, vmem_limit_bytes=60 * 1024 * 1024
        ),
        cost_estimate=pl.CostEstimate(
            flops=4 * C * NB * BW * D, bytes_accessed=8 * 1024 * 1024, transcendentals=C * NB * BW
        ),
    )(e, k)
    return out[None]


def solution(mesh):
    return jax.shard_map(
        local,
        mesh=mesh,
        in_specs=(P("docs", None), P("cent", None)),
        out_specs=P("cent", "docs", None),
        check_vma=False,
    )
```

```python
import jax
import jax.numpy as jnp
import numpy as np
from jax import lax
from jax.experimental import pallas as pl
from jax.experimental.pallas import tpu as pltpu
from jax.sharding import PartitionSpec as P

MESH = pl.DeviceIdType.MESH
F32 = jnp.float32
BF16 = jnp.bfloat16

NX, NY, NZ = 4, 4, 8
D = 768
PIECE = 64
NB, BW = 8, 512
CH = 128
C = NZ * CH
TOTAL = 32768.0
EXP2_SCALE = 10.0 * float(np.log2(np.e))

GROUPS = ((4, 3, -3, 2), (-2, 1, -1, 0))
GROUP = len(GROUPS[0])
POS = {q: i for i, q in enumerate(q for group in GROUPS for q in group)}
LN2 = float(np.log(2.0))


def body(
    emb_hbm, cen_hbm, out_ref,
    emb, cen, kern, buf0, buf1,
    top_of, rl, rl2, ra, rb, fac, rw, part, scol, ml, mr, w0, w1, num, snd, rcv,
    ld_sem, ag_s, ag_r, r1_s, r1_r, r2_s, r2_r, m_s, m_r, rs_s, rs_r,
):
    docs = lax.axis_index("docs")
    cent = lax.axis_index("cent")
    z, y = docs // NY, docs % NY
    x, c = cent // 2, cent % 2

    def at(dz=0, dy=0, dx=0, flip=False):
        zz = (z + dz + NZ) % NZ
        yy = (y + dy + NY) % NY
        xx = (x + dx + NX) % NX
        return (zz * NY + yy, xx * 2 + ((1 - c) if flip else c))

    load_e = pltpu.make_async_copy(emb_hbm, emb.at[pl.ds(y * 16, 16)], ld_sem.at[0])
    load_c = pltpu.make_async_copy(cen_hbm.at[:, y], cen, ld_sem.at[1])
    load_e.start()
    load_c.start()

    cent_peers = [(docs, (cent + k) % 8) for k in range(1, 8)]
    y_peers = [at(dy=k) for k in range(1, NY)]
    z_peers = [at(dz=k) for k in range(1, NZ)]
    barrier = pltpu.get_barrier_semaphore()
    for peer in cent_peers + y_peers + z_peers:
        pl.semaphore_signal(barrier, inc=1, device_id=peer, device_id_type=MESH)
    pl.semaphore_wait(barrier, len(cent_peers) + len(y_peers) + len(z_peers))

    def piece(dy, h, dx):
        return ((y + dy + NY) % NY) * 16 + h * 8 + ((x + dx + NX) % NX) * 2 + c

    ag = {}

    def plan(name, where, target, src=None):
        i = len(ag)
        ag[name] = pltpu.make_async_remote_copy(
            src_ref=emb.at[where] if src is None else src, dst_ref=emb.at[where],
            send_sem=ag_s.at[i], recv_sem=ag_r.at[i], device_id=target, device_id_type=MESH,
        )

    def plan_own(name, h, dx, s):
        plan(name, piece(0, h, dx), at(dy=s), emb_hbm.at[h * 8 + ((x + dx + NX) % NX) * 2 + c])

    plan_own(("f", 1), 1, 0, 1)
    plan_own(("f", -1), 0, 0, -1)
    plan_own(("g", 1), 0, 0, 1)
    plan_own(("g", -1), 1, 0, -1)
    plan(("y3", 1), piece(-1, 1, 0), at(dy=1))
    plan(("y3", -1), piece(1, 0, 0), at(dy=-1))
    for k in (1, 2, -1):
        for s in (1, -1):
            plan_own(("k", s, k), 0, k, s)
    for dy, h in ((-1, 1), (1, 1), (2, 0), (2, 1)):
        for s in (1, -1):
            plan(("x1", s, dy, h), piece(dy, h, 0), at(dx=s))
    for s, dy, h in ((-1, -1, 1), (1, 1, 1), (1, 2, 0), (-1, 2, 1)):
        plan(("x2", s, dy, h), piece(dy, h, -s), at(dx=s))
    for dy in (-1, 1, 2):
        for h in (0, 1):
            for dx in (0, 1, 2, -1):
                plan(("s", dy, h, dx), piece(dy, h, dx), at(flip=True))

    def send(*names):
        for name in names:
            ag[name].start()

    def got(*names):
        for name in names:
            ag[name].wait_recv()

    def to_sibling(*pieces):
        send(*[("s", *p) for p in pieces])

    def block_ready(dy, h):
        got(*[("s", dy, h, dx) for dx in (0, 1, 2, -1)])

    send(("f", 1), ("f", -1), ("g", 1), ("g", -1))
    load_e.wait()
    load_c.wait()

    def phase_a():
        got(("f", 1), ("f", -1))
        send(("x1", 1, -1, 1), ("x1", -1, -1, 1), ("y3", 1), ("y3", -1))
        send(*[("k", s, k) for k in (1, 2, -1) for s in (1, -1)])
        to_sibling((-1, 1, 0), (1, 0, 0))

    def phase_c():
        got(("g", 1), ("g", -1))
        send(("x1", 1, 1, 1), ("x1", -1, 1, 1))
        to_sibling((-1, 0, 0), (1, 1, 0))
        got(("x1", -1, -1, 1), ("x1", 1, -1, 1))
        send(("x2", -1, -1, 1))
        to_sibling((-1, 1, 1), (-1, 1, -1))
        got(("x1", 1, 1, 1), ("x1", -1, 1, 1))
        send(("x2", 1, 1, 1))
        to_sibling((1, 1, -1), (1, 1, 1))
        got(("y3", 1), ("y3", -1))
        send(("x1", 1, 2, 0), ("x1", -1, 2, 1), ("x1", 1, 2, 1), ("x1", -1, 2, 0))
        to_sibling((2, 1, 0), (2, 0, 0))
        got(("x2", 1, 1, 1), ("x2", -1, -1, 1))
        to_sibling((1, 1, 2), (-1, 1, 2))
        block_ready(1, 1)

    def phase_f():
        for k in (1, 2):
            got(("k", 1, k), ("k", -1, k))
            to_sibling((1, 0, k), (-1, 0, k))
        block_ready(-1, 1)

    def phase_g():
        got(("x1", 1, 2, 0), ("x1", -1, 2, 1))
        send(("x2", 1, 2, 0), ("x2", -1, 2, 1))
        to_sibling((2, 0, -1), (2, 1, 1))
        got(("k", 1, -1), ("k", -1, -1))
        to_sibling((1, 0, -1), (-1, 0, -1))
        block_ready(1, 0)

    def phase_h():
        got(("x1", 1, 2, 1), ("x1", -1, 2, 0))
        to_sibling((2, 1, -1), (2, 0, 1))
        block_ready(-1, 0)

    def phase_i():
        got(("x2", 1, 2, 0), ("x2", -1, 2, 1))
        to_sibling((2, 0, 2), (2, 1, 2))
        block_ready(2, 0)

    def phase_j():
        block_ready(2, 1)

    sent = []

    def push(src, dst, peers, ssem, rsem, start=True):
        copies = []
        for k, peer in enumerate(peers):
            copy = pltpu.make_async_remote_copy(
                src_ref=src, dst_ref=dst.at[k], send_sem=ssem.at[k], recv_sem=rsem.at[k],
                device_id=peer, device_id_type=MESH,
            )
            copies.append(copy)
        sent.extend(copies)
        if start:
            begin(copies)
        return copies

    def begin(copies):
        for copy in copies:
            copy.start()

    def landed(copies):
        for copy in copies:
            copy.wait_recv()

    def push_1(n, half, start=True):
        return push(rl.at[n, half], ra.at[n, half], cent_peers, r1_s.at[n, half], r1_r.at[n, half], start)

    def push_2(n, half):
        return push(rl2.at[n, half], rb.at[n, half], y_peers, r2_s.at[n, half], r2_r.at[n, half])

    def summed(own, others, n):
        total = own
        for k in range(n):
            total = total + others[k]
        return total

    def log_summed(own, others, n):
        top = own
        for k in range(n):
            top = jnp.maximum(top, others[k])
        total = jnp.exp2(own - top)
        for k in range(n):
            total = total + jnp.exp2(others[k] - top)
        return top + jnp.log(total) * (1.0 / LN2)

    def place_of(p, odd):
        d = (p + 1) // 2
        if odd:
            return ((y - d + NY) % NY) * 2 + 1 - (1 - p % 2) * (p // 2)
        return ((y + d) % NY) * 2 + (p % 2) * (1 - p // 2)

    def step(new_buf, new, old_buf, old, old_max, half, row):
        top = jnp.max(old_max, axis=0, keepdims=True)
        total = jnp.zeros((8, BW), F32)
        new_max = []
        if new is not None:
            e = emb[pl.ds(new * 8, 8)].reshape(BW, D)
        for i in range(4):
            rows = slice(256 * i, 256 * i + 256)
            if new is not None and i % 2 == 0:
                lanes = slice(128 * i, 128 * i + 256)
                raw = lax.dot_general(
                    cen[...].reshape(C, D), e[lanes, :], (((1,), (1,)), ((), ())), preferred_element_type=F32
                )
                new_buf[:, lanes] = raw
                new_max.append(jnp.max(raw.reshape(C // 8, 8, 256), axis=0))
            value = jnp.exp2((old_buf[rows, :] - top) * EXP2_SCALE)
            kern[old, rows, :] = value
            total = total + jnp.sum(value.reshape(32, 8, BW), axis=0)
        if new is not None:
            new_max = jnp.concatenate(new_max, axis=1)
        scaled = top * EXP2_SCALE
        whole = scaled + jnp.log(jnp.sum(total, axis=0, keepdims=True)) * (1.0 / LN2)
        for j in range(2):
            lanes = slice(256 * j, 256 * j + 256)
            rl[0, half, pl.ds(row + j, 1), :] = whole[:, lanes]
            top_of[old // 4, pl.ds((old % 4) * 2 + j, 1), :] = scaled[:, lanes]
        return new_max

    first = push_1(0, 0, start=False)

    def two_steps(p, high):
        pl.when(p == 1)(phase_c)
        pl.when(p == 2)(phase_g)
        pl.when(p == 3)(phase_i)
        q = (p + 3) % 4
        high = step(buf0, place_of(p, False), buf1, place_of(q, True), high, q // 2, (q % 2) * 4 + 2)
        pl.when(p == 0)(phase_a)
        pl.when(p == 1)(phase_f)

        @pl.when(p == 2)
        def _():
            begin(first)
            phase_h()

        pl.when(p == 3)(phase_j)
        return step(buf1, place_of(p, True), buf0, place_of(p, False), high, p // 2, (p % 2) * 4)

    buf1[...] = jnp.zeros((C, BW), F32)
    high = lax.fori_loop(0, 4, two_steps, jnp.zeros((8, BW), F32))
    step(None, None, buf1, place_of(3, True), high, 1, 6)
    second = push_1(0, 1)
    for half, copies in ((0, first), (1, second)):
        landed(copies)
        merged = log_summed(rl[0, half], ra.at[0, half], 7)
        for j in range(8):
            place = place_of(2 * half + j // 4, j // 2 % 2 == 1)
            rl2[0, place // 4, pl.ds((place % 4) * 2 + j % 2, 1), :] = merged[j:j + 1, :]
    first, second = push_2(0, 0), push_2(0, 1)

    def start_weights(half):
        whole = log_summed(rl2[0, half], rb.at[0, half], 3)
        factor = jnp.exp2(top_of[half] - whole)
        fac[half] = factor
        rw[half] = factor * (1.0 / TOTAL)

    landed(first)
    start_weights(0)

    def weighted(b, rows, l):
        r = (b % 4) * 2 + l // 2
        w = rw[b // 4, r:r + 1, (l % 2) * 128:(l % 2) * 128 + 128]
        return kern[b, rows, l * 128:l * 128 + 128] * w

    def mass_half(half):
        def chunk(g, _):
            rows = pl.ds(pl.multiple_of(g * 64, 64), 64)
            acc = jnp.zeros((64, 128), F32) if half == 0 else part[rows, :]
            for b in range(4 * half, 4 * half + 4):
                for l in range(BW // 128):
                    acc = acc + weighted(b, rows, l)
            part[rows, :] = acc
            return 0

        lax.fori_loop(0, C // 64, chunk, 0)

    def row_half(n, half):
        def row_block(b, _):
            def chunk(g, acc):
                rows = pl.ds(pl.multiple_of(g * 128, 128), 128)
                s = scol[rows, :]
                value = kern[4 * half + b, rows, :] * jnp.concatenate([s] * (BW // 128), axis=1)
                return acc + jnp.sum(value.reshape(16, 8, BW), axis=0)

            acc = lax.fori_loop(0, C // 128, chunk, jnp.zeros((8, BW), F32))
            acc = jnp.sum(acc, axis=0, keepdims=True)
            for j in range(2):
                r = pl.ds(b * 2 + j, 1)
                rl[n, half, r, :] = acc[:, 256 * j:256 * j + 256] * fac[half, r, :]
            return 0

        lax.fori_loop(0, 4, row_block, 0)

    for n in range(2):
        mass_half(0)
        landed(second)
        if n == 0:
            start_weights(1)
        else:
            rw[1] = fac[1] / (TOTAL * summed(rl2[n, 1], rb.at[n, 1], 3))
        mass_half(1)
        for t in range(NZ):
            ml[n, t:t + 1, :] = jnp.sum(part[t * CH:(t + 1) * CH, :].T, axis=0, keepdims=True)
        landed(push(ml.at[n], mr.at[n], z_peers, m_s.at[n], m_r.at[n]))
        scale = 1.0 / (TOTAL * summed(ml[n], mr.at[n], 7))
        for t in range(NZ):
            scol[t * CH:(t + 1) * CH, :] = jnp.broadcast_to(scale[t:t + 1, :], (CH, CH)).T
        row_half(n + 1, 0)
        first = push_1(n + 1, 0)
        row_half(n + 1, 1)
        second = push_1(n + 1, 1)
        landed(first)
        rl2[n + 1, 0] = summed(rl[n + 1, 0], ra.at[n + 1, 0], 7)
        first = push_2(n + 1, 0)
        landed(second)
        rl2[n + 1, 1] = summed(rl[n + 1, 1], ra.at[n + 1, 1], 7)
        second = push_2(n + 1, 1)
        landed(first)
        rw[0] = fac[0] / (TOTAL * summed(rl2[n + 1, 0], rb.at[n + 1, 0], 3))

    def chunk_at(q):
        return (z + q + NZ) % NZ

    def weigh(w, i, b):
        ws = [rw[b // 4, pl.ds((b % 4) * 2 + j, 1), :] for j in range(2)]
        for j, q in enumerate(GROUPS[i]):
            rows = pl.ds(pl.multiple_of(chunk_at(q) * CH, CH), CH)
            place = slice((GROUP * i + j) * CH, (GROUP * i + j + 1) * CH)
            acc = part[place, :]
            for l in range(BW // 128):
                value = kern[b, rows, l * 128:l * 128 + 128] * ws[l // 2][:, (l % 2) * 128:(l % 2) * 128 + 128]
                acc = acc + value
                w[j * CH:(j + 1) * CH, l * 128:(l + 1) * 128] = value.astype(BF16)
            part[place, :] = acc

    def multiply(w, i, b):
        e = emb[pl.ds(b * 8, 8)].reshape(BW, D)
        num[GROUP * i:GROUP * i + GROUP] += jnp.dot(w[...], e, preferred_element_type=F32).reshape(GROUP, CH, D)

    def group(i, start, stop):
        def two(k, _):
            weigh(w1, i, 2 * k + 1)
            multiply(w0, i, 2 * k)
            weigh(w0, i, 2 * k + 2)
            multiply(w1, i, 2 * k + 1)
            return 0

        lax.fori_loop(start, stop, two, 0)

    def group_end(i):
        weigh(w1, i, 7)
        multiply(w0, i, 6)
        if i == 0:
            weigh(w0, i + 1, 0)
        multiply(w1, i, 7)

    rs = {}

    def hop(name, q, rows, before=None):
        sign = (1 if name[0] in ("RA", "RB") else -1)
        i = len(rs)
        value = num[POS[q], rows, :]
        if before is not None:
            rs[before].wait_recv()
            value = value + rcv[slot[before]].astype(F32)
        snd[i] = value.astype(BF16)
        slot[name] = i
        copy = pltpu.make_async_remote_copy(
            src_ref=snd.at[i], dst_ref=rcv.at[i], send_sem=rs_s.at[i], recv_sem=rs_r.at[i],
            device_id=at(dz=sign), device_id_type=MESH,
        )
        copy.start()
        rs[name] = copy

    slot = {}
    lo, hi = slice(0, 64), slice(64, 128)

    part[...] = jnp.zeros((C, 128), F32)
    weigh(w0, 0, 0)
    landed(second)
    rw[1] = fac[1] / (TOTAL * summed(rl2[2, 1], rb.at[2, 1], 3))
    num[...] = jnp.zeros((NZ, CH, D), F32)
    group(0, 0, 3)
    group_end(0)
    hop(("RB", 0), 4, lo)
    hop(("LB", 0), 4, hi)
    hop(("RA", 1), 3, hi)
    hop(("LA", 1), -3, lo)
    group(1, 0, 2)
    hop(("RB", 1), 3, lo, ("RB", 0))
    hop(("LB", 1), -3, hi, ("LB", 0))
    group(1, 2, 3)
    group_end(1)
    for j, q in enumerate(q for g in GROUPS for q in g):
        ml[2, pl.ds(chunk_at(q), 1), :] = jnp.sum(part[j * CH:(j + 1) * CH, :].T, axis=0, keepdims=True)
    last = push(ml.at[2], mr.at[2], z_peers, m_s.at[2], m_r.at[2])
    hop(("RA", 2), 2, hi, ("RA", 1))
    hop(("LA", 2), -2, lo, ("LA", 1))
    hop(("RB", 2), 2, lo, ("RB", 1))
    hop(("LB", 2), -2, hi, ("LB", 1))
    hop(("RA", 3), 1, hi, ("RA", 2))
    hop(("LA", 3), -1, lo, ("LA", 2))
    hop(("RB", 3), 1, lo, ("RB", 2))
    hop(("LB", 3), -1, hi, ("LB", 2))

    for copy in last:
        copy.wait_recv()
    mass = ml[2, pl.ds(z, 1), :]
    for k in range(7):
        mass = mass + mr[2, k, pl.ds(z, 1), :]
    column = jnp.broadcast_to(mass, (CH, CH)).T
    column = jnp.concatenate([column] * (D // CH), axis=1)
    for rows, one, two in ((hi, ("RA", 3), ("LB", 3)), (lo, ("LA", 3), ("RB", 3))):
        rs[one].wait_recv()
        rs[two].wait_recv()
        total = num[POS[0], rows, :] + rcv[slot[one]].astype(F32) + rcv[slot[two]].astype(F32)
        out_ref[rows, :] = (total / column[rows, :]).astype(BF16)

    for copy in list(ag.values()) + sent + list(rs.values()):
        copy.wait_send()


def local(embeddings, centroids):
    e = embeddings.reshape(16, PIECE, D)
    k = centroids.reshape(NZ, NY, CH, D)
    dma = pltpu.SemaphoreType.DMA
    v = pltpu.VMEM
    out = pl.pallas_call(
        body,
        out_shape=jax.ShapeDtypeStruct((CH, D), BF16),
        in_specs=[pl.BlockSpec(memory_space=pl.ANY)] * 2,
        out_specs=pl.BlockSpec(memory_space=pltpu.VMEM),
        scratch_shapes=[
            v((64, PIECE, D), BF16), v((NZ, CH, D), BF16), v((NB, C, BW), F32), v((C, BW), F32), v((C, BW), F32),
            v((2, 8, 256), F32), v((3, 2, 8, 256), F32), v((3, 2, 8, 256), F32),
            v((3, 2, 7, 8, 256), F32), v((3, 2, 3, 8, 256), F32),
            v((2, 8, 256), F32), v((2, 8, 256), F32), v((C, 128), F32), v((C, 128), F32),
            v((3, NZ, CH), F32), v((3, 7, NZ, CH), F32),
            v((GROUP * CH, BW), BF16), v((GROUP * CH, BW), BF16), v((NZ, CH, D), F32),
            v((14, 64, D), BF16), v((14, 64, D), BF16),
            dma((2,)), dma((48,)), dma((48,)), dma((3, 2, 7)), dma((3, 2, 7)), dma((3, 2, 3)), dma((3, 2, 3)),
            dma((3, 7)), dma((3, 7)), dma((14,)), dma((14,)),
        ],
        compiler_params=pltpu.CompilerParams(
            collective_id=0, has_side_effects=True, vmem_limit_bytes=60 * 1024 * 1024
        ),
        cost_estimate=pl.CostEstimate(
            flops=4 * C * NB * BW * D, bytes_accessed=8 * 1024 * 1024, transcendentals=C * NB * BW
        ),
    )(e, k)
    return out[None]


def solution(mesh):
    return jax.shard_map(
        local,
        mesh=mesh,
        in_specs=(P("docs", None), P("cent", None)),
        out_specs=P("cent", "docs", None),
        check_vma=False,
    )
```

```python
import jax
import jax.numpy as jnp
import numpy as np
from jax import lax
from jax.experimental import pallas as pl
from jax.experimental.pallas import tpu as pltpu
from jax.sharding import PartitionSpec as P

MESH = pl.DeviceIdType.MESH
F32 = jnp.float32
BF16 = jnp.bfloat16

NX, NY, NZ = 4, 4, 8
D = 768
PIECE = 64
NB, BW = 8, 512
CH = 128
C = NZ * CH
TOTAL = 32768.0
EXP2_SCALE = 10.0 * float(np.log2(np.e))

GROUPS = ((4, 3, -3, 2), (-2, 1, -1, 0))
GROUP = len(GROUPS[0])
POS = {q: i for i, q in enumerate(q for group in GROUPS for q in group)}
LN2 = float(np.log(2.0))


def body(
    emb_hbm, cen_hbm, out_ref,
    emb, cen, kern, buf0, buf1,
    top_of, rl, rl2, ra, rb, fac, rw, part, scol, col, ml, mr, w0, w1, num, snd, rcv,
    ld_sem, ag_s, ag_r, r1_s, r1_r, r2_s, r2_r, m_s, m_r, rs_s, rs_r,
):
    docs = lax.axis_index("docs")
    cent = lax.axis_index("cent")
    z, y = docs // NY, docs % NY
    x, c = cent // 2, cent % 2

    def at(dz=0, dy=0, dx=0, flip=False):
        zz = (z + dz + NZ) % NZ
        yy = (y + dy + NY) % NY
        xx = (x + dx + NX) % NX
        return (zz * NY + yy, xx * 2 + ((1 - c) if flip else c))

    load_e = pltpu.make_async_copy(emb_hbm, emb.at[pl.ds(y * 16, 16)], ld_sem.at[0])
    load_c = pltpu.make_async_copy(cen_hbm.at[:, y], cen, ld_sem.at[1])
    load_e.start()
    load_c.start()

    cent_peers = [(docs, (cent + k) % 8) for k in range(1, 8)]
    y_peers = [at(dy=k) for k in range(1, NY)]
    z_peers = [at(dz=k) for k in range(1, NZ)]
    barrier = pltpu.get_barrier_semaphore()
    for peer in cent_peers + y_peers + z_peers:
        pl.semaphore_signal(barrier, inc=1, device_id=peer, device_id_type=MESH)
    pl.semaphore_wait(barrier, len(cent_peers) + len(y_peers) + len(z_peers))

    def piece(dy, h, dx):
        return ((y + dy + NY) % NY) * 16 + h * 8 + ((x + dx + NX) % NX) * 2 + c

    ag = {}

    def plan(name, where, target, src=None):
        i = len(ag)
        ag[name] = pltpu.make_async_remote_copy(
            src_ref=emb.at[where] if src is None else src, dst_ref=emb.at[where],
            send_sem=ag_s.at[i], recv_sem=ag_r.at[i], device_id=target, device_id_type=MESH,
        )

    def plan_own(name, h, dx, s):
        plan(name, piece(0, h, dx), at(dy=s), emb_hbm.at[h * 8 + ((x + dx + NX) % NX) * 2 + c])

    plan_own(("f", 1), 1, 0, 1)
    plan_own(("f", -1), 0, 0, -1)
    plan_own(("g", 1), 0, 0, 1)
    plan_own(("g", -1), 1, 0, -1)
    plan(("y3", 1), piece(-1, 1, 0), at(dy=1))
    plan(("y3", -1), piece(1, 0, 0), at(dy=-1))
    for k in (1, 2, -1):
        for s in (1, -1):
            plan_own(("k", s, k), 0, k, s)
    for dy, h in ((-1, 1), (1, 1), (2, 0), (2, 1)):
        for s in (1, -1):
            plan(("x1", s, dy, h), piece(dy, h, 0), at(dx=s))
    for s, dy, h in ((-1, -1, 1), (1, 1, 1), (1, 2, 0), (-1, 2, 1)):
        plan(("x2", s, dy, h), piece(dy, h, -s), at(dx=s))
    for dy in (-1, 1, 2):
        for h in (0, 1):
            for dx in (0, 1, 2, -1):
                plan(("s", dy, h, dx), piece(dy, h, dx), at(flip=True))

    def send(*names):
        for name in names:
            ag[name].start()

    def got(*names):
        for name in names:
            ag[name].wait_recv()

    def to_sibling(*pieces):
        send(*[("s", *p) for p in pieces])

    def block_ready(dy, h):
        got(*[("s", dy, h, dx) for dx in (0, 1, 2, -1)])

    send(("f", 1), ("f", -1), ("g", 1), ("g", -1))
    load_e.wait()
    load_c.wait()

    def phase_a():
        got(("f", 1), ("f", -1))
        send(("x1", 1, -1, 1), ("x1", -1, -1, 1), ("y3", 1), ("y3", -1))
        send(*[("k", s, k) for k in (1, 2, -1) for s in (1, -1)])
        to_sibling((-1, 1, 0), (1, 0, 0))

    def phase_c():
        got(("g", 1), ("g", -1))
        send(("x1", 1, 1, 1), ("x1", -1, 1, 1))
        to_sibling((-1, 0, 0), (1, 1, 0))
        got(("x1", -1, -1, 1), ("x1", 1, -1, 1))
        send(("x2", -1, -1, 1))
        to_sibling((-1, 1, 1), (-1, 1, -1))
        got(("x1", 1, 1, 1), ("x1", -1, 1, 1))
        send(("x2", 1, 1, 1))
        to_sibling((1, 1, -1), (1, 1, 1))
        got(("y3", 1), ("y3", -1))
        send(("x1", 1, 2, 0), ("x1", -1, 2, 1), ("x1", 1, 2, 1), ("x1", -1, 2, 0))
        to_sibling((2, 1, 0), (2, 0, 0))
        got(("x2", 1, 1, 1), ("x2", -1, -1, 1))
        to_sibling((1, 1, 2), (-1, 1, 2))
        block_ready(1, 1)

    def phase_f():
        for k in (1, 2):
            got(("k", 1, k), ("k", -1, k))
            to_sibling((1, 0, k), (-1, 0, k))
        block_ready(-1, 1)

    def phase_g():
        got(("x1", 1, 2, 0), ("x1", -1, 2, 1))
        send(("x2", 1, 2, 0), ("x2", -1, 2, 1))
        to_sibling((2, 0, -1), (2, 1, 1))
        got(("k", 1, -1), ("k", -1, -1))
        to_sibling((1, 0, -1), (-1, 0, -1))
        block_ready(1, 0)

    def phase_h():
        got(("x1", 1, 2, 1), ("x1", -1, 2, 0))
        to_sibling((2, 1, -1), (2, 0, 1))
        block_ready(-1, 0)

    def phase_i():
        got(("x2", 1, 2, 0), ("x2", -1, 2, 1))
        to_sibling((2, 0, 2), (2, 1, 2))
        block_ready(2, 0)

    def phase_j():
        block_ready(2, 1)

    sent = []

    def push(src, dst, peers, ssem, rsem, start=True):
        copies = []
        for k, peer in enumerate(peers):
            copy = pltpu.make_async_remote_copy(
                src_ref=src, dst_ref=dst.at[k], send_sem=ssem.at[k], recv_sem=rsem.at[k],
                device_id=peer, device_id_type=MESH,
            )
            copies.append(copy)
        sent.extend(copies)
        if start:
            begin(copies)
        return copies

    def begin(copies):
        for copy in copies:
            copy.start()

    def landed(copies):
        for copy in copies:
            copy.wait_recv()

    def push_1(n, half, start=True):
        return push(rl.at[n, half], ra.at[n, half], cent_peers, r1_s.at[n, half], r1_r.at[n, half], start)

    def push_2(n, half):
        return push(rl2.at[n, half], rb.at[n, half], y_peers, r2_s.at[n, half], r2_r.at[n, half])

    def summed(own, others, n):
        total = own
        for k in range(n):
            total = total + others[k]
        return total

    def log_summed(own, others, n):
        top = own
        for k in range(n):
            top = jnp.maximum(top, others[k])
        total = jnp.exp2(own - top)
        for k in range(n):
            total = total + jnp.exp2(others[k] - top)
        return top + jnp.log(total) * (1.0 / LN2)

    def place_of(p, odd):
        d = (p + 1) // 2
        if odd:
            return ((y - d + NY) % NY) * 2 + 1 - (1 - p % 2) * (p // 2)
        return ((y + d) % NY) * 2 + (p % 2) * (1 - p // 2)

    def step(new_buf, new, old_buf, old, old_max, half, row):
        top = jnp.max(old_max, axis=0, keepdims=True)
        total = jnp.zeros((8, BW), F32)
        new_max = []
        if new is not None:
            e = emb[pl.ds(new * 8, 8)].reshape(BW, D)
        for i in range(4):
            if new is not None and i % 2 == 0:
                lanes = slice(128 * i, 128 * i + 256)
                raw = lax.dot_general(
                    cen[...].reshape(C, D), e[lanes, :], (((1,), (1,)), ((), ())), preferred_element_type=F32
                )
                new_buf[:, lanes] = raw
                new_max.append(jnp.max(raw.reshape(C // 8, 8, 256), axis=0))
            for k in range(4):
                rows = slice(256 * i + 64 * k, 256 * i + 64 * k + 64)
                value = jnp.exp2((old_buf[rows, :] - top) * EXP2_SCALE)
                kern[old, rows, :] = value
                total = total + jnp.sum(value.reshape(8, 8, BW), axis=0)
        if new is not None:
            new_max = jnp.concatenate(new_max, axis=1)
        scaled = top * EXP2_SCALE
        whole = scaled + jnp.log(jnp.sum(total, axis=0, keepdims=True)) * (1.0 / LN2)
        for j in range(2):
            lanes = slice(256 * j, 256 * j + 256)
            rl[0, half, pl.ds(row + j, 1), :] = whole[:, lanes]
            top_of[old // 4, pl.ds((old % 4) * 2 + j, 1), :] = scaled[:, lanes]
        return new_max

    first = push_1(0, 0, start=False)

    def two_steps(p, high):
        pl.when(p == 1)(phase_c)
        pl.when(p == 2)(phase_g)
        pl.when(p == 3)(phase_i)
        q = (p + 3) % 4
        high = step(buf0, place_of(p, False), buf1, place_of(q, True), high, q // 2, (q % 2) * 4 + 2)
        pl.when(p == 0)(phase_a)
        pl.when(p == 1)(phase_f)

        @pl.when(p == 2)
        def _():
            begin(first)
            phase_h()

        pl.when(p == 3)(phase_j)
        return step(buf1, place_of(p, True), buf0, place_of(p, False), high, p // 2, (p % 2) * 4)

    buf1[...] = jnp.zeros((C, BW), F32)
    high = lax.fori_loop(0, 4, two_steps, jnp.zeros((8, BW), F32))
    step(None, None, buf1, place_of(3, True), high, 1, 6)
    second = push_1(0, 1)
    for half, copies in ((0, first), (1, second)):
        landed(copies)
        merged = log_summed(rl[0, half], ra.at[0, half], 7)
        for j in range(8):
            place = place_of(2 * half + j // 4, j // 2 % 2 == 1)
            rl2[0, place // 4, pl.ds((place % 4) * 2 + j % 2, 1), :] = merged[j:j + 1, :]
    first, second = push_2(0, 0), push_2(0, 1)

    def start_weights(half):
        whole = log_summed(rl2[0, half], rb.at[0, half], 3)
        factor = jnp.exp2(top_of[half] - whole)
        fac[half] = factor
        rw[half] = factor * (1.0 / TOTAL)

    landed(first)
    start_weights(0)

    lane = lax.broadcasted_iota(jnp.int32, (8, 128), 1)

    def mass_half(half):
        def chunk(t, _):
            def tile(i):
                return pl.ds(pl.multiple_of(t * CH + 8 * i, 8), 8)

            acc = [None if half == 0 else part[tile(i), :] for i in range(16)]
            for b in range(4 * half, 4 * half + 4):
                for l in range(4):
                    r = (b % 4) * 2 + l // 2
                    w = jnp.broadcast_to(rw[half, r:r + 1, (l % 2) * 128:(l % 2) * 128 + 128], (8, 128))
                    for i in range(16):
                        value = kern[b, tile(i), l * 128:l * 128 + 128] * w
                        acc[i] = value if acc[i] is None else acc[i] + value
            for i in range(16):
                if half == 0:
                    part[tile(i), :] = acc[i]
                else:
                    total = jnp.sum(acc[i], axis=1, keepdims=True)
                    rows = slice(8 * i, 8 * i + 8)
                    col[rows, :] = jnp.where(lane == t, total, col[rows, :])
            return 0

        lax.fori_loop(0, NZ, chunk, 0)

    def row_half(n, half):
        def chunk(t, acc):
            acc = list(acc)
            for i in range(16):
                tile = pl.ds(pl.multiple_of(t * CH + 8 * i, 8), 8)
                s = scol[tile, :]
                for b in range(4):
                    for l in range(4):
                        acc[4 * b + l] += kern[4 * half + b, tile, l * 128:l * 128 + 128] * s
            return tuple(acc)

        acc = lax.fori_loop(0, NZ, chunk, tuple(jnp.zeros((8, 128), F32) for _ in range(16)))
        for b in range(4):
            for l in range(4):
                r, lanes = b * 2 + l // 2, slice((l % 2) * 128, (l % 2) * 128 + 128)
                total = jnp.sum(acc[4 * b + l], axis=0, keepdims=True)
                rl[n, half, r:r + 1, lanes] = total * fac[half, r:r + 1, lanes]

    col[...] = jnp.zeros((CH, CH), F32)
    for n in range(2):
        mass_half(0)
        landed(second)
        if n == 0:
            start_weights(1)
        else:
            rw[1] = fac[1] / (TOTAL * summed(rl2[n, 1], rb.at[n, 1], 3))
        mass_half(1)
        ml[n] = col[...].T[0:NZ, :]
        landed(push(ml.at[n], mr.at[n], z_peers, m_s.at[n], m_r.at[n]))
        scale = 1.0 / (TOTAL * summed(ml[n], mr.at[n], 7))
        columns = jnp.concatenate([scale, jnp.zeros((CH - NZ, CH), F32)], axis=0).T
        for t in range(NZ):
            scol[t * CH:(t + 1) * CH, :] = jnp.broadcast_to(columns[:, t:t + 1], (CH, CH))
        row_half(n + 1, 0)
        first = push_1(n + 1, 0)
        row_half(n + 1, 1)
        second = push_1(n + 1, 1)
        landed(first)
        rl2[n + 1, 0] = summed(rl[n + 1, 0], ra.at[n + 1, 0], 7)
        first = push_2(n + 1, 0)
        landed(second)
        rl2[n + 1, 1] = summed(rl[n + 1, 1], ra.at[n + 1, 1], 7)
        second = push_2(n + 1, 1)
        landed(first)
        rw[0] = fac[0] / (TOTAL * summed(rl2[n + 1, 0], rb.at[n + 1, 0], 3))

    def chunk_at(q):
        return (z + q + NZ) % NZ

    def weigh(w, i, b):
        ws = [rw[b // 4, pl.ds((b % 4) * 2 + j, 1), :] for j in range(2)]
        for j, q in enumerate(GROUPS[i]):
            rows = pl.ds(pl.multiple_of(chunk_at(q) * CH, CH), CH)
            place = slice((GROUP * i + j) * CH, (GROUP * i + j + 1) * CH)
            acc = part[place, :]
            for l in range(BW // 128):
                value = kern[b, rows, l * 128:l * 128 + 128] * ws[l // 2][:, (l % 2) * 128:(l % 2) * 128 + 128]
                acc = acc + value
                w[j * CH:(j + 1) * CH, l * 128:(l + 1) * 128] = value.astype(BF16)
            part[place, :] = acc

    def multiply(w, i, b):
        e = emb[pl.ds(b * 8, 8)].reshape(BW, D)
        num[GROUP * i:GROUP * i + GROUP] += jnp.dot(w[...], e, preferred_element_type=F32).reshape(GROUP, CH, D)

    def group(i, start, stop):
        def two(k, _):
            weigh(w1, i, 2 * k + 1)
            multiply(w0, i, 2 * k)
            weigh(w0, i, 2 * k + 2)
            multiply(w1, i, 2 * k + 1)
            return 0

        lax.fori_loop(start, stop, two, 0)

    def group_end(i):
        weigh(w1, i, 7)
        multiply(w0, i, 6)
        if i == 0:
            weigh(w0, i + 1, 0)
        multiply(w1, i, 7)

    rs = {}

    def hop(name, q, rows, before=None):
        sign = (1 if name[0] in ("RA", "RB") else -1)
        i = len(rs)
        value = num[POS[q], rows, :]
        if before is not None:
            rs[before].wait_recv()
            value = value + rcv[slot[before]].astype(F32)
        snd[i] = value.astype(BF16)
        slot[name] = i
        copy = pltpu.make_async_remote_copy(
            src_ref=snd.at[i], dst_ref=rcv.at[i], send_sem=rs_s.at[i], recv_sem=rs_r.at[i],
            device_id=at(dz=sign), device_id_type=MESH,
        )
        copy.start()
        rs[name] = copy

    slot = {}
    lo, hi = slice(0, 64), slice(64, 128)

    part[...] = jnp.zeros((C, 128), F32)
    weigh(w0, 0, 0)
    landed(second)
    rw[1] = fac[1] / (TOTAL * summed(rl2[2, 1], rb.at[2, 1], 3))
    num[...] = jnp.zeros((NZ, CH, D), F32)
    group(0, 0, 3)
    group_end(0)
    hop(("RB", 0), 4, lo)
    hop(("LB", 0), 4, hi)
    hop(("RA", 1), 3, hi)
    hop(("LA", 1), -3, lo)
    group(1, 0, 2)
    hop(("RB", 1), 3, lo, ("RB", 0))
    hop(("LB", 1), -3, hi, ("LB", 0))
    group(1, 2, 3)
    group_end(1)
    for j, q in enumerate(q for g in GROUPS for q in g):
        for i in range(16):
            rows = slice(8 * i, 8 * i + 8)
            total = jnp.sum(part[j * CH + 8 * i:j * CH + 8 * i + 8, :], axis=1, keepdims=True)
            col[rows, :] = jnp.where(lane == chunk_at(q), total, col[rows, :])
    ml[2] = col[...].T[0:NZ, :]
    last = push(ml.at[2], mr.at[2], z_peers, m_s.at[2], m_r.at[2])
    hop(("RA", 2), 2, hi, ("RA", 1))
    hop(("LA", 2), -2, lo, ("LA", 1))
    hop(("RB", 2), 2, lo, ("RB", 1))
    hop(("LB", 2), -2, hi, ("LB", 1))
    hop(("RA", 3), 1, hi, ("RA", 2))
    hop(("LA", 3), -1, lo, ("LA", 2))
    hop(("RB", 3), 1, lo, ("RB", 2))
    hop(("LB", 3), -1, hi, ("LB", 2))

    for copy in last:
        copy.wait_recv()
    mass = ml[2, pl.ds(z, 1), :]
    for k in range(7):
        mass = mass + mr[2, k, pl.ds(z, 1), :]
    column = jnp.broadcast_to(mass, (CH, CH)).T
    column = jnp.concatenate([column] * (D // CH), axis=1)
    for rows, one, two in ((hi, ("RA", 3), ("LB", 3)), (lo, ("LA", 3), ("RB", 3))):
        rs[one].wait_recv()
        rs[two].wait_recv()
        total = num[POS[0], rows, :] + rcv[slot[one]].astype(F32) + rcv[slot[two]].astype(F32)
        out_ref[rows, :] = (total / column[rows, :]).astype(BF16)

    for copy in list(ag.values()) + sent + list(rs.values()):
        copy.wait_send()


def local(embeddings, centroids):
    e = embeddings.reshape(16, PIECE, D)
    k = centroids.reshape(NZ, NY, CH, D)
    dma = pltpu.SemaphoreType.DMA
    v = pltpu.VMEM
    out = pl.pallas_call(
        body,
        out_shape=jax.ShapeDtypeStruct((CH, D), BF16),
        in_specs=[pl.BlockSpec(memory_space=pl.ANY)] * 2,
        out_specs=pl.BlockSpec(memory_space=pltpu.VMEM),
        scratch_shapes=[
            v((64, PIECE, D), BF16), v((NZ, CH, D), BF16), v((NB, C, BW), F32), v((C, BW), F32), v((C, BW), F32),
            v((2, 8, 256), F32), v((3, 2, 8, 256), F32), v((3, 2, 8, 256), F32),
            v((3, 2, 7, 8, 256), F32), v((3, 2, 3, 8, 256), F32),
            v((2, 8, 256), F32), v((2, 8, 256), F32), v((C, 128), F32), v((C, 128), F32), v((CH, CH), F32),
            v((3, NZ, CH), F32), v((3, 7, NZ, CH), F32),
            v((GROUP * CH, BW), BF16), v((GROUP * CH, BW), BF16), v((NZ, CH, D), F32),
            v((14, 64, D), BF16), v((14, 64, D), BF16),
            dma((2,)), dma((48,)), dma((48,)), dma((3, 2, 7)), dma((3, 2, 7)), dma((3, 2, 3)), dma((3, 2, 3)),
            dma((3, 7)), dma((3, 7)), dma((14,)), dma((14,)),
        ],
        compiler_params=pltpu.CompilerParams(
            collective_id=0, has_side_effects=True, vmem_limit_bytes=60 * 1024 * 1024
        ),
        cost_estimate=pl.CostEstimate(
            flops=4 * C * NB * BW * D, bytes_accessed=8 * 1024 * 1024, transcendentals=C * NB * BW
        ),
    )(e, k)
    return out[None]


def solution(mesh):
    return jax.shard_map(
        local,
        mesh=mesh,
        in_specs=(P("docs", None), P("cent", None)),
        out_specs=P("cent", "docs", None),
        check_vma=False,
    )
```

```python
import jax
import jax.numpy as jnp
import numpy as np
from jax import lax
from jax.experimental import pallas as pl
from jax.experimental.pallas import tpu as pltpu
from jax.sharding import PartitionSpec as P

MESH = pl.DeviceIdType.MESH
F32 = jnp.float32
BF16 = jnp.bfloat16

NX, NY, NZ = 4, 4, 8
D = 768
PIECE = 64
NB, BW = 8, 512
CH = 128
C = NZ * CH
TOTAL = 32768.0
EXP2_SCALE = 10.0 * float(np.log2(np.e))

GROUPS = ((4, 3), (-3, 2), (-2, 1), (-1, 0))
GROUP = len(GROUPS[0])
POS = {q: i for i, q in enumerate(q for group in GROUPS for q in group)}
LN2 = float(np.log(2.0))


def body(
    emb_hbm, cen_hbm, out_ref,
    emb, cen, kern, buf0, buf1,
    top_of, rl, rl2, ra, rb, fac, rw, part, scol, col, ml, mr, w0, w1, num, snd, rcv,
    ld_sem, ag_s, ag_r, r1_s, r1_r, r2_s, r2_r, m_s, m_r, rs_s, rs_r,
):
    docs = lax.axis_index("docs")
    cent = lax.axis_index("cent")
    z, y = docs // NY, docs % NY
    x, c = cent // 2, cent % 2

    def at(dz=0, dy=0, dx=0, flip=False):
        zz = (z + dz + NZ) % NZ
        yy = (y + dy + NY) % NY
        xx = (x + dx + NX) % NX
        return (zz * NY + yy, xx * 2 + ((1 - c) if flip else c))

    load_e = pltpu.make_async_copy(emb_hbm, emb.at[pl.ds(y * 16, 16)], ld_sem.at[0])
    load_c = pltpu.make_async_copy(cen_hbm.at[:, y], cen, ld_sem.at[1])
    load_e.start()
    load_c.start()

    cent_peers = [(docs, (cent + k) % 8) for k in range(1, 8)]
    y_peers = [at(dy=k) for k in range(1, NY)]
    z_peers = [at(dz=k) for k in range(1, NZ)]
    barrier = pltpu.get_barrier_semaphore()
    for peer in cent_peers + y_peers + z_peers:
        pl.semaphore_signal(barrier, inc=1, device_id=peer, device_id_type=MESH)
    pl.semaphore_wait(barrier, len(cent_peers) + len(y_peers) + len(z_peers))

    def piece(dy, h, dx):
        return ((y + dy + NY) % NY) * 16 + h * 8 + ((x + dx + NX) % NX) * 2 + c

    ag = {}

    def plan(name, where, target, src=None):
        i = len(ag)
        ag[name] = pltpu.make_async_remote_copy(
            src_ref=emb.at[where] if src is None else src, dst_ref=emb.at[where],
            send_sem=ag_s.at[i], recv_sem=ag_r.at[i], device_id=target, device_id_type=MESH,
        )

    def plan_own(name, h, dx, s):
        plan(name, piece(0, h, dx), at(dy=s), emb_hbm.at[h * 8 + ((x + dx + NX) % NX) * 2 + c])

    plan_own(("f", 1), 1, 0, 1)
    plan_own(("f", -1), 0, 0, -1)
    plan_own(("g", 1), 0, 0, 1)
    plan_own(("g", -1), 1, 0, -1)
    plan(("y3", 1), piece(-1, 1, 0), at(dy=1))
    plan(("y3", -1), piece(1, 0, 0), at(dy=-1))
    for k in (1, 2, -1):
        for s in (1, -1):
            plan_own(("k", s, k), 0, k, s)
    for dy, h in ((-1, 1), (1, 1), (2, 0), (2, 1)):
        for s in (1, -1):
            plan(("x1", s, dy, h), piece(dy, h, 0), at(dx=s))
    for s, dy, h in ((-1, -1, 1), (1, 1, 1), (1, 2, 0), (-1, 2, 1)):
        plan(("x2", s, dy, h), piece(dy, h, -s), at(dx=s))
    for dy in (-1, 1, 2):
        for h in (0, 1):
            for dx in (0, 1, 2, -1):
                plan(("s", dy, h, dx), piece(dy, h, dx), at(flip=True))

    def send(*names):
        for name in names:
            ag[name].start()

    def got(*names):
        for name in names:
            ag[name].wait_recv()

    def to_sibling(*pieces):
        send(*[("s", *p) for p in pieces])

    def block_ready(dy, h):
        got(*[("s", dy, h, dx) for dx in (0, 1, 2, -1)])

    send(("f", 1), ("f", -1), ("g", 1), ("g", -1))
    load_e.wait()
    load_c.wait()

    def phase_a():
        got(("f", 1), ("f", -1))
        send(("x1", 1, -1, 1), ("x1", -1, -1, 1), ("y3", 1), ("y3", -1))
        send(*[("k", s, k) for k in (1, 2, -1) for s in (1, -1)])
        to_sibling((-1, 1, 0), (1, 0, 0))

    def phase_c():
        got(("g", 1), ("g", -1))
        send(("x1", 1, 1, 1), ("x1", -1, 1, 1))
        to_sibling((-1, 0, 0), (1, 1, 0))
        got(("x1", -1, -1, 1), ("x1", 1, -1, 1))
        send(("x2", -1, -1, 1))
        to_sibling((-1, 1, 1), (-1, 1, -1))
        got(("x1", 1, 1, 1), ("x1", -1, 1, 1))
        send(("x2", 1, 1, 1))
        to_sibling((1, 1, -1), (1, 1, 1))
        got(("y3", 1), ("y3", -1))
        send(("x1", 1, 2, 0), ("x1", -1, 2, 1), ("x1", 1, 2, 1), ("x1", -1, 2, 0))
        to_sibling((2, 1, 0), (2, 0, 0))
        got(("x2", 1, 1, 1), ("x2", -1, -1, 1))
        to_sibling((1, 1, 2), (-1, 1, 2))
        block_ready(1, 1)

    def phase_f():
        for k in (1, 2):
            got(("k", 1, k), ("k", -1, k))
            to_sibling((1, 0, k), (-1, 0, k))
        block_ready(-1, 1)

    def phase_g():
        got(("x1", 1, 2, 0), ("x1", -1, 2, 1))
        send(("x2", 1, 2, 0), ("x2", -1, 2, 1))
        to_sibling((2, 0, -1), (2, 1, 1))
        got(("k", 1, -1), ("k", -1, -1))
        to_sibling((1, 0, -1), (-1, 0, -1))
        block_ready(1, 0)

    def phase_h():
        got(("x1", 1, 2, 1), ("x1", -1, 2, 0))
        to_sibling((2, 1, -1), (2, 0, 1))
        block_ready(-1, 0)

    def phase_i():
        got(("x2", 1, 2, 0), ("x2", -1, 2, 1))
        to_sibling((2, 0, 2), (2, 1, 2))
        block_ready(2, 0)

    def phase_j():
        block_ready(2, 1)

    sent = []

    def push(src, dst, peers, ssem, rsem, start=True):
        copies = []
        for k, peer in enumerate(peers):
            copy = pltpu.make_async_remote_copy(
                src_ref=src, dst_ref=dst.at[k], send_sem=ssem.at[k], recv_sem=rsem.at[k],
                device_id=peer, device_id_type=MESH,
            )
            copies.append(copy)
        sent.extend(copies)
        if start:
            begin(copies)
        return copies

    def begin(copies):
        for copy in copies:
            copy.start()

    def landed(copies):
        for copy in copies:
            copy.wait_recv()

    def drain(copies):
        for copy in copies:
            copy.wait_send()

    def push_1(n, half, start=True):
        return push(rl.at[n, half], ra.at[n, half], cent_peers, r1_s.at[n, half], r1_r.at[n, half], start)

    def push_2(n, half):
        return push(rl2.at[n, half], rb.at[n, half], y_peers, r2_s.at[n, half], r2_r.at[n, half])

    def summed(own, others, n):
        total = own
        for k in range(n):
            total = total + others[k]
        return total

    def log_summed(own, others, n):
        top = own
        for k in range(n):
            top = jnp.maximum(top, others[k])
        total = jnp.exp2(own - top)
        for k in range(n):
            total = total + jnp.exp2(others[k] - top)
        return top + jnp.log(total) * (1.0 / LN2)

    def place_of(p, odd):
        d = (p + 1) // 2
        if odd:
            return ((y - d + NY) % NY) * 2 + 1 - (1 - p % 2) * (p // 2)
        return ((y + d) % NY) * 2 + (p % 2) * (1 - p // 2)

    def step(new_buf, new, old_buf, old, old_max, half, row):
        top = jnp.max(old_max, axis=0, keepdims=True)
        total = jnp.zeros((8, BW), F32)
        new_max = []
        if new is not None:
            e = emb[pl.ds(new * 8, 8)].reshape(BW, D)
        for i in range(4):
            if new is not None and i % 2 == 0:
                lanes = slice(128 * i, 128 * i + 256)
                raw = lax.dot_general(
                    cen[...].reshape(C, D), e[lanes, :], (((1,), (1,)), ((), ())), preferred_element_type=F32
                )
                new_buf[:, lanes] = raw
                new_max.append(jnp.max(raw.reshape(C // 8, 8, 256), axis=0))
            for k in range(4):
                rows = slice(256 * i + 64 * k, 256 * i + 64 * k + 64)
                value = jnp.exp2((old_buf[rows, :] - top) * EXP2_SCALE)
                kern[old, rows, :] = value
                total = total + jnp.sum(value.reshape(8, 8, BW), axis=0)
        if new is not None:
            new_max = jnp.concatenate(new_max, axis=1)
        scaled = top * EXP2_SCALE
        whole = scaled + jnp.log(jnp.sum(total, axis=0, keepdims=True)) * (1.0 / LN2)
        for j in range(2):
            lanes = slice(256 * j, 256 * j + 256)
            rl[0, half, pl.ds(row + j, 1), :] = whole[:, lanes]
            top_of[old // 4, pl.ds((old % 4) * 2 + j, 1), :] = scaled[:, lanes]
        return new_max

    first = push_1(0, 0, start=False)

    def two_steps(p, high):
        pl.when(p == 1)(phase_c)
        pl.when(p == 2)(phase_g)
        pl.when(p == 3)(phase_i)
        q = (p + 3) % 4
        high = step(buf0, place_of(p, False), buf1, place_of(q, True), high, q // 2, (q % 2) * 4 + 2)
        pl.when(p == 0)(phase_a)
        pl.when(p == 1)(phase_f)

        @pl.when(p == 2)
        def _():
            begin(first)
            phase_h()

        pl.when(p == 3)(phase_j)
        return step(buf1, place_of(p, True), buf0, place_of(p, False), high, p // 2, (p % 2) * 4)

    buf1[...] = jnp.zeros((C, BW), F32)
    high = lax.fori_loop(0, 4, two_steps, jnp.zeros((8, BW), F32))
    step(None, None, buf1, place_of(3, True), high, 1, 6)
    second = push_1(0, 1)
    drain(ag.values())
    for half, copies in ((0, first), (1, second)):
        landed(copies)
        merged = log_summed(rl[0, half], ra.at[0, half], 7)
        for j in range(8):
            place = place_of(2 * half + j // 4, j // 2 % 2 == 1)
            rl2[0, place // 4, pl.ds((place % 4) * 2 + j % 2, 1), :] = merged[j:j + 1, :]
    first, second = push_2(0, 0), push_2(0, 1)

    def start_weights(half):
        whole = log_summed(rl2[0, half], rb.at[0, half], 3)
        factor = jnp.exp2(top_of[half] - whole)
        fac[half] = factor
        rw[half] = factor * (1.0 / TOTAL)

    landed(first)
    start_weights(0)

    lane = lax.broadcasted_iota(jnp.int32, (8, 128), 1)

    def mass_half(half):
        def chunk(t, _):
            def tile(i):
                return pl.ds(pl.multiple_of(t * CH + 8 * i, 8), 8)

            acc = [None if half == 0 else part[tile(i), :] for i in range(16)]
            for b in range(4 * half, 4 * half + 4):
                for l in range(4):
                    r = (b % 4) * 2 + l // 2
                    w = jnp.broadcast_to(rw[half, r:r + 1, (l % 2) * 128:(l % 2) * 128 + 128], (8, 128))
                    for i in range(16):
                        value = kern[b, tile(i), l * 128:l * 128 + 128] * w
                        acc[i] = value if acc[i] is None else acc[i] + value
            for i in range(16):
                if half == 0:
                    part[tile(i), :] = acc[i]
                else:
                    total = jnp.sum(acc[i], axis=1, keepdims=True)
                    rows = slice(8 * i, 8 * i + 8)
                    col[rows, :] = jnp.where(lane == t, total, col[rows, :])
            return 0

        lax.fori_loop(0, NZ, chunk, 0)

    def row_half(n, half):
        def chunk(t, acc):
            acc = list(acc)
            for i in range(16):
                tile = pl.ds(pl.multiple_of(t * CH + 8 * i, 8), 8)
                s = scol[tile, :]
                for b in range(4):
                    for l in range(4):
                        acc[4 * b + l] += kern[4 * half + b, tile, l * 128:l * 128 + 128] * s
            return tuple(acc)

        acc = lax.fori_loop(0, NZ, chunk, tuple(jnp.zeros((8, 128), F32) for _ in range(16)))
        for b in range(4):
            for l in range(4):
                r, lanes = b * 2 + l // 2, slice((l % 2) * 128, (l % 2) * 128 + 128)
                total = jnp.sum(acc[4 * b + l], axis=0, keepdims=True)
                rl[n, half, r:r + 1, lanes] = total * fac[half, r:r + 1, lanes]

    col[...] = jnp.zeros((CH, CH), F32)
    for n in range(2):
        mass_half(0)
        landed(second)
        if n == 0:
            start_weights(1)
        else:
            rw[1] = fac[1] / (TOTAL * summed(rl2[n, 1], rb.at[n, 1], 3))
        mass_half(1)
        ml[n] = col[...].T[0:NZ, :]
        before = sent[:]
        sent.clear()
        copies = push(ml.at[n], mr.at[n], z_peers, m_s.at[n], m_r.at[n])
        drain(before)
        landed(copies)
        scale = 1.0 / (TOTAL * summed(ml[n], mr.at[n], 7))
        columns = jnp.concatenate([scale, jnp.zeros((CH - NZ, CH), F32)], axis=0).T
        for t in range(NZ):
            scol[t * CH:(t + 1) * CH, :] = jnp.broadcast_to(columns[:, t:t + 1], (CH, CH))
        row_half(n + 1, 0)
        first = push_1(n + 1, 0)
        row_half(n + 1, 1)
        second = push_1(n + 1, 1)
        landed(first)
        rl2[n + 1, 0] = summed(rl[n + 1, 0], ra.at[n + 1, 0], 7)
        first = push_2(n + 1, 0)
        landed(second)
        rl2[n + 1, 1] = summed(rl[n + 1, 1], ra.at[n + 1, 1], 7)
        second = push_2(n + 1, 1)
        landed(first)
        rw[0] = fac[0] / (TOTAL * summed(rl2[n + 1, 0], rb.at[n + 1, 0], 3))

    def chunk_at(q):
        return (z + q + NZ) % NZ

    def weigh(w, i, b):
        ws = [rw[b // 4, pl.ds((b % 4) * 2 + j, 1), :] for j in range(2)]
        for j, q in enumerate(GROUPS[i]):
            rows = pl.ds(pl.multiple_of(chunk_at(q) * CH, CH), CH)
            place = slice((GROUP * i + j) * CH, (GROUP * i + j + 1) * CH)
            acc = part[place, :]
            for l in range(BW // 128):
                value = kern[b, rows, l * 128:l * 128 + 128] * ws[l // 2][:, (l % 2) * 128:(l % 2) * 128 + 128]
                acc = acc + value
                w[j * CH:(j + 1) * CH, l * 128:(l + 1) * 128] = value.astype(BF16)
            part[place, :] = acc

    def multiply(w, i, b):
        e = emb[pl.ds(b * 8, 8)].reshape(BW, D)
        num[GROUP * i:GROUP * i + GROUP] += jnp.dot(w[...], e, preferred_element_type=F32).reshape(GROUP, CH, D)

    def group(i, start, stop):
        def two(k, _):
            weigh(w1, i, 2 * k + 1)
            multiply(w0, i, 2 * k)
            weigh(w0, i, 2 * k + 2)
            multiply(w1, i, 2 * k + 1)
            return 0

        lax.fori_loop(start, stop, two, 0)

    def group_end(i):
        weigh(w1, i, 7)
        multiply(w0, i, 6)
        if i + 1 < len(GROUPS):
            weigh(w0, i + 1, 0)
        multiply(w1, i, 7)

    rs = {}

    def hop(name, q, rows, before=None):
        sign = (1 if name[0] in ("RA", "RB") else -1)
        i = len(rs)
        value = num[POS[q], rows, :]
        if before is not None:
            rs[before].wait_recv()
            value = value + rcv[slot[before]].astype(F32)
        snd[i] = value.astype(BF16)
        slot[name] = i
        copy = pltpu.make_async_remote_copy(
            src_ref=snd.at[i], dst_ref=rcv.at[i], send_sem=rs_s.at[i], recv_sem=rs_r.at[i],
            device_id=at(dz=sign), device_id_type=MESH,
        )
        copy.start()
        rs[name] = copy

    slot = {}
    lo, hi = slice(0, 64), slice(64, 128)

    part[...] = jnp.zeros((C, 128), F32)
    weigh(w0, 0, 0)
    num[...] = jnp.zeros((NZ, CH, D), F32)
    group(0, 0, 1)
    landed(second)
    rw[1] = fac[1] / (TOTAL * summed(rl2[2, 1], rb.at[2, 1], 3))
    group(0, 1, 3)
    group_end(0)
    hop(("RB", 0), 4, lo)
    hop(("LB", 0), 4, hi)
    hop(("RA", 1), 3, hi)
    drain(sent)
    sent.clear()
    group(1, 0, 3)
    group_end(1)
    hop(("LA", 1), -3, lo)
    hop(("RB", 1), 3, lo, ("RB", 0))
    hop(("LB", 1), -3, hi, ("LB", 0))
    group(2, 0, 1)
    hop(("RA", 2), 2, hi, ("RA", 1))
    group(2, 1, 3)
    group_end(2)
    hop(("LA", 2), -2, lo, ("LA", 1))
    hop(("RB", 2), 2, lo, ("RB", 1))
    hop(("LB", 2), -2, hi, ("LB", 1))
    group(3, 0, 1)
    hop(("RA", 3), 1, hi, ("RA", 2))
    group(3, 1, 3)
    weigh(w1, 3, 7)
    for j, q in enumerate(q for g in GROUPS for q in g):
        for i in range(16):
            rows = slice(8 * i, 8 * i + 8)
            total = jnp.sum(part[j * CH + 8 * i:j * CH + 8 * i + 8, :], axis=1, keepdims=True)
            col[rows, :] = jnp.where(lane == chunk_at(q), total, col[rows, :])
    ml[2] = col[...].T[0:NZ, :]
    last = push(ml.at[2], mr.at[2], z_peers, m_s.at[2], m_r.at[2])
    multiply(w0, 3, 6)
    multiply(w1, 3, 7)
    hop(("LA", 3), -1, lo, ("LA", 2))
    hop(("RB", 3), 1, lo, ("RB", 2))
    hop(("LB", 3), -1, hi, ("LB", 2))
    drain(last)
    drain(rs.values())

    for copy in last:
        copy.wait_recv()
    mass = ml[2, pl.ds(z, 1), :]
    for k in range(7):
        mass = mass + mr[2, k, pl.ds(z, 1), :]
    column = jnp.broadcast_to(mass, (CH, CH)).T
    column = jnp.concatenate([column] * (D // CH), axis=1)
    for rows, one, two in ((hi, ("RA", 3), ("LB", 3)), (lo, ("LA", 3), ("RB", 3))):
        rs[one].wait_recv()
        rs[two].wait_recv()
        total = num[POS[0], rows, :] + rcv[slot[one]].astype(F32) + rcv[slot[two]].astype(F32)
        out_ref[rows, :] = (total / column[rows, :]).astype(BF16)


def local(embeddings, centroids):
    e = embeddings.reshape(16, PIECE, D)
    k = centroids.reshape(NZ, NY, CH, D)
    dma = pltpu.SemaphoreType.DMA
    v = pltpu.VMEM
    out = pl.pallas_call(
        body,
        out_shape=jax.ShapeDtypeStruct((CH, D), BF16),
        in_specs=[pl.BlockSpec(memory_space=pl.ANY)] * 2,
        out_specs=pl.BlockSpec(memory_space=pltpu.VMEM),
        scratch_shapes=[
            v((64, PIECE, D), BF16), v((NZ, CH, D), BF16), v((NB, C, BW), F32), v((C, BW), F32), v((C, BW), F32),
            v((2, 8, 256), F32), v((3, 2, 8, 256), F32), v((3, 2, 8, 256), F32),
            v((3, 2, 7, 8, 256), F32), v((3, 2, 3, 8, 256), F32),
            v((2, 8, 256), F32), v((2, 8, 256), F32), v((C, 128), F32), v((C, 128), F32), v((CH, CH), F32),
            v((3, NZ, CH), F32), v((3, 7, NZ, CH), F32),
            v((GROUP * CH, BW), BF16), v((GROUP * CH, BW), BF16), v((NZ, CH, D), F32),
            v((14, 64, D), BF16), v((14, 64, D), BF16),
            dma((2,)), dma((48,)), dma((48,)), dma((3, 2, 7)), dma((3, 2, 7)), dma((3, 2, 3)), dma((3, 2, 3)),
            dma((3, 7)), dma((3, 7)), dma((14,)), dma((14,)),
        ],
        compiler_params=pltpu.CompilerParams(
            collective_id=0, has_side_effects=True, vmem_limit_bytes=60 * 1024 * 1024
        ),
        cost_estimate=pl.CostEstimate(
            flops=4 * C * NB * BW * D, bytes_accessed=8 * 1024 * 1024, transcendentals=C * NB * BW
        ),
    )(e, k)
    return out[None]


def solution(mesh):
    return jax.shard_map(
        local,
        mesh=mesh,
        in_specs=(P("docs", None), P("cent", None)),
        out_specs=P("cent", "docs", None),
        check_vma=False,
    )
```

```python
import jax
import jax.numpy as jnp
import numpy as np
from jax import lax
from jax.experimental import pallas as pl
from jax.experimental.pallas import tpu as pltpu
from jax.sharding import PartitionSpec as P

MESH = pl.DeviceIdType.MESH
F32 = jnp.float32
BF16 = jnp.bfloat16

NX, NY, NZ = 4, 4, 8
D = 768
PIECE = 64
NB, BW = 8, 512
CH = 128
C = NZ * CH
TOTAL = 32768.0
EXP2_SCALE = 10.0 * float(np.log2(np.e))

GROUPS = ((4, 3), (-3, 2), (-2, 1), (-1, 0))
GROUP = len(GROUPS[0])
POS = {q: i for i, q in enumerate(q for group in GROUPS for q in group)}
LN2 = float(np.log(2.0))


def body(
    emb_hbm, cen_hbm, out_ref,
    emb, cen, kern, buf0, buf1,
    top_of, rl, rl2, ra, rb, fac, rw, part, scol, col, ml, mr, w0, w1, num, snd, rcv,
    ld_sem, ag_s, ag_r, r1_s, r1_r, r2_s, r2_r, m_s, m_r, rs_s, rs_r,
):
    docs = lax.axis_index("docs")
    cent = lax.axis_index("cent")
    z, y = docs // NY, docs % NY
    x, c = cent // 2, cent % 2

    def at(dz=0, dy=0, dx=0, flip=False):
        zz = (z + dz + NZ) % NZ
        yy = (y + dy + NY) % NY
        xx = (x + dx + NX) % NX
        return (zz * NY + yy, xx * 2 + ((1 - c) if flip else c))

    load_e = pltpu.make_async_copy(emb_hbm, emb.at[pl.ds(y * 16, 16)], ld_sem.at[0])
    load_c = pltpu.make_async_copy(cen_hbm.at[:, y], cen, ld_sem.at[1])
    load_e.start()
    load_c.start()

    cent_peers = [(docs, (cent + k) % 8) for k in range(1, 8)]
    y_peers = [at(dy=k) for k in range(1, NY)]
    z_peers = [at(dz=k) for k in range(1, NZ)]
    barrier = pltpu.get_barrier_semaphore()
    for peer in cent_peers + y_peers + z_peers:
        pl.semaphore_signal(barrier, inc=1, device_id=peer, device_id_type=MESH)
    pl.semaphore_wait(barrier, len(cent_peers) + len(y_peers) + len(z_peers))

    def piece(dy, h, dx):
        return ((y + dy + NY) % NY) * 16 + h * 8 + ((x + dx + NX) % NX) * 2 + c

    ag = {}

    landing = {}

    def plan(name, where, target, together, src=None):
        ag[name] = pltpu.make_async_remote_copy(
            src_ref=emb.at[where] if src is None else src, dst_ref=emb.at[where], send_sem=ag_s.at[0],
            recv_sem=ag_r.at[landing.setdefault(together, len(landing))], device_id=target, device_id_type=MESH,
        )

    def plan_own(name, h, dx, s, together):
        plan(name, piece(0, h, dx), at(dy=s), together, emb_hbm.at[h * 8 + ((x + dx + NX) % NX) * 2 + c])

    plan_own(("f", 1), 1, 0, 1, "f")
    plan_own(("f", -1), 0, 0, -1, "f")
    plan_own(("g", 1), 0, 0, 1, "g")
    plan_own(("g", -1), 1, 0, -1, "g")
    plan(("y3", 1), piece(-1, 1, 0), at(dy=1), "y3")
    plan(("y3", -1), piece(1, 0, 0), at(dy=-1), "y3")
    for k in (1, 2, -1):
        for s in (1, -1):
            plan_own(("k", s, k), 0, k, s, ("k", k > 0))
    for dy, h in ((-1, 1), (1, 1), (2, 0), (2, 1)):
        for s in (1, -1):
            key = ("x1", dy) if h == 1 and dy != 2 else ("x1", 2, (h == 0) == (s == 1))
            plan(("x1", s, dy, h), piece(dy, h, 0), at(dx=s), key)
    for s, dy, h in ((-1, -1, 1), (1, 1, 1), (1, 2, 0), (-1, 2, 1)):
        plan(("x2", s, dy, h), piece(dy, h, -s), at(dx=s), ("x2", dy == 2))
    for dy in (-1, 1, 2):
        for h in (0, 1):
            for dx in (0, 1, 2, -1):
                plan(("s", dy, h, dx), piece(dy, h, dx), at(flip=True), ("s", dy, h))

    def whole(ref, ssem, rsem):
        return pltpu.make_async_remote_copy(
            src_ref=ref, dst_ref=ref, send_sem=ssem, recv_sem=rsem, device_id=at(flip=True), device_id_type=MESH
        )

    def send(*names):
        for name in names:
            ag[name].start()

    def got(together, n=2):
        whole(emb.at[pl.ds(0, n)], ag_s.at[0], ag_r.at[landing[together]]).wait_recv()

    def to_sibling(*pieces):
        send(*[("s", *p) for p in pieces])

    def block_ready(dy, h):
        got(("s", dy, h), 4)

    send(("f", 1), ("f", -1), ("g", 1), ("g", -1))
    load_e.wait()
    load_c.wait()

    def phase_a():
        got("f")
        send(("x1", 1, -1, 1), ("x1", -1, -1, 1), ("y3", 1), ("y3", -1))
        send(*[("k", s, k) for k in (1, 2, -1) for s in (1, -1)])
        to_sibling((-1, 1, 0), (1, 0, 0))

    def phase_c():
        got("g")
        send(("x1", 1, 1, 1), ("x1", -1, 1, 1))
        to_sibling((-1, 0, 0), (1, 1, 0))
        got(("x1", -1))
        send(("x2", -1, -1, 1))
        to_sibling((-1, 1, 1), (-1, 1, -1))
        got(("x1", 1))
        send(("x2", 1, 1, 1))
        to_sibling((1, 1, -1), (1, 1, 1))
        got("y3")
        send(("x1", 1, 2, 0), ("x1", -1, 2, 1), ("x1", 1, 2, 1), ("x1", -1, 2, 0))
        to_sibling((2, 1, 0), (2, 0, 0))
        got(("x2", False))
        to_sibling((1, 1, 2), (-1, 1, 2))
        block_ready(1, 1)

    def phase_f():
        got(("k", True), 4)
        for k in (1, 2):
            to_sibling((1, 0, k), (-1, 0, k))
        block_ready(-1, 1)

    def phase_g():
        got(("x1", 2, True))
        send(("x2", 1, 2, 0), ("x2", -1, 2, 1))
        to_sibling((2, 0, -1), (2, 1, 1))
        got(("k", False))
        to_sibling((1, 0, -1), (-1, 0, -1))
        block_ready(1, 0)

    def phase_h():
        got(("x1", 2, False))
        to_sibling((2, 1, -1), (2, 0, 1))
        block_ready(-1, 0)

    def phase_i():
        got(("x2", True))
        to_sibling((2, 0, 2), (2, 1, 2))
        block_ready(2, 0)

    def phase_j():
        block_ready(2, 1)

    sent = []

    def push(src, dst, peers, ssem, rsem, start=True):
        copies = [
            pltpu.make_async_remote_copy(
                src_ref=src, dst_ref=dst.at[k], send_sem=ssem, recv_sem=rsem, device_id=peer, device_id_type=MESH
            )
            for k, peer in enumerate(peers)
        ]
        if start:
            begin(copies)
        both = whole(dst, ssem, rsem)
        sent.append(both)
        return both, copies

    def begin(copies):
        for copy in copies:
            copy.start()

    def landed(pushed):
        pushed[0].wait_recv()

    def drain(wholes):
        for copy in wholes:
            copy.wait_send()

    def push_1(n, half, start=True):
        return push(rl.at[n, half], ra.at[n, half], cent_peers, r1_s.at[n, half], r1_r.at[n, half], start)

    def push_2(n, half):
        return push(rl2.at[n, half], rb.at[n, half], y_peers, r2_s.at[n, half], r2_r.at[n, half])

    def summed(own, others, n):
        total = own
        for k in range(n):
            total = total + others[k]
        return total

    def log_summed(own, others, n):
        top = own
        for k in range(n):
            top = jnp.maximum(top, others[k])
        total = jnp.exp2(own - top)
        for k in range(n):
            total = total + jnp.exp2(others[k] - top)
        return top + jnp.log(total) * (1.0 / LN2)

    def place_of(p, odd):
        d = (p + 1) // 2
        if odd:
            return ((y - d + NY) % NY) * 2 + 1 - (1 - p % 2) * (p // 2)
        return ((y + d) % NY) * 2 + (p % 2) * (1 - p // 2)

    def step(new_buf, new, old_buf, old, old_max, half, row):
        top = jnp.max(old_max, axis=0, keepdims=True)
        total = jnp.zeros((8, BW), F32)
        new_max = []
        if new is not None:
            e = emb[pl.ds(new * 8, 8)].reshape(BW, D)
        for i in range(4):
            if new is not None and i % 2 == 0:
                lanes = slice(128 * i, 128 * i + 256)
                raw = lax.dot_general(
                    cen[...].reshape(C, D), e[lanes, :], (((1,), (1,)), ((), ())), preferred_element_type=F32
                )
                new_buf[:, lanes] = raw
                new_max.append(jnp.max(raw.reshape(C // 8, 8, 256), axis=0))
            for k in range(4):
                rows = slice(256 * i + 64 * k, 256 * i + 64 * k + 64)
                value = jnp.exp2((old_buf[rows, :] - top) * EXP2_SCALE)
                kern[old, rows, :] = value
                total = total + jnp.sum(value.reshape(8, 8, BW), axis=0)
        if new is not None:
            new_max = jnp.concatenate(new_max, axis=1)
        scaled = top * EXP2_SCALE
        whole = scaled + jnp.log(jnp.sum(total, axis=0, keepdims=True)) * (1.0 / LN2)
        for j in range(2):
            lanes = slice(256 * j, 256 * j + 256)
            rl[0, half, pl.ds(row + j, 1), :] = whole[:, lanes]
            top_of[old // 4, pl.ds((old % 4) * 2 + j, 1), :] = scaled[:, lanes]
        return new_max

    first = push_1(0, 0, start=False)

    def two_steps(p, high):
        pl.when(p == 1)(phase_c)
        pl.when(p == 2)(phase_g)
        pl.when(p == 3)(phase_i)
        q = (p + 3) % 4
        high = step(buf0, place_of(p, False), buf1, place_of(q, True), high, q // 2, (q % 2) * 4 + 2)
        pl.when(p == 0)(phase_a)
        pl.when(p == 1)(phase_f)

        @pl.when(p == 2)
        def _():
            begin(first[1])
            phase_h()

        pl.when(p == 3)(phase_j)
        return step(buf1, place_of(p, True), buf0, place_of(p, False), high, p // 2, (p % 2) * 4)

    buf1[...] = jnp.zeros((C, BW), F32)
    high = lax.fori_loop(0, 4, two_steps, jnp.zeros((8, BW), F32))
    step(None, None, buf1, place_of(3, True), high, 1, 6)
    second = push_1(0, 1)
    whole(emb.at[pl.ds(0, 48)], ag_s.at[0], ag_r.at[0]).wait_send()
    for half, copies in ((0, first), (1, second)):
        landed(copies)
        merged = log_summed(rl[0, half], ra.at[0, half], 7)
        for j in range(8):
            place = place_of(2 * half + j // 4, j // 2 % 2 == 1)
            rl2[0, place // 4, pl.ds((place % 4) * 2 + j % 2, 1), :] = merged[j:j + 1, :]
    first, second = push_2(0, 0), push_2(0, 1)

    def start_weights(half):
        whole = log_summed(rl2[0, half], rb.at[0, half], 3)
        factor = jnp.exp2(top_of[half] - whole)
        fac[half] = factor
        rw[half] = factor * (1.0 / TOTAL)

    landed(first)
    start_weights(0)

    lane = lax.broadcasted_iota(jnp.int32, (8, 128), 1)

    def mass_half(half):
        def chunk(t, _):
            def tile(i):
                return pl.ds(pl.multiple_of(t * CH + 8 * i, 8), 8)

            acc = [None if half == 0 else part[tile(i), :] for i in range(16)]
            for b in range(4 * half, 4 * half + 4):
                for l in range(4):
                    r = (b % 4) * 2 + l // 2
                    w = jnp.broadcast_to(rw[half, r:r + 1, (l % 2) * 128:(l % 2) * 128 + 128], (8, 128))
                    for i in range(16):
                        value = kern[b, tile(i), l * 128:l * 128 + 128] * w
                        acc[i] = value if acc[i] is None else acc[i] + value
            for i in range(16):
                if half == 0:
                    part[tile(i), :] = acc[i]
                else:
                    total = jnp.sum(acc[i], axis=1, keepdims=True)
                    rows = slice(8 * i, 8 * i + 8)
                    col[rows, :] = jnp.where(lane == t, total, col[rows, :])
            return 0

        lax.fori_loop(0, NZ, chunk, 0)

    def row_half(n, half):
        def chunk(t, acc):
            acc = list(acc)
            for i in range(16):
                tile = pl.ds(pl.multiple_of(t * CH + 8 * i, 8), 8)
                s = scol[tile, :]
                for b in range(4):
                    for l in range(4):
                        acc[4 * b + l] += kern[4 * half + b, tile, l * 128:l * 128 + 128] * s
            return tuple(acc)

        acc = lax.fori_loop(0, NZ, chunk, tuple(jnp.zeros((8, 128), F32) for _ in range(16)))
        for b in range(4):
            for l in range(4):
                r, lanes = b * 2 + l // 2, slice((l % 2) * 128, (l % 2) * 128 + 128)
                total = jnp.sum(acc[4 * b + l], axis=0, keepdims=True)
                rl[n, half, r:r + 1, lanes] = total * fac[half, r:r + 1, lanes]

    col[...] = jnp.zeros((CH, CH), F32)
    for n in range(2):
        mass_half(0)
        landed(second)
        if n == 0:
            start_weights(1)
        else:
            rw[1] = fac[1] / (TOTAL * summed(rl2[n, 1], rb.at[n, 1], 3))
        mass_half(1)
        ml[n] = col[...].T[0:NZ, :]
        before = sent[:]
        sent.clear()
        copies = push(ml.at[n], mr.at[n], z_peers, m_s.at[n], m_r.at[n])
        drain(before)
        landed(copies)
        scale = 1.0 / (TOTAL * summed(ml[n], mr.at[n], 7))
        columns = jnp.concatenate([scale, jnp.zeros((CH - NZ, CH), F32)], axis=0).T
        for t in range(NZ):
            scol[t * CH:(t + 1) * CH, :] = jnp.broadcast_to(columns[:, t:t + 1], (CH, CH))
        row_half(n + 1, 0)
        first = push_1(n + 1, 0)
        row_half(n + 1, 1)
        second = push_1(n + 1, 1)
        landed(first)
        rl2[n + 1, 0] = summed(rl[n + 1, 0], ra.at[n + 1, 0], 7)
        first = push_2(n + 1, 0)
        landed(second)
        rl2[n + 1, 1] = summed(rl[n + 1, 1], ra.at[n + 1, 1], 7)
        second = push_2(n + 1, 1)
        landed(first)
        rw[0] = fac[0] / (TOTAL * summed(rl2[n + 1, 0], rb.at[n + 1, 0], 3))

    def chunk_at(q):
        return (z + q + NZ) % NZ

    def weigh(w, i, b):
        ws = [rw[b // 4, pl.ds((b % 4) * 2 + j, 1), :] for j in range(2)]
        for j, q in enumerate(GROUPS[i]):
            rows = pl.ds(pl.multiple_of(chunk_at(q) * CH, CH), CH)
            place = slice((GROUP * i + j) * CH, (GROUP * i + j + 1) * CH)
            acc = part[place, :]
            for l in range(BW // 128):
                value = kern[b, rows, l * 128:l * 128 + 128] * ws[l // 2][:, (l % 2) * 128:(l % 2) * 128 + 128]
                acc = acc + value
                w[j * CH:(j + 1) * CH, l * 128:(l + 1) * 128] = value.astype(BF16)
            part[place, :] = acc

    def multiply(w, i, b):
        e = emb[pl.ds(b * 8, 8)].reshape(BW, D)
        num[GROUP * i:GROUP * i + GROUP] += jnp.dot(w[...], e, preferred_element_type=F32).reshape(GROUP, CH, D)

    def group(i, start, stop):
        def two(k, _):
            weigh(w1, i, 2 * k + 1)
            multiply(w0, i, 2 * k)
            weigh(w0, i, 2 * k + 2)
            multiply(w1, i, 2 * k + 1)
            return 0

        lax.fori_loop(start, stop, two, 0)

    def group_end(i):
        weigh(w1, i, 7)
        multiply(w0, i, 6)
        if i + 1 < len(GROUPS):
            weigh(w0, i + 1, 0)
        multiply(w1, i, 7)

    rs = {}

    def hop(name, q, rows, before=None):
        sign = (1 if name[0] in ("RA", "RB") else -1)
        i = len(rs)
        value = num[POS[q], rows, :]
        if before is not None:
            rs[before].wait_recv()
            value = value + rcv[slot[before]].astype(F32)
        snd[i] = value.astype(BF16)
        slot[name] = i
        copy = pltpu.make_async_remote_copy(
            src_ref=snd.at[i], dst_ref=rcv.at[i], send_sem=rs_s.at[0], recv_sem=rs_r.at[i],
            device_id=at(dz=sign), device_id_type=MESH,
        )
        copy.start()
        rs[name] = copy

    slot = {}
    lo, hi = slice(0, 64), slice(64, 128)

    part[...] = jnp.zeros((C, 128), F32)
    weigh(w0, 0, 0)
    num[...] = jnp.zeros((NZ, CH, D), F32)
    group(0, 0, 1)
    landed(second)
    rw[1] = fac[1] / (TOTAL * summed(rl2[2, 1], rb.at[2, 1], 3))
    group(0, 1, 3)
    group_end(0)
    hop(("RB", 0), 4, lo)
    hop(("LB", 0), 4, hi)
    hop(("RA", 1), 3, hi)
    drain(sent)
    sent.clear()
    group(1, 0, 3)
    group_end(1)
    hop(("LA", 1), -3, lo)
    hop(("RB", 1), 3, lo, ("RB", 0))
    hop(("LB", 1), -3, hi, ("LB", 0))
    group(2, 0, 1)
    hop(("RA", 2), 2, hi, ("RA", 1))
    group(2, 1, 3)
    group_end(2)
    hop(("LA", 2), -2, lo, ("LA", 1))
    hop(("RB", 2), 2, lo, ("RB", 1))
    hop(("LB", 2), -2, hi, ("LB", 1))
    group(3, 0, 1)
    hop(("RA", 3), 1, hi, ("RA", 2))
    group(3, 1, 3)
    weigh(w1, 3, 7)
    for j, q in enumerate(q for g in GROUPS for q in g):
        for i in range(16):
            rows = slice(8 * i, 8 * i + 8)
            total = jnp.sum(part[j * CH + 8 * i:j * CH + 8 * i + 8, :], axis=1, keepdims=True)
            col[rows, :] = jnp.where(lane == chunk_at(q), total, col[rows, :])
    ml[2] = col[...].T[0:NZ, :]
    last = push(ml.at[2], mr.at[2], z_peers, m_s.at[2], m_r.at[2])
    multiply(w0, 3, 6)
    multiply(w1, 3, 7)
    hop(("LA", 3), -1, lo, ("LA", 2))
    hop(("RB", 3), 1, lo, ("RB", 2))
    hop(("LB", 3), -1, hi, ("LB", 2))
    drain(last[:1])
    whole(snd, rs_s.at[0], rs_r.at[0]).wait_send()

    landed(last)
    mass = ml[2, pl.ds(z, 1), :]
    for k in range(7):
        mass = mass + mr[2, k, pl.ds(z, 1), :]
    column = jnp.broadcast_to(mass, (CH, CH)).T
    column = jnp.concatenate([column] * (D // CH), axis=1)
    for rows, one, two in ((hi, ("RA", 3), ("LB", 3)), (lo, ("LA", 3), ("RB", 3))):
        rs[one].wait_recv()
        rs[two].wait_recv()
        total = num[POS[0], rows, :] + rcv[slot[one]].astype(F32) + rcv[slot[two]].astype(F32)
        out_ref[rows, :] = (total / column[rows, :]).astype(BF16)


def local(embeddings, centroids):
    e = embeddings.reshape(16, PIECE, D)
    k = centroids.reshape(NZ, NY, CH, D)
    dma = pltpu.SemaphoreType.DMA
    v = pltpu.VMEM
    out = pl.pallas_call(
        body,
        out_shape=jax.ShapeDtypeStruct((CH, D), BF16),
        in_specs=[pl.BlockSpec(memory_space=pl.ANY)] * 2,
        out_specs=pl.BlockSpec(memory_space=pltpu.VMEM),
        scratch_shapes=[
            v((64, PIECE, D), BF16), v((NZ, CH, D), BF16), v((NB, C, BW), F32), v((C, BW), F32), v((C, BW), F32),
            v((2, 8, 256), F32), v((3, 2, 8, 256), F32), v((3, 2, 8, 256), F32),
            v((3, 2, 7, 8, 256), F32), v((3, 2, 3, 8, 256), F32),
            v((2, 8, 256), F32), v((2, 8, 256), F32), v((C, 128), F32), v((C, 128), F32), v((CH, CH), F32),
            v((3, NZ, CH), F32), v((3, 7, NZ, CH), F32),
            v((GROUP * CH, BW), BF16), v((GROUP * CH, BW), BF16), v((NZ, CH, D), F32),
            v((14, 64, D), BF16), v((14, 64, D), BF16),
            dma((2,)), dma((1,)), dma((17,)), dma((3, 2)), dma((3, 2)), dma((3, 2)), dma((3, 2)),
            dma((3,)), dma((3,)), dma((1,)), dma((14,)),
        ],
        compiler_params=pltpu.CompilerParams(
            collective_id=0, has_side_effects=True, vmem_limit_bytes=60 * 1024 * 1024
        ),
        cost_estimate=pl.CostEstimate(
            flops=4 * C * NB * BW * D, bytes_accessed=8 * 1024 * 1024, transcendentals=C * NB * BW
        ),
    )(e, k)
    return out[None]


def solution(mesh):
    return jax.shard_map(
        local,
        mesh=mesh,
        in_specs=(P("docs", None), P("cent", None)),
        out_specs=P("cent", "docs", None),
        check_vma=False,
    )
```

```python
import jax
import jax.numpy as jnp
import numpy as np
from jax import lax
from jax.experimental import pallas as pl
from jax.experimental.pallas import tpu as pltpu
from jax.sharding import PartitionSpec as P

MESH = pl.DeviceIdType.MESH
F32 = jnp.float32
BF16 = jnp.bfloat16

NX, NY, NZ = 4, 4, 8
D = 768
PIECE = 64
NB, BW = 8, 512
CH = 128
C = NZ * CH
TOTAL = 32768.0
EXP2_SCALE = 10.0 * float(np.log2(np.e))

GROUPS = ((4, 3), (-3, 2), (-2, 1), (-1, 0))
GROUP = len(GROUPS[0])
POS = {q: i for i, q in enumerate(q for group in GROUPS for q in group)}
LN2 = float(np.log(2.0))


def body(
    emb_hbm, cen_hbm, out_ref,
    emb, cen, kern, buf0, buf1,
    top_of, rl, rl2, ra, rb, fac, rw, part, scol, col, ml, mr, w0, w1, num, snd, rcv,
    ld_sem, ag_s, ag_r, r1_s, r1_r, r2_s, r2_r, m_s, m_r, rs_s, rs_r,
):
    docs = lax.axis_index("docs")
    cent = lax.axis_index("cent")
    z, y = docs // NY, docs % NY
    x, c = cent // 2, cent % 2

    def at(dz=0, dy=0, dx=0, flip=False):
        zz = (z + dz + NZ) % NZ
        yy = (y + dy + NY) % NY
        xx = (x + dx + NX) % NX
        return (zz * NY + yy, xx * 2 + ((1 - c) if flip else c))

    load_e = pltpu.make_async_copy(emb_hbm, emb.at[pl.ds(y * 16, 16)], ld_sem.at[0])
    load_c = pltpu.make_async_copy(cen_hbm.at[:, y], cen, ld_sem.at[1])
    load_e.start()
    load_c.start()

    cent_peers = [(docs, (cent + k) % 8) for k in range(1, 8)]
    y_peers = [at(dy=k) for k in range(1, NY)]
    z_peers = [at(dz=k) for k in range(1, NZ)]
    barrier = pltpu.get_barrier_semaphore()
    for peer in cent_peers + y_peers + z_peers:
        pl.semaphore_signal(barrier, inc=1, device_id=peer, device_id_type=MESH)
    pl.semaphore_wait(barrier, len(cent_peers) + len(y_peers) + len(z_peers))

    def piece(dy, h, dx):
        return ((y + dy + NY) % NY) * 16 + h * 8 + ((x + dx + NX) % NX) * 2 + c

    ag = {}

    landing = {}

    def plan(name, where, target, together, src=None):
        ag[name] = pltpu.make_async_remote_copy(
            src_ref=emb.at[where] if src is None else src, dst_ref=emb.at[where], send_sem=ag_s.at[0],
            recv_sem=ag_r.at[landing.setdefault(together, len(landing))], device_id=target, device_id_type=MESH,
        )

    def plan_own(name, h, dx, s, together):
        plan(name, piece(0, h, dx), at(dy=s), together, emb_hbm.at[h * 8 + ((x + dx + NX) % NX) * 2 + c])

    plan_own(("f", 1), 1, 0, 1, "f")
    plan_own(("f", -1), 0, 0, -1, "f")
    plan_own(("g", 1), 0, 0, 1, "g")
    plan_own(("g", -1), 1, 0, -1, "g")
    plan(("y3", 1), piece(-1, 1, 0), at(dy=1), "y3")
    plan(("y3", -1), piece(1, 0, 0), at(dy=-1), "y3")
    for k in (1, 2, -1):
        for s in (1, -1):
            plan_own(("k", s, k), 0, k, s, ("k", k))
    for dy, h in ((-1, 1), (1, 1), (2, 0), (2, 1)):
        for s in (1, -1):
            key = ("x1", dy) if h == 1 and dy != 2 else ("x1", 2, (h == 0) == (s == 1))
            plan(("x1", s, dy, h), piece(dy, h, 0), at(dx=s), key)
    for s, dy, h in ((-1, -1, 1), (1, 1, 1), (1, 2, 0), (-1, 2, 1)):
        plan(("x2", s, dy, h), piece(dy, h, -s), at(dx=s), ("x2", dy))
    for dy in (-1, 1, 2):
        for h in (0, 1):
            for dx in (0, 1, 2, -1):
                plan(("s", dy, h, dx), piece(dy, h, dx), at(flip=True), ("s", dy, h))

    def whole(ref, ssem, rsem):
        return pltpu.make_async_remote_copy(
            src_ref=ref, dst_ref=ref, send_sem=ssem, recv_sem=rsem, device_id=at(flip=True), device_id_type=MESH
        )

    def send(*names):
        for name in names:
            ag[name].start()

    def got(together, n=2):
        whole(emb.at[pl.ds(0, n)], ag_s.at[0], ag_r.at[landing[together]]).wait_recv()

    def to_sibling(*pieces):
        send(*[("s", *p) for p in pieces])

    def block_ready(dy, h):
        got(("s", dy, h), 4)

    send(("f", 1), ("f", -1))
    load_e.wait()
    load_c.wait()

    def phase_a():
        send(("g", 1), ("g", -1))
        got("f")
        send(("y3", 1), ("y3", -1), ("x1", 1, -1, 1), ("x1", -1, -1, 1))
        to_sibling((-1, 1, 0), (1, 0, 0))

    def phase_c():
        got("g")
        send(("x1", 1, 1, 1), ("x1", -1, 1, 1), ("k", 1, 1), ("k", -1, 1))
        to_sibling((-1, 0, 0), (1, 1, 0))
        got(("x1", -1))
        send(("x2", -1, -1, 1))
        to_sibling((-1, 1, 1), (-1, 1, -1))
        got("y3")
        send(("x1", 1, 2, 0), ("x1", -1, 2, 1), ("k", 1, 2), ("k", -1, 2))
        to_sibling((2, 1, 0), (2, 0, 0))
        got(("x1", 1))
        send(("x2", 1, 1, 1), ("x1", 1, 2, 1), ("x1", -1, 2, 0), ("k", 1, -1), ("k", -1, -1))
        to_sibling((1, 1, -1), (1, 1, 1))
        got(("x2", -1), 1)
        to_sibling((-1, 1, 2))
        block_ready(-1, 1)

    def phase_f():
        for k in (1, 2):
            got(("k", k))
            to_sibling((1, 0, k), (-1, 0, k))
        got(("x1", 2, True))
        send(("x2", 1, 2, 0), ("x2", -1, 2, 1))
        to_sibling((2, 0, -1), (2, 1, 1))
        got(("x2", 1), 1)
        to_sibling((1, 1, 2))
        block_ready(1, 1)

    def phase_g():
        got(("k", -1))
        to_sibling((1, 0, -1), (-1, 0, -1))
        block_ready(-1, 0)

    def phase_h():
        got(("x1", 2, False))
        to_sibling((2, 1, -1), (2, 0, 1))
        block_ready(1, 0)

    def phase_i():
        got(("x2", 2))
        to_sibling((2, 0, 2), (2, 1, 2))
        block_ready(2, 0)

    def phase_j():
        block_ready(2, 1)

    sent = []

    def push(src, dst, peers, ssem, rsem, start=True):
        copies = [
            pltpu.make_async_remote_copy(
                src_ref=src, dst_ref=dst.at[k], send_sem=ssem, recv_sem=rsem, device_id=peer, device_id_type=MESH
            )
            for k, peer in enumerate(peers)
        ]
        if start:
            begin(copies)
        both = whole(dst, ssem, rsem)
        sent.append(both)
        return both, copies

    def begin(copies):
        for copy in copies:
            copy.start()

    def landed(pushed):
        pushed[0].wait_recv()

    def drain(wholes):
        for copy in wholes:
            copy.wait_send()

    def push_1(n, half, start=True):
        return push(rl.at[n, half], ra.at[n, half], cent_peers, r1_s.at[n, half], r1_r.at[n, half], start)

    def push_2(n, half):
        return push(rl2.at[n, half], rb.at[n, half], y_peers, r2_s.at[n, half], r2_r.at[n, half])

    def summed(own, others, n):
        total = own
        for k in range(n):
            total = total + others[k]
        return total

    def log_summed(own, others, n):
        top = own
        for k in range(n):
            top = jnp.maximum(top, others[k])
        total = jnp.exp2(own - top)
        for k in range(n):
            total = total + jnp.exp2(others[k] - top)
        return top + jnp.log(total) * (1.0 / LN2)

    def place_of(p, odd):
        d = (p + 1) // 2
        if odd:
            return ((y + d) % NY) * 2 + 1 - (1 - p % 2) * (p // 2)
        return ((y - d + NY) % NY) * 2 + (p % 2) * (1 - p // 2)

    def step(new_buf, new, old_buf, old, old_max, half, row):
        top = jnp.max(old_max, axis=0, keepdims=True)
        total = jnp.zeros((8, BW), F32)
        new_max = []
        if new is not None:
            e = emb[pl.ds(new * 8, 8)].reshape(BW, D)
        for i in range(4):
            if new is not None and i % 2 == 0:
                lanes = slice(128 * i, 128 * i + 256)
                raw = lax.dot_general(
                    cen[...].reshape(C, D), e[lanes, :], (((1,), (1,)), ((), ())), preferred_element_type=F32
                )
                new_buf[:, lanes] = raw
                new_max.append(jnp.max(raw.reshape(C // 8, 8, 256), axis=0))
            for k in range(4):
                rows = slice(256 * i + 64 * k, 256 * i + 64 * k + 64)
                value = jnp.exp2((old_buf[rows, :] - top) * EXP2_SCALE)
                kern[old, rows, :] = value
                total = total + jnp.sum(value.reshape(8, 8, BW), axis=0)
        if new is not None:
            new_max = jnp.concatenate(new_max, axis=1)
        scaled = top * EXP2_SCALE
        whole = scaled + jnp.log(jnp.sum(total, axis=0, keepdims=True)) * (1.0 / LN2)
        for j in range(2):
            lanes = slice(256 * j, 256 * j + 256)
            rl[0, half, pl.ds(row + j, 1), :] = whole[:, lanes]
            top_of[old // 4, pl.ds((old % 4) * 2 + j, 1), :] = scaled[:, lanes]
        return new_max

    first = push_1(0, 0, start=False)

    def two_steps(p, high):
        pl.when(p == 1)(phase_c)
        pl.when(p == 2)(phase_g)
        pl.when(p == 3)(phase_i)
        q = (p + 3) % 4
        high = step(buf0, place_of(p, False), buf1, place_of(q, True), high, q // 2, (q % 2) * 4 + 2)
        pl.when(p == 0)(phase_a)
        pl.when(p == 1)(phase_f)

        @pl.when(p == 2)
        def _():
            begin(first[1])
            phase_h()

        pl.when(p == 3)(phase_j)
        return step(buf1, place_of(p, True), buf0, place_of(p, False), high, p // 2, (p % 2) * 4)

    buf1[...] = jnp.zeros((C, BW), F32)
    high = lax.fori_loop(0, 4, two_steps, jnp.zeros((8, BW), F32))
    step(None, None, buf1, place_of(3, True), high, 1, 6)
    second = push_1(0, 1)
    whole(emb.at[pl.ds(0, 48)], ag_s.at[0], ag_r.at[0]).wait_send()
    for half, copies in ((0, first), (1, second)):
        landed(copies)
        merged = log_summed(rl[0, half], ra.at[0, half], 7)
        for j in range(8):
            place = place_of(2 * half + j // 4, j // 2 % 2 == 1)
            rl2[0, place // 4, pl.ds((place % 4) * 2 + j % 2, 1), :] = merged[j:j + 1, :]
    first, second = push_2(0, 0), push_2(0, 1)

    def start_weights(half):
        whole = log_summed(rl2[0, half], rb.at[0, half], 3)
        factor = jnp.exp2(top_of[half] - whole)
        fac[half] = factor
        rw[half] = factor * (1.0 / TOTAL)

    landed(first)
    start_weights(0)

    lane = lax.broadcasted_iota(jnp.int32, (8, 128), 1)

    def mass_half(half):
        def chunk(t, _):
            def tile(i):
                return pl.ds(pl.multiple_of(t * CH + 8 * i, 8), 8)

            acc = [None if half == 0 else part[tile(i), :] for i in range(16)]
            for b in range(4 * half, 4 * half + 4):
                for l in range(4):
                    r = (b % 4) * 2 + l // 2
                    w = jnp.broadcast_to(rw[half, r:r + 1, (l % 2) * 128:(l % 2) * 128 + 128], (8, 128))
                    for i in range(16):
                        value = kern[b, tile(i), l * 128:l * 128 + 128] * w
                        acc[i] = value if acc[i] is None else acc[i] + value
            for i in range(16):
                if half == 0:
                    part[tile(i), :] = acc[i]
                else:
                    total = jnp.sum(acc[i], axis=1, keepdims=True)
                    rows = slice(8 * i, 8 * i + 8)
                    col[rows, :] = jnp.where(lane == t, total, col[rows, :])
            return 0

        lax.fori_loop(0, NZ, chunk, 0)

    def row_half(n, half):
        def chunk(t, acc):
            acc = list(acc)
            for i in range(16):
                tile = pl.ds(pl.multiple_of(t * CH + 8 * i, 8), 8)
                s = scol[tile, :]
                for b in range(4):
                    for l in range(4):
                        acc[4 * b + l] += kern[4 * half + b, tile, l * 128:l * 128 + 128] * s
            return tuple(acc)

        acc = lax.fori_loop(0, NZ, chunk, tuple(jnp.zeros((8, 128), F32) for _ in range(16)))
        for b in range(4):
            for l in range(4):
                r, lanes = b * 2 + l // 2, slice((l % 2) * 128, (l % 2) * 128 + 128)
                total = jnp.sum(acc[4 * b + l], axis=0, keepdims=True)
                rl[n, half, r:r + 1, lanes] = total * fac[half, r:r + 1, lanes]

    col[...] = jnp.zeros((CH, CH), F32)
    for n in range(2):
        mass_half(0)
        landed(second)
        if n == 0:
            start_weights(1)
        else:
            rw[1] = fac[1] / (TOTAL * summed(rl2[n, 1], rb.at[n, 1], 3))
        mass_half(1)
        ml[n] = col[...].T[0:NZ, :]
        before = sent[:]
        sent.clear()
        copies = push(ml.at[n], mr.at[n], z_peers, m_s.at[n], m_r.at[n])
        drain(before)
        landed(copies)
        scale = 1.0 / (TOTAL * summed(ml[n], mr.at[n], 7))
        columns = jnp.concatenate([scale, jnp.zeros((CH - NZ, CH), F32)], axis=0).T
        for t in range(NZ):
            scol[t * CH:(t + 1) * CH, :] = jnp.broadcast_to(columns[:, t:t + 1], (CH, CH))
        row_half(n + 1, 0)
        first = push_1(n + 1, 0)
        row_half(n + 1, 1)
        second = push_1(n + 1, 1)
        landed(first)
        rl2[n + 1, 0] = summed(rl[n + 1, 0], ra.at[n + 1, 0], 7)
        first = push_2(n + 1, 0)
        landed(second)
        rl2[n + 1, 1] = summed(rl[n + 1, 1], ra.at[n + 1, 1], 7)
        second = push_2(n + 1, 1)
        landed(first)
        rw[0] = fac[0] / (TOTAL * summed(rl2[n + 1, 0], rb.at[n + 1, 0], 3))

    def chunk_at(q):
        return (z + q + NZ) % NZ

    def weigh(w, i, b):
        ws = [rw[b // 4, pl.ds((b % 4) * 2 + j, 1), :] for j in range(2)]
        for j, q in enumerate(GROUPS[i]):
            rows = pl.ds(pl.multiple_of(chunk_at(q) * CH, CH), CH)
            place = slice((GROUP * i + j) * CH, (GROUP * i + j + 1) * CH)
            acc = part[place, :]
            for l in range(BW // 128):
                value = kern[b, rows, l * 128:l * 128 + 128] * ws[l // 2][:, (l % 2) * 128:(l % 2) * 128 + 128]
                acc = acc + value
                w[j * CH:(j + 1) * CH, l * 128:(l + 1) * 128] = value.astype(BF16)
            part[place, :] = acc

    def multiply(w, i, b):
        e = emb[pl.ds(b * 8, 8)].reshape(BW, D)
        num[GROUP * i:GROUP * i + GROUP] += jnp.dot(w[...], e, preferred_element_type=F32).reshape(GROUP, CH, D)

    def group(i, start, stop):
        def two(k, _):
            weigh(w1, i, 2 * k + 1)
            multiply(w0, i, 2 * k)
            weigh(w0, i, 2 * k + 2)
            multiply(w1, i, 2 * k + 1)
            return 0

        lax.fori_loop(start, stop, two, 0)

    def group_end(i):
        weigh(w1, i, 7)
        multiply(w0, i, 6)
        if i + 1 < len(GROUPS):
            weigh(w0, i + 1, 0)
        multiply(w1, i, 7)

    rs = {}

    def hop(name, q, rows, before=None):
        sign = (1 if name[0] in ("RA", "RB") else -1)
        i = len(rs)
        value = num[POS[q], rows, :]
        if before is not None:
            rs[before].wait_recv()
            value = value + rcv[slot[before]].astype(F32)
        snd[i] = value.astype(BF16)
        slot[name] = i
        copy = pltpu.make_async_remote_copy(
            src_ref=snd.at[i], dst_ref=rcv.at[i], send_sem=rs_s.at[0], recv_sem=rs_r.at[i],
            device_id=at(dz=sign), device_id_type=MESH,
        )
        copy.start()
        rs[name] = copy

    slot = {}
    lo, hi = slice(0, 64), slice(64, 128)

    part[...] = jnp.zeros((C, 128), F32)
    weigh(w0, 0, 0)
    num[...] = jnp.zeros((NZ, CH, D), F32)
    group(0, 0, 1)
    landed(second)
    rw[1] = fac[1] / (TOTAL * summed(rl2[2, 1], rb.at[2, 1], 3))
    group(0, 1, 3)
    group_end(0)
    hop(("RB", 0), 4, lo)
    hop(("LB", 0), 4, hi)
    drain(sent)
    sent.clear()
    group(1, 0, 1)
    hop(("RA", 1), 3, hi)
    group(1, 1, 3)
    group_end(1)
    hop(("RB", 1), 3, lo, ("RB", 0))
    hop(("LA", 1), -3, lo)
    group(2, 0, 1)
    hop(("LB", 1), -3, hi, ("LB", 0))
    hop(("RA", 2), 2, hi, ("RA", 1))
    group(2, 1, 3)
    group_end(2)
    hop(("RB", 2), 2, lo, ("RB", 1))
    hop(("LA", 2), -2, lo, ("LA", 1))
    group(3, 0, 1)
    hop(("LB", 2), -2, hi, ("LB", 1))
    hop(("RA", 3), 1, hi, ("RA", 2))
    group(3, 1, 3)
    weigh(w1, 3, 7)
    for j, q in enumerate(q for g in GROUPS for q in g):
        for i in range(16):
            rows = slice(8 * i, 8 * i + 8)
            total = jnp.sum(part[j * CH + 8 * i:j * CH + 8 * i + 8, :], axis=1, keepdims=True)
            col[rows, :] = jnp.where(lane == chunk_at(q), total, col[rows, :])
    ml[2] = col[...].T[0:NZ, :]
    last = push(ml.at[2], mr.at[2], z_peers, m_s.at[2], m_r.at[2])
    multiply(w0, 3, 6)
    multiply(w1, 3, 7)
    hop(("RB", 3), 1, lo, ("RB", 2))
    hop(("LA", 3), -1, lo, ("LA", 2))
    hop(("LB", 3), -1, hi, ("LB", 2))
    drain(last[:1])
    whole(snd, rs_s.at[0], rs_r.at[0]).wait_send()

    landed(last)
    mass = ml[2, pl.ds(z, 1), :]
    for k in range(7):
        mass = mass + mr[2, k, pl.ds(z, 1), :]
    column = jnp.broadcast_to(mass, (CH, CH)).T
    column = jnp.concatenate([column] * (D // CH), axis=1)
    for rows, one, two in ((hi, ("RA", 3), ("LB", 3)), (lo, ("LA", 3), ("RB", 3))):
        rs[one].wait_recv()
        rs[two].wait_recv()
        total = num[POS[0], rows, :] + rcv[slot[one]].astype(F32) + rcv[slot[two]].astype(F32)
        out_ref[rows, :] = (total / column[rows, :]).astype(BF16)


def local(embeddings, centroids):
    e = embeddings.reshape(16, PIECE, D)
    k = centroids.reshape(NZ, NY, CH, D)
    dma = pltpu.SemaphoreType.DMA
    v = pltpu.VMEM
    out = pl.pallas_call(
        body,
        out_shape=jax.ShapeDtypeStruct((CH, D), BF16),
        in_specs=[pl.BlockSpec(memory_space=pl.ANY)] * 2,
        out_specs=pl.BlockSpec(memory_space=pltpu.VMEM),
        scratch_shapes=[
            v((64, PIECE, D), BF16), v((NZ, CH, D), BF16), v((NB, C, BW), F32), v((C, BW), F32), v((C, BW), F32),
            v((2, 8, 256), F32), v((3, 2, 8, 256), F32), v((3, 2, 8, 256), F32),
            v((3, 2, 7, 8, 256), F32), v((3, 2, 3, 8, 256), F32),
            v((2, 8, 256), F32), v((2, 8, 256), F32), v((C, 128), F32), v((C, 128), F32), v((CH, CH), F32),
            v((3, NZ, CH), F32), v((3, 7, NZ, CH), F32),
            v((GROUP * CH, BW), BF16), v((GROUP * CH, BW), BF16), v((NZ, CH, D), F32),
            v((14, 64, D), BF16), v((14, 64, D), BF16),
            dma((2,)), dma((1,)), dma((20,)), dma((3, 2)), dma((3, 2)), dma((3, 2)), dma((3, 2)),
            dma((3,)), dma((3,)), dma((1,)), dma((14,)),
        ],
        compiler_params=pltpu.CompilerParams(
            collective_id=0, has_side_effects=True, vmem_limit_bytes=60 * 1024 * 1024
        ),
        cost_estimate=pl.CostEstimate(
            flops=4 * C * NB * BW * D, bytes_accessed=8 * 1024 * 1024, transcendentals=C * NB * BW
        ),
    )(e, k)
    return out[None]


def solution(mesh):
    return jax.shard_map(
        local,
        mesh=mesh,
        in_specs=(P("docs", None), P("cent", None)),
        out_specs=P("cent", "docs", None),
        check_vma=False,
    )
```

```python
import jax
import jax.numpy as jnp
import numpy as np
from jax import lax
from jax.experimental import pallas as pl
from jax.experimental.pallas import tpu as pltpu
from jax.sharding import PartitionSpec as P

MESH = pl.DeviceIdType.MESH
F32 = jnp.float32
BF16 = jnp.bfloat16

NX, NY, NZ = 4, 4, 8
D = 768
PIECE = 64
NB, BW = 8, 512
CH = 128
C = NZ * CH
TOTAL = 32768.0
EXP2_SCALE = 10.0 * float(np.log2(np.e))

GROUPS = ((4, 3), (-3, 2), (-2, 1), (-1, 0))
GROUP = len(GROUPS[0])
POS = {q: i for i, q in enumerate(q for group in GROUPS for q in group)}
LN2 = float(np.log(2.0))


def body(
    emb_hbm, cen_hbm, out_ref,
    emb, cen, kern, buf0, buf1,
    top_of, rl, rl2, ra, rb, fac, rw, part, scol, col, ml, mr, w0, w1, num, snd, rcv,
    ld_sem, ag_s, ag_r, r1_s, r1_r, r2_s, r2_r, m_s, m_r, rs_s, rs_r,
):
    docs = lax.axis_index("docs")
    cent = lax.axis_index("cent")
    z, y = docs // NY, docs % NY
    x, c = cent // 2, cent % 2

    def at(dz=0, dy=0, dx=0, flip=False):
        zz = (z + dz + NZ) % NZ
        yy = (y + dy + NY) % NY
        xx = (x + dx + NX) % NX
        return (zz * NY + yy, xx * 2 + ((1 - c) if flip else c))

    load_e = pltpu.make_async_copy(emb_hbm, emb.at[pl.ds(y * 16, 16)], ld_sem.at[0])
    load_c = pltpu.make_async_copy(cen_hbm.at[:, y], cen, ld_sem.at[1])
    load_e.start()
    load_c.start()

    cent_peers = [(docs, (cent + k) % 8) for k in range(1, 8)]
    y_peers = [at(dy=k) for k in range(1, NY)]
    z_peers = [at(dz=k) for k in range(1, NZ)]
    barrier = pltpu.get_barrier_semaphore()
    for peer in cent_peers + y_peers + z_peers:
        pl.semaphore_signal(barrier, inc=1, device_id=peer, device_id_type=MESH)
    pl.semaphore_wait(barrier, len(cent_peers) + len(y_peers) + len(z_peers))

    def piece(dy, h, dx):
        return ((y + dy + NY) % NY) * 16 + h * 8 + ((x + dx + NX) % NX) * 2 + c

    ag = {}

    landing = {}

    def plan(name, where, target, together, src=None):
        ag[name] = pltpu.make_async_remote_copy(
            src_ref=emb.at[where] if src is None else src, dst_ref=emb.at[where], send_sem=ag_s.at[0],
            recv_sem=ag_r.at[landing.setdefault(together, len(landing))], device_id=target, device_id_type=MESH,
        )

    def plan_own(name, h, dx, s, together):
        plan(name, piece(0, h, dx), at(dy=s), together, emb_hbm.at[h * 8 + ((x + dx + NX) % NX) * 2 + c])

    plan_own(("f", 1), 1, 0, 1, "f")
    plan_own(("f", -1), 0, 0, -1, "f")
    plan_own(("g", 1), 0, 0, 1, "g")
    plan_own(("g", -1), 1, 0, -1, "g")
    plan(("y3", 1), piece(-1, 1, 0), at(dy=1), "y3")
    plan(("y3", -1), piece(1, 0, 0), at(dy=-1), "y3")
    for k in (1, 2, -1):
        for s in (1, -1):
            plan_own(("k", s, k), 0, k, s, ("k", k))
    for dy, h in ((-1, 1), (1, 1), (2, 0), (2, 1)):
        for s in (1, -1):
            key = ("x1", dy) if h == 1 and dy != 2 else ("x1", 2, (h == 0) == (s == 1))
            plan(("x1", s, dy, h), piece(dy, h, 0), at(dx=s), key)
    for s, dy, h in ((-1, -1, 1), (1, 1, 1), (1, 2, 0), (-1, 2, 1)):
        plan(("x2", s, dy, h), piece(dy, h, -s), at(dx=s), ("x2", dy))
    for dy in (-1, 1, 2):
        for h in (0, 1):
            for dx in (0, 1, 2, -1):
                plan(("s", dy, h, dx), piece(dy, h, dx), at(flip=True), ("s", dy, h))

    def whole(ref, ssem, rsem):
        return pltpu.make_async_remote_copy(
            src_ref=ref, dst_ref=ref, send_sem=ssem, recv_sem=rsem, device_id=at(flip=True), device_id_type=MESH
        )

    def send(*names):
        for name in names:
            ag[name].start()

    def got(together, n=2):
        whole(emb.at[pl.ds(0, n)], ag_s.at[0], ag_r.at[landing[together]]).wait_recv()

    def to_sibling(*pieces):
        send(*[("s", *p) for p in pieces])

    def block_ready(dy, h):
        got(("s", dy, h), 4)

    send(("f", 1), ("f", -1))
    load_e.wait()
    load_c.wait()

    def phase_a():
        send(("g", 1), ("g", -1))
        got("f")
        send(("y3", 1), ("y3", -1), ("x1", 1, -1, 1), ("x1", -1, -1, 1))
        to_sibling((-1, 1, 0), (1, 0, 0))

    def phase_c():
        got("g")
        send(("x1", 1, 1, 1), ("x1", -1, 1, 1), ("k", 1, 1), ("k", -1, 1))
        to_sibling((-1, 0, 0), (1, 1, 0))
        got(("x1", -1))
        send(("x2", -1, -1, 1))
        to_sibling((-1, 1, 1), (-1, 1, -1))
        got("y3")
        send(("x1", 1, 2, 0), ("x1", -1, 2, 1), ("k", 1, 2), ("k", -1, 2))
        to_sibling((2, 1, 0), (2, 0, 0))
        got(("x1", 1))
        send(("x2", 1, 1, 1), ("x1", 1, 2, 1), ("x1", -1, 2, 0), ("k", 1, -1), ("k", -1, -1))
        to_sibling((1, 1, -1), (1, 1, 1))
        got(("x2", -1), 1)
        to_sibling((-1, 1, 2))
        block_ready(-1, 1)

    def phase_f():
        for k in (1, 2):
            got(("k", k))
            to_sibling((1, 0, k), (-1, 0, k))
        got(("x1", 2, True))
        send(("x2", 1, 2, 0), ("x2", -1, 2, 1))
        to_sibling((2, 0, -1), (2, 1, 1))
        got(("x2", 1), 1)
        to_sibling((1, 1, 2))
        block_ready(1, 1)

    def phase_g():
        got(("k", -1))
        to_sibling((1, 0, -1), (-1, 0, -1))
        block_ready(-1, 0)

    def phase_h():
        got(("x1", 2, False))
        to_sibling((2, 1, -1), (2, 0, 1))
        block_ready(1, 0)

    def phase_i():
        got(("x2", 2))
        to_sibling((2, 0, 2), (2, 1, 2))
        block_ready(2, 0)

    def phase_j():
        block_ready(2, 1)

    sent = []

    def push(src, dst, peers, ssem, rsem, start=True):
        copies = [
            pltpu.make_async_remote_copy(
                src_ref=src, dst_ref=dst.at[k], send_sem=ssem, recv_sem=rsem, device_id=peer, device_id_type=MESH
            )
            for k, peer in enumerate(peers)
        ]
        if start:
            begin(copies)
        both = whole(dst, ssem, rsem)
        sent.append(both)
        return both, copies

    def begin(copies):
        for copy in copies:
            copy.start()

    def landed(pushed):
        pushed[0].wait_recv()

    def drain(wholes):
        for copy in wholes:
            copy.wait_send()

    def push_1(n, half, start=True):
        return push(rl.at[n, half], ra.at[n, half], cent_peers, r1_s.at[n, half], r1_r.at[n, half], start)

    def push_2(n, half):
        return push(rl2.at[n, half], rb.at[n, half], y_peers, r2_s.at[n, half], r2_r.at[n, half])

    def summed(own, others, n):
        total = own
        for k in range(n):
            total = total + others[k]
        return total

    def log_summed(own, others, n):
        top = own
        for k in range(n):
            top = jnp.maximum(top, others[k])
        total = jnp.exp2(own - top)
        for k in range(n):
            total = total + jnp.exp2(others[k] - top)
        return top + jnp.log(total) * (1.0 / LN2)

    def place_of(p, odd):
        d = (p + 1) // 2
        if odd:
            return ((y + d) % NY) * 2 + 1 - (1 - p % 2) * (p // 2)
        return ((y - d + NY) % NY) * 2 + (p % 2) * (1 - p // 2)

    def step(new_buf, new, old_buf, old, old_max, half, row):
        top = jnp.max(old_max, axis=0, keepdims=True)
        total = jnp.zeros((8, BW), F32)
        new_max = []
        if new is not None:
            e = emb[pl.ds(new * 8, 8)].reshape(BW, D)
        for i in range(4):
            if new is not None and i % 2 == 0:
                lanes = slice(128 * i, 128 * i + 256)
                raw = lax.dot_general(
                    cen[...].reshape(C, D), e[lanes, :], (((1,), (1,)), ((), ())), preferred_element_type=F32
                )
                new_buf[:, lanes] = raw
                new_max.append(jnp.max(raw.reshape(C // 8, 8, 256), axis=0))
            for k in range(4):
                rows = slice(256 * i + 64 * k, 256 * i + 64 * k + 64)
                value = jnp.exp2((old_buf[rows, :] - top) * EXP2_SCALE)
                kern[old, rows, :] = value
                total = total + jnp.sum(value.reshape(8, 8, BW), axis=0)
        if new is not None:
            new_max = jnp.concatenate(new_max, axis=1)
        scaled = top * EXP2_SCALE
        whole = scaled + jnp.log(jnp.sum(total, axis=0, keepdims=True)) * (1.0 / LN2)
        for j in range(2):
            lanes = slice(256 * j, 256 * j + 256)
            rl[0, half, pl.ds(row + j, 1), :] = whole[:, lanes]
            top_of[old // 4, pl.ds((old % 4) * 2 + j, 1), :] = scaled[:, lanes]
        return new_max

    first = push_1(0, 0, start=False)

    def two_steps(p, high):
        pl.when(p == 1)(phase_c)
        pl.when(p == 2)(phase_g)
        pl.when(p == 3)(phase_i)
        q = (p + 3) % 4
        high = step(buf0, place_of(p, False), buf1, place_of(q, True), high, q // 2, (q % 2) * 4 + 2)
        pl.when(p == 0)(phase_a)
        pl.when(p == 1)(phase_f)

        @pl.when(p == 2)
        def _():
            begin(first[1])
            phase_h()

        pl.when(p == 3)(phase_j)
        return step(buf1, place_of(p, True), buf0, place_of(p, False), high, p // 2, (p % 2) * 4)

    buf1[...] = jnp.zeros((C, BW), F32)
    with jax.named_scope("logits"):
        high = lax.fori_loop(0, 4, two_steps, jnp.zeros((8, BW), F32))
        step(None, None, buf1, place_of(3, True), high, 1, 6)
    second = push_1(0, 1)
    whole(emb.at[pl.ds(0, 48)], ag_s.at[0], ag_r.at[0]).wait_send()
    for half, copies in ((0, first), (1, second)):
        landed(copies)
        merged = log_summed(rl[0, half], ra.at[0, half], 7)
        for j in range(8):
            place = place_of(2 * half + j // 4, j // 2 % 2 == 1)
            rl2[0, place // 4, pl.ds((place % 4) * 2 + j % 2, 1), :] = merged[j:j + 1, :]
    first, second = push_2(0, 0), push_2(0, 1)

    def start_weights(half):
        whole = log_summed(rl2[0, half], rb.at[0, half], 3)
        factor = jnp.exp2(top_of[half] - whole)
        fac[half] = factor
        rw[half] = factor * (1.0 / TOTAL)

    landed(first)
    start_weights(0)

    lane = lax.broadcasted_iota(jnp.int32, (8, 128), 1)

    def mass_half(half):
        def chunk(t, _):
            def tile(i):
                return pl.ds(pl.multiple_of(t * CH + 8 * i, 8), 8)

            acc = [None if half == 0 else part[tile(i), :] for i in range(16)]
            for b in range(4 * half, 4 * half + 4):
                for l in range(4):
                    r = (b % 4) * 2 + l // 2
                    w = jnp.broadcast_to(rw[half, r:r + 1, (l % 2) * 128:(l % 2) * 128 + 128], (8, 128))
                    for i in range(16):
                        value = kern[b, tile(i), l * 128:l * 128 + 128] * w
                        acc[i] = value if acc[i] is None else acc[i] + value
            for i in range(16):
                if half == 0:
                    part[tile(i), :] = acc[i]
                else:
                    total = jnp.sum(acc[i], axis=1, keepdims=True)
                    rows = slice(8 * i, 8 * i + 8)
                    col[rows, :] = jnp.where(lane == t, total, col[rows, :])
            return 0

        lax.fori_loop(0, NZ, chunk, 0)

    def row_half(n, half):
        def chunk(t, acc):
            acc = list(acc)
            for i in range(16):
                tile = pl.ds(pl.multiple_of(t * CH + 8 * i, 8), 8)
                s = scol[tile, :]
                for b in range(4):
                    for l in range(4):
                        acc[4 * b + l] += kern[4 * half + b, tile, l * 128:l * 128 + 128] * s
            return tuple(acc)

        acc = lax.fori_loop(0, NZ, chunk, tuple(jnp.zeros((8, 128), F32) for _ in range(16)))
        for b in range(4):
            for l in range(4):
                r, lanes = b * 2 + l // 2, slice((l % 2) * 128, (l % 2) * 128 + 128)
                total = jnp.sum(acc[4 * b + l], axis=0, keepdims=True)
                rl[n, half, r:r + 1, lanes] = total * fac[half, r:r + 1, lanes]

    col[...] = jnp.zeros((CH, CH), F32)
    for n in range(2):
        with jax.named_scope("mass"):
            mass_half(0)
        landed(second)
        if n == 0:
            start_weights(1)
        else:
            rw[1] = fac[1] / (TOTAL * summed(rl2[n, 1], rb.at[n, 1], 3))
        with jax.named_scope("mass"):
            mass_half(1)
        ml[n] = col[...].T[0:NZ, :]
        before = sent[:]
        sent.clear()
        copies = push(ml.at[n], mr.at[n], z_peers, m_s.at[n], m_r.at[n])
        drain(before)
        landed(copies)
        scale = 1.0 / (TOTAL * summed(ml[n], mr.at[n], 7))
        columns = jnp.concatenate([scale, jnp.zeros((CH - NZ, CH), F32)], axis=0).T
        for t in range(NZ):
            scol[t * CH:(t + 1) * CH, :] = jnp.broadcast_to(columns[:, t:t + 1], (CH, CH))
        with jax.named_scope("rows"):
            row_half(n + 1, 0)
        first = push_1(n + 1, 0)
        with jax.named_scope("rows"):
            row_half(n + 1, 1)
        second = push_1(n + 1, 1)
        landed(first)
        rl2[n + 1, 0] = summed(rl[n + 1, 0], ra.at[n + 1, 0], 7)
        first = push_2(n + 1, 0)
        landed(second)
        rl2[n + 1, 1] = summed(rl[n + 1, 1], ra.at[n + 1, 1], 7)
        second = push_2(n + 1, 1)
        landed(first)
        rw[0] = fac[0] / (TOTAL * summed(rl2[n + 1, 0], rb.at[n + 1, 0], 3))

    def chunk_at(q):
        return (z + q + NZ) % NZ

    def weigh(w, i, b):
        ws = [rw[b // 4, pl.ds((b % 4) * 2 + j, 1), :] for j in range(2)]
        for j, q in enumerate(GROUPS[i]):
            rows = pl.ds(pl.multiple_of(chunk_at(q) * CH, CH), CH)
            place = slice((GROUP * i + j) * CH, (GROUP * i + j + 1) * CH)
            acc = part[place, :]
            for l in range(BW // 128):
                value = kern[b, rows, l * 128:l * 128 + 128] * ws[l // 2][:, (l % 2) * 128:(l % 2) * 128 + 128]
                acc = acc + value
                w[j * CH:(j + 1) * CH, l * 128:(l + 1) * 128] = value.astype(BF16)
            part[place, :] = acc

    def multiply(w, i, b):
        e = emb[pl.ds(b * 8, 8)].reshape(BW, D)
        num[GROUP * i:GROUP * i + GROUP] += jnp.dot(w[...], e, preferred_element_type=F32).reshape(GROUP, CH, D)

    def group(i, start, stop):
        def two(k, _):
            weigh(w1, i, 2 * k + 1)
            multiply(w0, i, 2 * k)
            weigh(w0, i, 2 * k + 2)
            multiply(w1, i, 2 * k + 1)
            return 0

        with jax.named_scope("numerators"):
            lax.fori_loop(start, stop, two, 0)

    def group_end(i):
        weigh(w1, i, 7)
        multiply(w0, i, 6)
        if i + 1 < len(GROUPS):
            weigh(w0, i + 1, 0)
        multiply(w1, i, 7)

    rs = {}

    def hop(name, q, rows, before=None):
        sign = 1 if name[0] in ("RA", "RB") else -1
        for part_of in range(2):
            i = len(rs)
            value = num[POS[q], rows.start + 32 * part_of:rows.start + 32 * part_of + 32, :]
            if before is not None:
                rs[(*before, part_of)].wait_recv()
                value = value + rcv[slot[(*before, part_of)]].astype(F32)
            snd[i] = value.astype(BF16)
            slot[(*name, part_of)] = i
            copy = pltpu.make_async_remote_copy(
                src_ref=snd.at[i], dst_ref=rcv.at[i], send_sem=rs_s.at[0], recv_sem=rs_r.at[i],
                device_id=at(dz=sign), device_id_type=MESH,
            )
            copy.start()
            rs[(*name, part_of)] = copy

    slot = {}
    lo, hi = slice(0, 64), slice(64, 128)

    part[...] = jnp.zeros((C, 128), F32)
    weigh(w0, 0, 0)
    num[...] = jnp.zeros((NZ, CH, D), F32)
    group(0, 0, 1)
    landed(second)
    rw[1] = fac[1] / (TOTAL * summed(rl2[2, 1], rb.at[2, 1], 3))
    group(0, 1, 3)
    group_end(0)
    hop(("RB", 0), 4, lo)
    hop(("LB", 0), 4, hi)
    drain(sent)
    sent.clear()
    group(1, 0, 1)
    hop(("RA", 1), 3, hi)
    group(1, 1, 3)
    group_end(1)
    hop(("RB", 1), 3, lo, ("RB", 0))
    hop(("LA", 1), -3, lo)
    group(2, 0, 1)
    hop(("LB", 1), -3, hi, ("LB", 0))
    hop(("RA", 2), 2, hi, ("RA", 1))
    group(2, 1, 3)
    group_end(2)
    hop(("RB", 2), 2, lo, ("RB", 1))
    hop(("LA", 2), -2, lo, ("LA", 1))
    group(3, 0, 1)
    hop(("LB", 2), -2, hi, ("LB", 1))
    hop(("RA", 3), 1, hi, ("RA", 2))
    group(3, 1, 3)
    weigh(w1, 3, 7)
    for j, q in enumerate(q for g in GROUPS for q in g):
        for i in range(16):
            rows = slice(8 * i, 8 * i + 8)
            total = jnp.sum(part[j * CH + 8 * i:j * CH + 8 * i + 8, :], axis=1, keepdims=True)
            col[rows, :] = jnp.where(lane == chunk_at(q), total, col[rows, :])
    ml[2] = col[...].T[0:NZ, :]
    last = push(ml.at[2], mr.at[2], z_peers, m_s.at[2], m_r.at[2])
    multiply(w0, 3, 6)
    multiply(w1, 3, 7)
    hop(("RB", 3), 1, lo, ("RB", 2))
    hop(("LA", 3), -1, lo, ("LA", 2))
    hop(("LB", 3), -1, hi, ("LB", 2))
    drain(last[:1])
    whole(snd, rs_s.at[0], rs_r.at[0]).wait_send()

    with jax.named_scope("last_hops"):
        landed(last)
        rs[("RB", 3, 0)].wait_recv()
    mass = ml[2, pl.ds(z, 1), :]
    for k in range(7):
        mass = mass + mr[2, k, pl.ds(z, 1), :]
    column = jnp.broadcast_to(mass, (CH, CH)).T
    column = jnp.concatenate([column] * (D // CH), axis=1)
    for start, one, two in ((64, ("RA", 3), ("LB", 3)), (0, ("LA", 3), ("RB", 3))):
        for part_of in range(2):
            rows = slice(start + 32 * part_of, start + 32 * part_of + 32)
            total = num[POS[0], rows, :]
            for name in (one, two):
                if (*name, part_of) != ("RB", 3, 0):
                    rs[(*name, part_of)].wait_recv()
                total = total + rcv[slot[(*name, part_of)]].astype(F32)
            out_ref[rows, :] = (total / column[rows, :]).astype(BF16)


def local(embeddings, centroids):
    e = embeddings.reshape(16, PIECE, D)
    k = centroids.reshape(NZ, NY, CH, D)
    dma = pltpu.SemaphoreType.DMA
    v = pltpu.VMEM
    out = pl.pallas_call(
        body,
        out_shape=jax.ShapeDtypeStruct((CH, D), BF16),
        in_specs=[pl.BlockSpec(memory_space=pl.ANY)] * 2,
        out_specs=pl.BlockSpec(memory_space=pltpu.VMEM),
        scratch_shapes=[
            v((64, PIECE, D), BF16), v((NZ, CH, D), BF16), v((NB, C, BW), F32), v((C, BW), F32), v((C, BW), F32),
            v((2, 8, 256), F32), v((3, 2, 8, 256), F32), v((3, 2, 8, 256), F32),
            v((3, 2, 7, 8, 256), F32), v((3, 2, 3, 8, 256), F32),
            v((2, 8, 256), F32), v((2, 8, 256), F32), v((C, 128), F32), v((C, 128), F32), v((CH, CH), F32),
            v((3, NZ, CH), F32), v((3, 7, NZ, CH), F32),
            v((GROUP * CH, BW), BF16), v((GROUP * CH, BW), BF16), v((NZ, CH, D), F32),
            v((28, 32, D), BF16), v((28, 32, D), BF16),
            dma((2,)), dma((1,)), dma((20,)), dma((3, 2)), dma((3, 2)), dma((3, 2)), dma((3, 2)),
            dma((3,)), dma((3,)), dma((1,)), dma((28,)),
        ],
        compiler_params=pltpu.CompilerParams(
            collective_id=0, has_side_effects=True, vmem_limit_bytes=60 * 1024 * 1024
        ),
        cost_estimate=pl.CostEstimate(
            flops=4 * C * NB * BW * D, bytes_accessed=8 * 1024 * 1024, transcendentals=C * NB * BW
        ),
    )(e, k)
    return out[None]


def solution(mesh):
    return jax.shard_map(
        local,
        mesh=mesh,
        in_specs=(P("docs", None), P("cent", None)),
        out_specs=P("cent", "docs", None),
        check_vma=False,
    )
```

```python
import jax
import jax.numpy as jnp
import numpy as np
from jax import lax
from jax.experimental import pallas as pl
from jax.experimental.pallas import tpu as pltpu
from jax.sharding import PartitionSpec as P

MESH = pl.DeviceIdType.MESH
F32 = jnp.float32
BF16 = jnp.bfloat16

NX, NY, NZ = 4, 4, 8
D = 768
PIECE = 64
NB, BW = 8, 512
CH = 128
C = NZ * CH
TOTAL = 32768.0
EXP2_SCALE = 10.0 * float(np.log2(np.e))

GROUPS = ((4,), (3, -3), (2, -2), (1, -1), (0,))
GROUP = 2
POS = {q: i for i, q in enumerate(q for group in GROUPS for q in group)}
LN2 = float(np.log(2.0))


def body(
    emb_hbm, cen_hbm, out_ref,
    emb, cen, kern, buf0, buf1,
    top_of, rl, rl2, ra, rb, fac, rw, part, scol, col, ml, mr, w0, w1, num, snd, rcv,
    ld_sem, ag_s, ag_r, r1_s, r1_r, r2_s, r2_r, m_s, m_r, rs_s, rs_r,
):
    docs = lax.axis_index("docs")
    cent = lax.axis_index("cent")
    z, y = docs // NY, docs % NY
    x, c = cent // 2, cent % 2

    def at(dz=0, dy=0, dx=0, flip=False):
        zz = (z + dz + NZ) % NZ
        yy = (y + dy + NY) % NY
        xx = (x + dx + NX) % NX
        return (zz * NY + yy, xx * 2 + ((1 - c) if flip else c))

    load_e = pltpu.make_async_copy(emb_hbm, emb.at[pl.ds(y * 16, 16)], ld_sem.at[0])
    load_c = pltpu.make_async_copy(cen_hbm.at[:, y], cen, ld_sem.at[1])
    load_e.start()
    load_c.start()

    cent_peers = [(docs, (cent + k) % 8) for k in range(1, 8)]
    y_peers = [at(dy=k) for k in range(1, NY)]
    z_peers = [at(dz=k) for k in range(1, NZ)]
    barrier = pltpu.get_barrier_semaphore()
    for peer in cent_peers + y_peers + z_peers:
        pl.semaphore_signal(barrier, inc=1, device_id=peer, device_id_type=MESH)
    pl.semaphore_wait(barrier, len(cent_peers) + len(y_peers) + len(z_peers))

    def piece(dy, h, dx):
        return ((y + dy + NY) % NY) * 16 + h * 8 + ((x + dx + NX) % NX) * 2 + c

    ag = {}

    landing = {}

    def plan(name, where, target, together, src=None):
        ag[name] = pltpu.make_async_remote_copy(
            src_ref=emb.at[where] if src is None else src, dst_ref=emb.at[where], send_sem=ag_s.at[0],
            recv_sem=ag_r.at[landing.setdefault(together, len(landing))], device_id=target, device_id_type=MESH,
        )

    def plan_own(name, h, dx, s, together):
        plan(name, piece(0, h, dx), at(dy=s), together, emb_hbm.at[h * 8 + ((x + dx + NX) % NX) * 2 + c])

    plan_own(("f", 1), 1, 0, 1, "f")
    plan_own(("f", -1), 0, 0, -1, "f")
    plan_own(("g", 1), 0, 0, 1, "g")
    plan_own(("g", -1), 1, 0, -1, "g")
    plan(("y3", 1), piece(-1, 1, 0), at(dy=1), "y3")
    plan(("y3", -1), piece(1, 0, 0), at(dy=-1), "y3")
    for k in (1, 2, -1):
        for s in (1, -1):
            plan_own(("k", s, k), 0, k, s, ("k", k))
    for dy, h in ((-1, 1), (1, 1), (2, 0), (2, 1)):
        for s in (1, -1):
            key = ("x1", dy) if h == 1 and dy != 2 else ("x1", 2, (h == 0) == (s == 1))
            plan(("x1", s, dy, h), piece(dy, h, 0), at(dx=s), key)
    for s, dy, h in ((-1, -1, 1), (1, 1, 1), (1, 2, 0), (-1, 2, 1)):
        plan(("x2", s, dy, h), piece(dy, h, -s), at(dx=s), ("x2", dy))
    for dy in (-1, 1, 2):
        for h in (0, 1):
            for dx in (0, 1, 2, -1):
                plan(("s", dy, h, dx), piece(dy, h, dx), at(flip=True), ("s", dy, h))

    def whole(ref, ssem, rsem):
        return pltpu.make_async_remote_copy(
            src_ref=ref, dst_ref=ref, send_sem=ssem, recv_sem=rsem, device_id=at(flip=True), device_id_type=MESH
        )

    def send(*names):
        for name in names:
            ag[name].start()

    def got(together, n=2):
        whole(emb.at[pl.ds(0, n)], ag_s.at[0], ag_r.at[landing[together]]).wait_recv()

    def to_sibling(*pieces):
        send(*[("s", *p) for p in pieces])

    def block_ready(dy, h):
        got(("s", dy, h), 4)

    send(("f", 1), ("f", -1))
    load_e.wait()
    load_c.wait()

    def phase_a():
        send(("g", 1), ("g", -1))
        got("f")
        send(("y3", 1), ("y3", -1), ("x1", 1, -1, 1), ("x1", -1, -1, 1))
        to_sibling((-1, 1, 0), (1, 0, 0))

    def phase_c():
        got("g")
        send(("x1", 1, 1, 1), ("x1", -1, 1, 1), ("k", 1, 1), ("k", -1, 1))
        to_sibling((-1, 0, 0), (1, 1, 0))
        got(("x1", -1))
        send(("x2", -1, -1, 1))
        to_sibling((-1, 1, 1), (-1, 1, -1))
        got("y3")
        send(("x1", 1, 2, 0), ("x1", -1, 2, 1), ("k", 1, 2), ("k", -1, 2))
        to_sibling((2, 1, 0), (2, 0, 0))
        got(("x1", 1))
        send(("x2", 1, 1, 1), ("x1", 1, 2, 1), ("x1", -1, 2, 0), ("k", 1, -1), ("k", -1, -1))
        to_sibling((1, 1, -1), (1, 1, 1))
        got(("x2", -1), 1)
        to_sibling((-1, 1, 2))
        block_ready(-1, 1)

    def phase_f():
        for k in (1, 2):
            got(("k", k))
            to_sibling((1, 0, k), (-1, 0, k))
        got(("x1", 2, True))
        send(("x2", 1, 2, 0), ("x2", -1, 2, 1))
        to_sibling((2, 0, -1), (2, 1, 1))
        got(("x2", 1), 1)
        to_sibling((1, 1, 2))
        block_ready(1, 1)

    def phase_g():
        got(("k", -1))
        to_sibling((1, 0, -1), (-1, 0, -1))
        block_ready(-1, 0)

    def phase_h():
        got(("x1", 2, False))
        to_sibling((2, 1, -1), (2, 0, 1))
        block_ready(1, 0)

    def phase_i():
        got(("x2", 2))
        to_sibling((2, 0, 2), (2, 1, 2))
        block_ready(2, 0)

    def phase_j():
        block_ready(2, 1)

    sent = []

    def push(src, dst, peers, ssem, rsem, start=True):
        copies = [
            pltpu.make_async_remote_copy(
                src_ref=src, dst_ref=dst.at[k], send_sem=ssem, recv_sem=rsem, device_id=peer, device_id_type=MESH
            )
            for k, peer in enumerate(peers)
        ]
        if start:
            begin(copies)
        both = whole(dst, ssem, rsem)
        sent.append(both)
        return both, copies

    def begin(copies):
        for copy in copies:
            copy.start()

    def landed(pushed):
        pushed[0].wait_recv()

    def drain(wholes):
        for copy in wholes:
            copy.wait_send()

    def push_1(n, half, start=True):
        return push(rl.at[n, half], ra.at[n, half], cent_peers, r1_s.at[n, half], r1_r.at[n, half], start)

    def push_2(n, half):
        return push(rl2.at[n, half], rb.at[n, half], y_peers, r2_s.at[n, half], r2_r.at[n, half])

    def summed(own, others, n):
        total = own
        for k in range(n):
            total = total + others[k]
        return total

    def log_summed(own, others, n):
        top = own
        for k in range(n):
            top = jnp.maximum(top, others[k])
        total = jnp.exp2(own - top)
        for k in range(n):
            total = total + jnp.exp2(others[k] - top)
        return top + jnp.log(total) * (1.0 / LN2)

    def place_of(p, odd):
        d = (p + 1) // 2
        if odd:
            return ((y + d) % NY) * 2 + 1 - (1 - p % 2) * (p // 2)
        return ((y - d + NY) % NY) * 2 + (p % 2) * (1 - p // 2)

    def step(new_buf, new, old_buf, old, old_max, half, row):
        top = jnp.max(old_max, axis=0, keepdims=True)
        total = jnp.zeros((8, BW), F32)
        new_max = []
        if new is not None:
            e = emb[pl.ds(new * 8, 8)].reshape(BW, D)
        for i in range(4):
            if new is not None and i % 2 == 0:
                lanes = slice(128 * i, 128 * i + 256)
                raw = lax.dot_general(
                    cen[...].reshape(C, D), e[lanes, :], (((1,), (1,)), ((), ())), preferred_element_type=F32
                )
                new_buf[:, lanes] = raw
                new_max.append(jnp.max(raw.reshape(C // 8, 8, 256), axis=0))
            for k in range(4):
                rows = slice(256 * i + 64 * k, 256 * i + 64 * k + 64)
                value = jnp.exp2((old_buf[rows, :] - top) * EXP2_SCALE)
                kern[old, rows, :] = value
                total = total + jnp.sum(value.reshape(8, 8, BW), axis=0)
        if new is not None:
            new_max = jnp.concatenate(new_max, axis=1)
        scaled = top * EXP2_SCALE
        whole = scaled + jnp.log(jnp.sum(total, axis=0, keepdims=True)) * (1.0 / LN2)
        for j in range(2):
            lanes = slice(256 * j, 256 * j + 256)
            rl[0, half, pl.ds(row + j, 1), :] = whole[:, lanes]
            top_of[old // 4, pl.ds((old % 4) * 2 + j, 1), :] = scaled[:, lanes]
        return new_max

    first = push_1(0, 0, start=False)

    def two_steps(p, high):
        pl.when(p == 1)(phase_c)
        pl.when(p == 2)(phase_g)
        pl.when(p == 3)(phase_i)
        q = (p + 3) % 4
        high = step(buf0, place_of(p, False), buf1, place_of(q, True), high, q // 2, (q % 2) * 4 + 2)
        pl.when(p == 0)(phase_a)
        pl.when(p == 1)(phase_f)

        @pl.when(p == 2)
        def _():
            begin(first[1])
            phase_h()

        pl.when(p == 3)(phase_j)
        return step(buf1, place_of(p, True), buf0, place_of(p, False), high, p // 2, (p % 2) * 4)

    buf1[...] = jnp.zeros((C, BW), F32)
    with jax.named_scope("logits"):
        high = lax.fori_loop(0, 4, two_steps, jnp.zeros((8, BW), F32))
        step(None, None, buf1, place_of(3, True), high, 1, 6)
    second = push_1(0, 1)
    whole(emb.at[pl.ds(0, 48)], ag_s.at[0], ag_r.at[0]).wait_send()
    for half, copies in ((0, first), (1, second)):
        landed(copies)
        merged = log_summed(rl[0, half], ra.at[0, half], 7)
        for j in range(8):
            place = place_of(2 * half + j // 4, j // 2 % 2 == 1)
            rl2[0, place // 4, pl.ds((place % 4) * 2 + j % 2, 1), :] = merged[j:j + 1, :]
    first, second = push_2(0, 0), push_2(0, 1)

    def start_weights(half):
        whole = log_summed(rl2[0, half], rb.at[0, half], 3)
        factor = jnp.exp2(top_of[half] - whole)
        fac[half] = factor
        rw[half] = factor * (1.0 / TOTAL)

    landed(first)
    start_weights(0)

    lane = lax.broadcasted_iota(jnp.int32, (8, 128), 1)

    def mass_half(half):
        def chunk(t, _):
            def tile(i):
                return pl.ds(pl.multiple_of(t * CH + 8 * i, 8), 8)

            acc = [None if half == 0 else part[tile(i), :] for i in range(16)]
            for b in range(4 * half, 4 * half + 4):
                for l in range(4):
                    r = (b % 4) * 2 + l // 2
                    w = jnp.broadcast_to(rw[half, r:r + 1, (l % 2) * 128:(l % 2) * 128 + 128], (8, 128))
                    for i in range(16):
                        value = kern[b, tile(i), l * 128:l * 128 + 128] * w
                        acc[i] = value if acc[i] is None else acc[i] + value
            for i in range(16):
                if half == 0:
                    part[tile(i), :] = acc[i]
                else:
                    total = jnp.sum(acc[i], axis=1, keepdims=True)
                    rows = slice(8 * i, 8 * i + 8)
                    col[rows, :] = jnp.where(lane == t, total, col[rows, :])
            return 0

        lax.fori_loop(0, NZ, chunk, 0)

    def row_half(n, half):
        def chunk(t, acc):
            acc = list(acc)
            for i in range(16):
                tile = pl.ds(pl.multiple_of(t * CH + 8 * i, 8), 8)
                s = scol[tile, :]
                for b in range(4):
                    for l in range(4):
                        acc[4 * b + l] += kern[4 * half + b, tile, l * 128:l * 128 + 128] * s
            return tuple(acc)

        acc = lax.fori_loop(0, NZ, chunk, tuple(jnp.zeros((8, 128), F32) for _ in range(16)))
        for b in range(4):
            for l in range(4):
                r, lanes = b * 2 + l // 2, slice((l % 2) * 128, (l % 2) * 128 + 128)
                total = jnp.sum(acc[4 * b + l], axis=0, keepdims=True)
                rl[n, half, r:r + 1, lanes] = total * fac[half, r:r + 1, lanes]

    col[...] = jnp.zeros((CH, CH), F32)
    for n in range(2):
        with jax.named_scope("mass"):
            mass_half(0)
        landed(second)
        if n == 0:
            start_weights(1)
        else:
            rw[1] = fac[1] / (TOTAL * summed(rl2[n, 1], rb.at[n, 1], 3))
        with jax.named_scope("mass"):
            mass_half(1)
        ml[n] = col[...].T[0:NZ, :]
        before = sent[:]
        sent.clear()
        copies = push(ml.at[n], mr.at[n], z_peers, m_s.at[n], m_r.at[n])
        drain(before)
        landed(copies)
        scale = 1.0 / (TOTAL * summed(ml[n], mr.at[n], 7))
        columns = jnp.concatenate([scale, jnp.zeros((CH - NZ, CH), F32)], axis=0).T
        for t in range(NZ):
            scol[t * CH:(t + 1) * CH, :] = jnp.broadcast_to(columns[:, t:t + 1], (CH, CH))
        with jax.named_scope("rows"):
            row_half(n + 1, 0)
        first = push_1(n + 1, 0)
        with jax.named_scope("rows"):
            row_half(n + 1, 1)
        second = push_1(n + 1, 1)
        landed(first)
        rl2[n + 1, 0] = summed(rl[n + 1, 0], ra.at[n + 1, 0], 7)
        first = push_2(n + 1, 0)
        landed(second)
        rl2[n + 1, 1] = summed(rl[n + 1, 1], ra.at[n + 1, 1], 7)
        second = push_2(n + 1, 1)
        landed(first)
        rw[0] = fac[0] / (TOTAL * summed(rl2[n + 1, 0], rb.at[n + 1, 0], 3))

    def chunk_at(q):
        return (z + q + NZ) % NZ

    def weigh(w, i, b):
        ws = [rw[b // 4, pl.ds((b % 4) * 2 + j, 1), :] for j in range(2)]
        for j, q in enumerate(GROUPS[i]):
            rows = pl.ds(pl.multiple_of(chunk_at(q) * CH, CH), CH)
            place = slice(POS[q] * CH, (POS[q] + 1) * CH)
            acc = part[place, :]
            for l in range(BW // 128):
                value = kern[b, rows, l * 128:l * 128 + 128] * ws[l // 2][:, (l % 2) * 128:(l % 2) * 128 + 128]
                acc = acc + value
                w[j * CH:(j + 1) * CH, l * 128:(l + 1) * 128] = value.astype(BF16)
            part[place, :] = acc

    def multiply(w, i, b):
        e = emb[pl.ds(b * 8, 8)].reshape(BW, D)
        n, first = len(GROUPS[i]), POS[GROUPS[i][0]]
        num[first:first + n] += jnp.dot(w[0:n * CH, :], e, preferred_element_type=F32).reshape(n, CH, D)

    def group(i, start, stop):
        def two(k, _):
            weigh(w1, i, 2 * k + 1)
            multiply(w0, i, 2 * k)
            weigh(w0, i, 2 * k + 2)
            multiply(w1, i, 2 * k + 1)
            return 0

        with jax.named_scope("numerators"):
            lax.fori_loop(start, stop, two, 0)

    def group_end(i):
        weigh(w1, i, 7)
        multiply(w0, i, 6)
        if i + 1 < len(GROUPS):
            weigh(w0, i + 1, 0)
        multiply(w1, i, 7)

    rs = {}

    def hop(name, q, rows, before=None):
        sign = 1 if name[0] in ("RA", "RB") else -1
        for part_of in range(2):
            i = len(rs)
            value = num[POS[q], rows.start + 32 * part_of:rows.start + 32 * part_of + 32, :]
            if before is not None:
                rs[(*before, part_of)].wait_recv()
                value = value + rcv[slot[(*before, part_of)]].astype(F32)
            snd[i] = value.astype(BF16)
            slot[(*name, part_of)] = i
            copy = pltpu.make_async_remote_copy(
                src_ref=snd.at[i], dst_ref=rcv.at[i], send_sem=rs_s.at[0], recv_sem=rs_r.at[i],
                device_id=at(dz=sign), device_id_type=MESH,
            )
            copy.start()
            rs[(*name, part_of)] = copy

    slot = {}
    lo, hi = slice(0, 64), slice(64, 128)

    part[...] = jnp.zeros((C, 128), F32)
    weigh(w0, 0, 0)
    num[...] = jnp.zeros((NZ, CH, D), F32)
    group(0, 0, 1)
    landed(second)
    rw[1] = fac[1] / (TOTAL * summed(rl2[2, 1], rb.at[2, 1], 3))
    group(0, 1, 3)
    group_end(0)
    hop(("RB", 0), 4, lo)
    hop(("LB", 0), 4, hi)
    drain(sent)
    sent.clear()
    group(1, 0, 3)
    group_end(1)
    hop(("RA", 1), 3, hi)
    hop(("LA", 1), -3, lo)
    group(2, 0, 1)
    hop(("RB", 1), 3, lo, ("RB", 0))
    hop(("LB", 1), -3, hi, ("LB", 0))
    group(2, 1, 3)
    group_end(2)
    hop(("RA", 2), 2, hi, ("RA", 1))
    hop(("LA", 2), -2, lo, ("LA", 1))
    group(3, 0, 2)
    hop(("RB", 2), 2, lo, ("RB", 1))
    hop(("LB", 2), -2, hi, ("LB", 1))
    group(3, 2, 3)
    group_end(3)
    hop(("RA", 3), 1, hi, ("RA", 2))
    hop(("LA", 3), -1, lo, ("LA", 2))
    group(4, 0, 3)
    weigh(w1, 4, 7)
    for j, q in enumerate(q for g in GROUPS for q in g):
        for i in range(16):
            rows = slice(8 * i, 8 * i + 8)
            total = jnp.sum(part[j * CH + 8 * i:j * CH + 8 * i + 8, :], axis=1, keepdims=True)
            col[rows, :] = jnp.where(lane == chunk_at(q), total, col[rows, :])
    ml[2] = col[...].T[0:NZ, :]
    last = push(ml.at[2], mr.at[2], z_peers, m_s.at[2], m_r.at[2])
    multiply(w0, 4, 6)
    multiply(w1, 4, 7)
    hop(("RB", 3), 1, lo, ("RB", 2))
    hop(("LB", 3), -1, hi, ("LB", 2))
    drain(last[:1])
    whole(snd, rs_s.at[0], rs_r.at[0]).wait_send()

    with jax.named_scope("last_hops"):
        landed(last)
        rs[("RB", 3, 0)].wait_recv()
    mass = ml[2, pl.ds(z, 1), :]
    for k in range(7):
        mass = mass + mr[2, k, pl.ds(z, 1), :]
    column = jnp.broadcast_to(mass, (CH, CH)).T
    column = jnp.concatenate([column] * (D // CH), axis=1)
    for start, one, two in ((64, ("RA", 3), ("LB", 3)), (0, ("LA", 3), ("RB", 3))):
        for part_of in range(2):
            rows = slice(start + 32 * part_of, start + 32 * part_of + 32)
            total = num[POS[0], rows, :]
            for name in (one, two):
                if (*name, part_of) != ("RB", 3, 0):
                    rs[(*name, part_of)].wait_recv()
                total = total + rcv[slot[(*name, part_of)]].astype(F32)
            out_ref[rows, :] = (total / column[rows, :]).astype(BF16)


def local(embeddings, centroids):
    e = embeddings.reshape(16, PIECE, D)
    k = centroids.reshape(NZ, NY, CH, D)
    dma = pltpu.SemaphoreType.DMA
    v = pltpu.VMEM
    out = pl.pallas_call(
        body,
        out_shape=jax.ShapeDtypeStruct((CH, D), BF16),
        in_specs=[pl.BlockSpec(memory_space=pl.ANY)] * 2,
        out_specs=pl.BlockSpec(memory_space=pltpu.VMEM),
        scratch_shapes=[
            v((64, PIECE, D), BF16), v((NZ, CH, D), BF16), v((NB, C, BW), F32), v((C, BW), F32), v((C, BW), F32),
            v((2, 8, 256), F32), v((3, 2, 8, 256), F32), v((3, 2, 8, 256), F32),
            v((3, 2, 7, 8, 256), F32), v((3, 2, 3, 8, 256), F32),
            v((2, 8, 256), F32), v((2, 8, 256), F32), v((C, 128), F32), v((C, 128), F32), v((CH, CH), F32),
            v((3, NZ, CH), F32), v((3, 7, NZ, CH), F32),
            v((GROUP * CH, BW), BF16), v((GROUP * CH, BW), BF16), v((NZ, CH, D), F32),
            v((28, 32, D), BF16), v((28, 32, D), BF16),
            dma((2,)), dma((1,)), dma((20,)), dma((3, 2)), dma((3, 2)), dma((3, 2)), dma((3, 2)),
            dma((3,)), dma((3,)), dma((1,)), dma((28,)),
        ],
        compiler_params=pltpu.CompilerParams(
            collective_id=0, has_side_effects=True, vmem_limit_bytes=60 * 1024 * 1024
        ),
        cost_estimate=pl.CostEstimate(
            flops=4 * C * NB * BW * D, bytes_accessed=8 * 1024 * 1024, transcendentals=C * NB * BW
        ),
    )(e, k)
    return out[None]


def solution(mesh):
    return jax.shard_map(
        local,
        mesh=mesh,
        in_specs=(P("docs", None), P("cent", None)),
        out_specs=P("cent", "docs", None),
        check_vma=False,
    )
```

```python
import jax
import jax.numpy as jnp
import numpy as np
from jax import lax
from jax.experimental import pallas as pl
from jax.experimental.pallas import tpu as pltpu
from jax.sharding import PartitionSpec as P

MESH = pl.DeviceIdType.MESH
F32 = jnp.float32
BF16 = jnp.bfloat16

NX, NY, NZ = 4, 4, 8
D = 768
PIECE = 64
NB, BW = 8, 512
CH = 128
C = NZ * CH
TOTAL = 32768.0
EXP2_SCALE = 10.0 * float(np.log2(np.e))

GROUPS = ((4,), (3, -3), (2, -2), (1, -1), (0,))
GROUP = 2
POS = {q: i for i, q in enumerate(q for group in GROUPS for q in group)}
LN2 = float(np.log(2.0))


def body(
    emb_hbm, cen_hbm, out_ref,
    emb, cen, kern, buf0, buf1,
    top_of, rl, rl2, ra, rb, fac, rw, part, scol, col, ml, mr, w0, w1, num, snd, rcv,
    ld_sem, ag_s, ag_r, r1_s, r1_r, r2_s, r2_r, m_s, m_r, rs_s, rs_r,
):
    docs = lax.axis_index("docs")
    cent = lax.axis_index("cent")
    z, y = docs // NY, docs % NY
    x, c = cent // 2, cent % 2

    def at(dz=0, dy=0, dx=0, flip=False):
        zz = (z + dz + NZ) % NZ
        yy = (y + dy + NY) % NY
        xx = (x + dx + NX) % NX
        return (zz * NY + yy, xx * 2 + ((1 - c) if flip else c))

    load_e = pltpu.make_async_copy(emb_hbm, emb.at[pl.ds(y * 16, 16)], ld_sem.at[0])
    load_c = pltpu.make_async_copy(cen_hbm.at[:, y], cen, ld_sem.at[1])
    load_e.start()
    load_c.start()

    cent_peers = [(docs, (cent + k) % 8) for k in range(1, 8)]
    y_peers = [at(dy=k) for k in range(1, NY)]
    z_peers = [at(dz=k) for k in range(1, NZ)]
    barrier = pltpu.get_barrier_semaphore()
    for peer in cent_peers + y_peers + z_peers:
        pl.semaphore_signal(barrier, inc=1, device_id=peer, device_id_type=MESH)
    pl.semaphore_wait(barrier, len(cent_peers) + len(y_peers) + len(z_peers))

    def piece(dy, h, dx):
        return ((y + dy + NY) % NY) * 16 + h * 8 + ((x + dx + NX) % NX) * 2 + c

    ag = {}

    landing = {}

    def plan(name, where, target, together, src=None):
        ag[name] = pltpu.make_async_remote_copy(
            src_ref=emb.at[where] if src is None else src, dst_ref=emb.at[where], send_sem=ag_s.at[0],
            recv_sem=ag_r.at[landing.setdefault(together, len(landing))], device_id=target, device_id_type=MESH,
        )

    def plan_own(name, h, dx, s, together):
        plan(name, piece(0, h, dx), at(dy=s), together, emb_hbm.at[h * 8 + ((x + dx + NX) % NX) * 2 + c])

    plan_own(("f", 1), 1, 0, 1, "f")
    plan_own(("f", -1), 0, 0, -1, "f")
    plan_own(("g", 1), 0, 0, 1, "g")
    plan_own(("g", -1), 1, 0, -1, "g")
    plan(("y3", 1), piece(-1, 1, 0), at(dy=1), "y3")
    plan(("y3", -1), piece(1, 0, 0), at(dy=-1), "y3")
    for k in (1, 2, -1):
        for s in (1, -1):
            plan_own(("k", s, k), 0, k, s, ("k", k))
    for dy, h in ((-1, 1), (1, 1), (2, 0), (2, 1)):
        for s in (1, -1):
            key = ("x1", dy) if h == 1 and dy != 2 else ("x1", 2, (h == 0) == (s == 1))
            plan(("x1", s, dy, h), piece(dy, h, 0), at(dx=s), key)
    for s, dy, h in ((-1, -1, 1), (1, 1, 1), (1, 2, 0), (-1, 2, 1)):
        plan(("x2", s, dy, h), piece(dy, h, -s), at(dx=s), ("x2", dy))
    for dy in (-1, 1, 2):
        for h in (0, 1):
            for dx in (0, 1, 2, -1):
                plan(("s", dy, h, dx), piece(dy, h, dx), at(flip=True), ("s", dy, h))

    def whole(ref, ssem, rsem):
        return pltpu.make_async_remote_copy(
            src_ref=ref, dst_ref=ref, send_sem=ssem, recv_sem=rsem, device_id=at(flip=True), device_id_type=MESH
        )

    def send(*names):
        for name in names:
            ag[name].start()

    def got(together, n=2):
        whole(emb.at[pl.ds(0, n)], ag_s.at[0], ag_r.at[landing[together]]).wait_recv()

    def to_sibling(*pieces):
        send(*[("s", *p) for p in pieces])

    def block_ready(dy, h):
        got(("s", dy, h), 4)

    send(("f", 1), ("f", -1))
    buf1[...] = jnp.zeros((C, BW), F32)
    load_e.wait()
    load_c.wait()

    def phase_a():
        send(("g", 1), ("g", -1))
        got("f")
        send(("y3", 1), ("y3", -1), ("x1", 1, -1, 1), ("x1", -1, -1, 1))
        to_sibling((-1, 1, 0), (1, 0, 0))

    def phase_c():
        got("g")
        send(("x1", 1, 1, 1), ("x1", -1, 1, 1), ("k", 1, 1), ("k", -1, 1))
        to_sibling((-1, 0, 0), (1, 1, 0))
        got(("x1", -1))
        send(("x2", -1, -1, 1))
        to_sibling((-1, 1, 1), (-1, 1, -1))
        got("y3")
        send(("x1", 1, 2, 0), ("x1", -1, 2, 1), ("k", 1, 2), ("k", -1, 2))
        to_sibling((2, 1, 0), (2, 0, 0))
        got(("x1", 1))
        send(("x2", 1, 1, 1), ("x1", 1, 2, 1), ("x1", -1, 2, 0), ("k", 1, -1), ("k", -1, -1))
        to_sibling((1, 1, -1), (1, 1, 1))
        got(("x2", -1), 1)
        to_sibling((-1, 1, 2))
        block_ready(-1, 1)

    def phase_f():
        for k in (1, 2):
            got(("k", k))
            to_sibling((1, 0, k), (-1, 0, k))
        got(("x1", 2, True))
        send(("x2", 1, 2, 0), ("x2", -1, 2, 1))
        to_sibling((2, 0, -1), (2, 1, 1))
        got(("x2", 1), 1)
        to_sibling((1, 1, 2))
        block_ready(1, 1)

    def phase_g():
        got(("k", -1))
        to_sibling((1, 0, -1), (-1, 0, -1))
        block_ready(-1, 0)

    def phase_h():
        got(("x1", 2, False))
        to_sibling((2, 1, -1), (2, 0, 1))
        block_ready(1, 0)

    def phase_i():
        got(("x2", 2))
        to_sibling((2, 0, 2), (2, 1, 2))
        block_ready(2, 0)

    def phase_j():
        block_ready(2, 1)

    sent = []

    def push(src, dst, peers, ssem, rsem, start=True):
        copies = [
            pltpu.make_async_remote_copy(
                src_ref=src, dst_ref=dst.at[k], send_sem=ssem, recv_sem=rsem, device_id=peer, device_id_type=MESH
            )
            for k, peer in enumerate(peers)
        ]
        if start:
            begin(copies)
        both = whole(dst, ssem, rsem)
        sent.append(both)
        return both, copies

    def begin(copies):
        for copy in copies:
            copy.start()

    def landed(pushed):
        pushed[0].wait_recv()

    def drain(wholes):
        for copy in wholes:
            copy.wait_send()

    def push_1(n, half, start=True):
        return push(rl.at[n, half], ra.at[n, half], cent_peers, r1_s.at[n, half], r1_r.at[n, half], start)

    def push_2(n, half):
        return push(rl2.at[n, half], rb.at[n, half], y_peers, r2_s.at[n, half], r2_r.at[n, half])

    def summed(own, others, n):
        total = own
        for k in range(n):
            total = total + others[k]
        return total

    def log_summed(own, others, n):
        top = own
        for k in range(n):
            top = jnp.maximum(top, others[k])
        total = jnp.exp2(own - top)
        for k in range(n):
            total = total + jnp.exp2(others[k] - top)
        return top + jnp.log(total) * (1.0 / LN2)

    def place_of(p, odd):
        d = (p + 1) // 2
        if odd:
            return ((y + d) % NY) * 2 + 1 - (1 - p % 2) * (p // 2)
        return ((y - d + NY) % NY) * 2 + (p % 2) * (1 - p // 2)

    def step(new_buf, new, old_buf, old, old_max, half, row):
        top = jnp.max(old_max, axis=0, keepdims=True)
        total = jnp.zeros((8, BW), F32)
        new_max = []
        if new is not None:
            e = emb[pl.ds(new * 8, 8)].reshape(BW, D)
        for i in range(4):
            if new is not None and i % 2 == 0:
                lanes = slice(128 * i, 128 * i + 256)
                raw = lax.dot_general(
                    cen[...].reshape(C, D), e[lanes, :], (((1,), (1,)), ((), ())), preferred_element_type=F32
                )
                new_buf[:, lanes] = raw
                new_max.append(jnp.max(raw.reshape(C // 8, 8, 256), axis=0))
            for k in range(4):
                rows = slice(256 * i + 64 * k, 256 * i + 64 * k + 64)
                value = jnp.exp2((old_buf[rows, :] - top) * EXP2_SCALE)
                kern[old, rows, :] = value
                total = total + jnp.sum(value.reshape(8, 8, BW), axis=0)
        if new is not None:
            new_max = jnp.concatenate(new_max, axis=1)
        scaled = top * EXP2_SCALE
        whole = scaled + jnp.log(jnp.sum(total, axis=0, keepdims=True)) * (1.0 / LN2)
        for j in range(2):
            lanes = slice(256 * j, 256 * j + 256)
            rl[0, half, pl.ds(row + j, 1), :] = whole[:, lanes]
            top_of[old // 4, pl.ds((old % 4) * 2 + j, 1), :] = scaled[:, lanes]
        return new_max

    first = push_1(0, 0, start=False)

    def two_steps(p, high):
        pl.when(p == 1)(phase_c)
        pl.when(p == 2)(phase_g)
        pl.when(p == 3)(phase_i)
        q = (p + 3) % 4
        high = step(buf0, place_of(p, False), buf1, place_of(q, True), high, q // 2, (q % 2) * 4 + 2)
        pl.when(p == 0)(phase_a)
        pl.when(p == 1)(phase_f)

        @pl.when(p == 2)
        def _():
            begin(first[1])
            phase_h()

        pl.when(p == 3)(phase_j)
        return step(buf1, place_of(p, True), buf0, place_of(p, False), high, p // 2, (p % 2) * 4)

    with jax.named_scope("logits"):
        high = lax.fori_loop(0, 4, two_steps, jnp.zeros((8, BW), F32))
        step(None, None, buf1, place_of(3, True), high, 1, 6)
    second = push_1(0, 1)
    whole(emb.at[pl.ds(0, 48)], ag_s.at[0], ag_r.at[0]).wait_send()
    for half, copies in ((0, first), (1, second)):
        landed(copies)
        merged = log_summed(rl[0, half], ra.at[0, half], 7)
        for j in range(8):
            place = place_of(2 * half + j // 4, j // 2 % 2 == 1)
            rl2[0, place // 4, pl.ds((place % 4) * 2 + j % 2, 1), :] = merged[j:j + 1, :]
    first, second = push_2(0, 0), push_2(0, 1)

    def start_weights(half):
        whole = log_summed(rl2[0, half], rb.at[0, half], 3)
        factor = jnp.exp2(top_of[half] - whole)
        fac[half] = factor
        rw[half] = factor * (1.0 / TOTAL)

    landed(first)
    start_weights(0)

    lane = lax.broadcasted_iota(jnp.int32, (8, 128), 1)

    def mass_half(half):
        def chunk(t, _):
            def tile(i):
                return pl.ds(pl.multiple_of(t * CH + 8 * i, 8), 8)

            acc = [None if half == 0 else part[tile(i), :] for i in range(16)]
            for b in range(4 * half, 4 * half + 4):
                for l in range(4):
                    r = (b % 4) * 2 + l // 2
                    w = jnp.broadcast_to(rw[half, r:r + 1, (l % 2) * 128:(l % 2) * 128 + 128], (8, 128))
                    for i in range(16):
                        value = kern[b, tile(i), l * 128:l * 128 + 128] * w
                        acc[i] = value if acc[i] is None else acc[i] + value
            for i in range(16):
                if half == 0:
                    part[tile(i), :] = acc[i]
                else:
                    total = jnp.sum(acc[i], axis=1, keepdims=True)
                    rows = slice(8 * i, 8 * i + 8)
                    col[rows, :] = jnp.where(lane == t, total, col[rows, :])
            return 0

        lax.fori_loop(0, NZ, chunk, 0)

    def row_half(n, half):
        def chunk(t, acc):
            acc = list(acc)
            for i in range(16):
                tile = pl.ds(pl.multiple_of(t * CH + 8 * i, 8), 8)
                s = scol[tile, :]
                for b in range(4):
                    for l in range(4):
                        acc[4 * b + l] += kern[4 * half + b, tile, l * 128:l * 128 + 128] * s
            return tuple(acc)

        acc = lax.fori_loop(0, NZ, chunk, tuple(jnp.zeros((8, 128), F32) for _ in range(16)))
        for b in range(4):
            for l in range(4):
                r, lanes = b * 2 + l // 2, slice((l % 2) * 128, (l % 2) * 128 + 128)
                total = jnp.sum(acc[4 * b + l], axis=0, keepdims=True)
                rl[n, half, r:r + 1, lanes] = total * fac[half, r:r + 1, lanes]

    col[...] = jnp.zeros((CH, CH), F32)
    for n in range(2):
        with jax.named_scope("mass"):
            mass_half(0)
        landed(second)
        if n == 0:
            start_weights(1)
        else:
            rw[1] = fac[1] / (TOTAL * summed(rl2[n, 1], rb.at[n, 1], 3))
        with jax.named_scope("mass"):
            mass_half(1)
        ml[n] = col[...].T[0:NZ, :]
        before = sent[:]
        sent.clear()
        copies = push(ml.at[n], mr.at[n], z_peers, m_s.at[n], m_r.at[n])
        drain(before)
        if n == 0:
            num[...] = jnp.zeros((NZ, CH, D), F32)
        else:
            part[...] = jnp.zeros((C, 128), F32)
        landed(copies)
        scale = 1.0 / (TOTAL * summed(ml[n], mr.at[n], 7))
        columns = jnp.concatenate([scale, jnp.zeros((CH - NZ, CH), F32)], axis=0).T
        for t in range(NZ):
            scol[t * CH:(t + 1) * CH, :] = jnp.broadcast_to(columns[:, t:t + 1], (CH, CH))
        with jax.named_scope("rows"):
            row_half(n + 1, 0)
        first = push_1(n + 1, 0)
        with jax.named_scope("rows"):
            row_half(n + 1, 1)
        second = push_1(n + 1, 1)
        landed(first)
        rl2[n + 1, 0] = summed(rl[n + 1, 0], ra.at[n + 1, 0], 7)
        first = push_2(n + 1, 0)
        landed(second)
        rl2[n + 1, 1] = summed(rl[n + 1, 1], ra.at[n + 1, 1], 7)
        second = push_2(n + 1, 1)
        landed(first)
        rw[0] = fac[0] / (TOTAL * summed(rl2[n + 1, 0], rb.at[n + 1, 0], 3))

    def chunk_at(q):
        return (z + q + NZ) % NZ

    def weigh(w, i, b):
        ws = [rw[b // 4, pl.ds((b % 4) * 2 + j, 1), :] for j in range(2)]
        for j, q in enumerate(GROUPS[i]):
            rows = pl.ds(pl.multiple_of(chunk_at(q) * CH, CH), CH)
            place = slice(POS[q] * CH, (POS[q] + 1) * CH)
            acc = part[place, :]
            for l in range(BW // 128):
                value = kern[b, rows, l * 128:l * 128 + 128] * ws[l // 2][:, (l % 2) * 128:(l % 2) * 128 + 128]
                acc = acc + value
                w[j * CH:(j + 1) * CH, l * 128:(l + 1) * 128] = value.astype(BF16)
            part[place, :] = acc

    def multiply(w, i, b):
        e = emb[pl.ds(b * 8, 8)].reshape(BW, D)
        n, first = len(GROUPS[i]), POS[GROUPS[i][0]]
        num[first:first + n] += jnp.dot(w[0:n * CH, :], e, preferred_element_type=F32).reshape(n, CH, D)

    def group(i, start, stop):
        def two(k, _):
            weigh(w1, i, 2 * k + 1)
            multiply(w0, i, 2 * k)
            weigh(w0, i, 2 * k + 2)
            multiply(w1, i, 2 * k + 1)
            return 0

        with jax.named_scope("numerators"):
            lax.fori_loop(start, stop, two, 0)

    def group_end(i):
        weigh(w1, i, 7)
        multiply(w0, i, 6)
        if i + 1 < len(GROUPS):
            weigh(w0, i + 1, 0)
        multiply(w1, i, 7)

    rs = {}

    def hop(name, q, rows, before=None):
        sign = 1 if name[0] in ("RA", "RB") else -1
        for part_of in range(2):
            i = len(rs)
            value = num[POS[q], rows.start + 32 * part_of:rows.start + 32 * part_of + 32, :]
            if before is not None:
                rs[(*before, part_of)].wait_recv()
                value = value + rcv[slot[(*before, part_of)]].astype(F32)
            snd[i] = value.astype(BF16)
            slot[(*name, part_of)] = i
            copy = pltpu.make_async_remote_copy(
                src_ref=snd.at[i], dst_ref=rcv.at[i], send_sem=rs_s.at[0], recv_sem=rs_r.at[i],
                device_id=at(dz=sign), device_id_type=MESH,
            )
            copy.start()
            rs[(*name, part_of)] = copy

    slot = {}
    lo, hi = slice(0, 64), slice(64, 128)

    weigh(w0, 0, 0)
    group(0, 0, 1)
    landed(second)
    rw[1] = fac[1] / (TOTAL * summed(rl2[2, 1], rb.at[2, 1], 3))
    group(0, 1, 3)
    group_end(0)
    hop(("RB", 0), 4, lo)
    hop(("LB", 0), 4, hi)
    drain(sent)
    sent.clear()
    group(1, 0, 3)
    group_end(1)
    hop(("RA", 1), 3, hi)
    hop(("LA", 1), -3, lo)
    group(2, 0, 1)
    hop(("RB", 1), 3, lo, ("RB", 0))
    hop(("LB", 1), -3, hi, ("LB", 0))
    group(2, 1, 3)
    group_end(2)
    hop(("RA", 2), 2, hi, ("RA", 1))
    hop(("LA", 2), -2, lo, ("LA", 1))
    group(3, 0, 2)
    hop(("RB", 2), 2, lo, ("RB", 1))
    hop(("LB", 2), -2, hi, ("LB", 1))
    group(3, 2, 3)
    group_end(3)
    hop(("RA", 3), 1, hi, ("RA", 2))
    hop(("LA", 3), -1, lo, ("LA", 2))
    group(4, 0, 3)
    weigh(w1, 4, 7)
    for j, q in enumerate(q for g in GROUPS for q in g):
        for i in range(16):
            rows = slice(8 * i, 8 * i + 8)
            total = jnp.sum(part[j * CH + 8 * i:j * CH + 8 * i + 8, :], axis=1, keepdims=True)
            col[rows, :] = jnp.where(lane == chunk_at(q), total, col[rows, :])
    ml[2] = col[...].T[0:NZ, :]
    last = push(ml.at[2], mr.at[2], z_peers, m_s.at[2], m_r.at[2])
    multiply(w0, 4, 6)
    multiply(w1, 4, 7)
    hop(("RB", 3), 1, lo, ("RB", 2))
    hop(("LB", 3), -1, hi, ("LB", 2))
    drain(last[:1])
    whole(snd, rs_s.at[0], rs_r.at[0]).wait_send()

    with jax.named_scope("last_hops"):
        landed(last)
        rs[("RB", 3, 0)].wait_recv()
    mass = ml[2, pl.ds(z, 1), :]
    for k in range(7):
        mass = mass + mr[2, k, pl.ds(z, 1), :]
    column = jnp.broadcast_to(mass, (CH, CH)).T
    column = jnp.concatenate([column] * (D // CH), axis=1)
    for start, one, two in ((64, ("RA", 3), ("LB", 3)), (0, ("LA", 3), ("RB", 3))):
        for part_of in range(2):
            rows = slice(start + 32 * part_of, start + 32 * part_of + 32)
            total = num[POS[0], rows, :]
            for name in (one, two):
                if (*name, part_of) != ("RB", 3, 0):
                    rs[(*name, part_of)].wait_recv()
                total = total + rcv[slot[(*name, part_of)]].astype(F32)
            out_ref[rows, :] = (total / column[rows, :]).astype(BF16)


def local(embeddings, centroids):
    e = embeddings.reshape(16, PIECE, D)
    k = centroids.reshape(NZ, NY, CH, D)
    dma = pltpu.SemaphoreType.DMA
    v = pltpu.VMEM
    out = pl.pallas_call(
        body,
        out_shape=jax.ShapeDtypeStruct((CH, D), BF16),
        in_specs=[pl.BlockSpec(memory_space=pl.ANY)] * 2,
        out_specs=pl.BlockSpec(memory_space=pltpu.VMEM),
        scratch_shapes=[
            v((64, PIECE, D), BF16), v((NZ, CH, D), BF16), v((NB, C, BW), F32), v((C, BW), F32), v((C, BW), F32),
            v((2, 8, 256), F32), v((3, 2, 8, 256), F32), v((3, 2, 8, 256), F32),
            v((3, 2, 7, 8, 256), F32), v((3, 2, 3, 8, 256), F32),
            v((2, 8, 256), F32), v((2, 8, 256), F32), v((C, 128), F32), v((C, 128), F32), v((CH, CH), F32),
            v((3, NZ, CH), F32), v((3, 7, NZ, CH), F32),
            v((GROUP * CH, BW), BF16), v((GROUP * CH, BW), BF16), v((NZ, CH, D), F32),
            v((28, 32, D), BF16), v((28, 32, D), BF16),
            dma((2,)), dma((1,)), dma((20,)), dma((3, 2)), dma((3, 2)), dma((3, 2)), dma((3, 2)),
            dma((3,)), dma((3,)), dma((1,)), dma((28,)),
        ],
        compiler_params=pltpu.CompilerParams(
            collective_id=0, has_side_effects=True, vmem_limit_bytes=60 * 1024 * 1024
        ),
        cost_estimate=pl.CostEstimate(
            flops=4 * C * NB * BW * D, bytes_accessed=8 * 1024 * 1024, transcendentals=C * NB * BW
        ),
    )(e, k)
    return out[None]


def solution(mesh):
    return jax.shard_map(
        local,
        mesh=mesh,
        in_specs=(P("docs", None), P("cent", None)),
        out_specs=P("cent", "docs", None),
        check_vma=False,
    )
```
